32 devices in a mesh: expert: 16 (over z, y, x), ffn: 2 (over core).
Axes of the slice: x: 2, y: 2, z: 4, core: 2. Of those that a mesh axis runs over, the one named last changes fastest.
Arguments:
- tokens: bfloat16 [2048, 4096], P('expert'), may hold values from -6 to 6
- cotangent: bfloat16 [2048, 4096], P('expert'), may hold values from -6 to 6
- expert_ids: int32 [2048, 1], P('expert'), may hold values from 0 to 1; in each aligned block of 128 rows (0 to 127, 128 to 255, ...) at most 80 rows name the same one
- in_weight: bfloat16 [16, 512, 5120], P('expert', None, 'ffn'), may hold values from -0.09375 to 0.09375
- out_weight: bfloat16 [16, 5120, 512], P('expert', 'ffn'), may hold values from -0.078125 to 0.078125
- width_states: float32 [2, 2, 4096], replicated, may hold values from 76.8 to 768
- hidden_states: float32 [2, 2, 5120], P(None, None, 'ffn'), may hold values from 76.8 to 768
Outputs:
- update_in: bfloat16 [16, 512, 5120], P('expert', None, 'ffn')
- update_out: bfloat16 [16, 5120, 512], P('expert', 'ffn')
The draws below stay inside these ranges and needn't reach their ends.
Inputs may be any that keep to these rules, and one draw needn't show every extreme that they name: `expert_ids`: within each block of 128 consecutive rows at most 80 name the same expert; in some block some expert is named by exactly 80 rows; every expert is named somewhere.
All inputs are finite; a program needn't handle non-finite values.
Results may differ from the reference program's by a relative error of at most 0.0049.
Values may be sent and summed in bfloat16 or wider, within the bound.
No kernel may reach another device: no remote copies, remote signals or barrier semaphores. Data moves between devices by JAX's collectives and lax.ppermute only.
A program may use at most 128 MiB of HBM per device.

```python
import math
import jax
import jax.numpy as jnp
import numpy as np
from jax import lax

D = 4096
FF = 5120
GROUP = 8
TOK_DEV = 128
EXPERTS = 2
CAP = 80
TOKENS = 2048
N_EXPERT = 16


def shard_levels(key, dims, pieces, least, high):
    factor_of = 1.0
    for position, parts in pieces:
        steps = jax.random.uniform(jax.random.fold_in(jax.random.fold_in(key, 6), position), (parts,), jnp.float32, least / len(pieces), high / len(pieces))
        factor_of = factor_of * jnp.repeat(jnp.exp(steps), dims[position] // parts).reshape((-1,) + (1,) * (len(dims) - 1 - position))
    return factor_of


def shared_out(key, own, number, rows, number_of, top, most, slope):
    order = jax.random.permutation(key, number_of)
    crowded, common = load_shares(number_of, rows * top, most, slope, True), load_shares(number_of, rows * top, most, slope, False)
    places = jnp.arange(number_of)

    def named(lengths, turn):
        used = int((lengths > 0).sum())
        fixed = max(1, used // 4)
        passed = fixed + (places - fixed + turn * (used - fixed)) % max(1, number_of - fixed)
        return jnp.zeros((number_of,), jnp.int32).at[order[jnp.where(places < fixed, places, passed)]].set(jnp.asarray(lengths, jnp.int32))

    lengths = jnp.where(number % 4 == 0, named(crowded, number // 4), named(common, number - number // 4 - 1))
    mixed = jax.random.permutation(jax.random.fold_in(own, 3), number_of)
    donor, sink = mixed[0:number_of // 2 * 2:2], mixed[1:number_of // 2 * 2:2]
    margin = jnp.minimum(lengths[donor] - 1, most - lengths[sink]) // 2
    margin = jnp.where((donor == order[0]) | (sink == order[0]) | (lengths[sink] == 0), 0, jnp.maximum(margin, 0))
    passed = jax.random.randint(jax.random.fold_in(own, 4), (number_of // 2,), 0, 1 << 20) % (margin + 1)
    lengths = lengths.at[donor].add(-passed).at[sink].add(passed)
    members = jnp.searchsorted(jnp.cumsum(lengths), jnp.arange(rows * top), side="right").astype(jnp.int32)
    listing = members.reshape(top, rows).T
    listing = listing[jax.random.permutation(jax.random.fold_in(own, 1), rows)]
    turn = jax.random.randint(jax.random.fold_in(own, 2), (rows, 1), 0, top)
    return jnp.take_along_axis(listing, (jnp.arange(top)[None, :] + turn) % top, axis=1)


def load_shares(amount, total, most, skew, full):
    weights = [(1 << 20) // math.isqrt(grade ** skew) + 1 for grade in range(1, amount + 1)]
    largest = most if full else min(most, max(-(-total // amount), total * weights[0] // sum(weights)))
    least = 1 if total - largest >= amount - 1 else 0
    given, surplus = [largest] + [least] * (amount - 1), total - largest - least * (amount - 1)
    while surplus > 0:
        movable = [i for i in range(1, amount) if given[i] < largest] or [i for i in range(1, amount) if given[i] < most]
        pool, left = sum([weights[i] for i in movable]), surplus
        for i in movable:
            more = min(most - given[i], max(1, left * weights[i] // pool), surplus)
            given[i] = given[i] + more
            surplus = surplus - more
    return np.array(given)


def gaussian(own_key, dims, scale, bound, pieces=(), kind=jnp.bfloat16):
    drawn = scale * jax.random.normal(own_key, dims, jnp.float32)
    if pieces:
        drawn = drawn * shard_levels(own_key, dims, pieces, -0.22, 0.18)
    return jnp.clip(drawn, -bound, bound).astype(kind)


def setup_inputs(seed: int = 0) -> dict:
    arg_keys = jax.random.split(jax.random.key(seed), 8)
    tokens = gaussian(arg_keys[0], (TOKENS, D), 1.0, 6.0, ((0, 16),))
    cotangent = gaussian(arg_keys[1], (TOKENS, D), 1.0, 6.0, ((0, 16),))
    expert_ids_keys = jax.random.split(jax.random.fold_in(arg_keys[2], 1), TOKENS // TOK_DEV)
    expert_ids_turns = jax.random.permutation(jax.random.fold_in(arg_keys[2], 3), TOKENS // TOK_DEV)
    expert_ids = jax.vmap(lambda own, number: shared_out(jax.random.fold_in(arg_keys[2], 2), own, number, TOK_DEV, EXPERTS, 1, CAP, 2))(expert_ids_keys, expert_ids_turns).reshape((TOKENS, 1))
    in_weight = gaussian(arg_keys[3], (EXPERTS * GROUP, D // GROUP, FF), D ** -0.5, 0.09375, ((0, 16), (2, 2)))
    out_weight = gaussian(arg_keys[4], (EXPERTS * GROUP, FF, D // GROUP), FF ** -0.5, 0.078125, ((0, 16), (1, 2)))
    width_states = jnp.clip(jnp.exp(jax.random.uniform(arg_keys[5], (2, EXPERTS, D), jnp.float32, math.log(76.8), math.log(768.0))), 76.8, 768.0)
    hidden_states = jnp.clip(jnp.exp(math.log(768.0) - 2.3025851 * jax.random.uniform(arg_keys[6], (2, EXPERTS, FF), jnp.float32) ** shard_levels(arg_keys[6], (2, EXPERTS, FF), ((2, 2),), -0.2, 0.2)), 76.8, 768.0)
    return dict(tokens=tokens, cotangent=cotangent, expert_ids=expert_ids, in_weight=in_weight, out_weight=out_weight, width_states=width_states, hidden_states=hidden_states)


DECAY_RATE = 0.9
EPS_ONE = 1e-30
ROOT_COEF = math.sqrt(2.0 / math.pi)
CUBIC_COEF = 0.044715

def gelu_pair(inputs):
    inner = ROOT_COEF * (inputs + CUBIC_COEF * inputs * inputs * inputs)
    tangent = jnp.tanh(inner)
    act_value = 0.5 * inputs * (1.0 + tangent)
    act_slope = 0.5 * (1.0 + tangent) + 0.5 * inputs * (1.0 - tangent * tangent) * ROOT_COEF * (1.0 + 3.0 * CUBIC_COEF * inputs * inputs)
    return (act_value, act_slope)

def factored(grad, row_prev, col_prev):
    squares = grad * grad + EPS_ONE
    row_factor = DECAY_RATE * row_prev + (1.0 - DECAY_RATE) * lax.optimization_barrier(jnp.mean(squares, axis=1))
    col_factor = DECAY_RATE * col_prev + (1.0 - DECAY_RATE) * lax.optimization_barrier(jnp.mean(squares, axis=0))
    scale_factor = row_factor[:, None] * col_factor[None, :] / jnp.mean(row_factor)
    update = grad * lax.rsqrt(scale_factor)
    clip_ratio = jnp.sqrt(jnp.mean(update * update))
    return (update / jnp.maximum(1.0, clip_ratio)).astype(jnp.bfloat16)

def reference(tokens, cotangent, expert_ids, in_weight, out_weight, width_states, hidden_states):
    route_ids = expert_ids[:, 0].reshape(N_EXPERT, TOK_DEV)
    onehot = (route_ids[:, :, None] == jnp.arange(EXPERTS, dtype=jnp.int32)[None, None, :]).astype(jnp.int32)
    before = jnp.cumsum(onehot, axis=1) - onehot
    slot_index = lax.optimization_barrier(jnp.sum(before * onehot, axis=2))
    source = jnp.arange(N_EXPERT, dtype=jnp.int32)[:, None]
    target = (source * CAP + slot_index).reshape(-1).astype(jnp.int32)
    flat_ids = route_ids.reshape(-1)
    token_index = jnp.arange(TOKENS, dtype=jnp.int32)
    in_all = in_weight.reshape(EXPERTS, D, FF)
    out_all = out_weight.reshape(EXPERTS, GROUP, FF, D // GROUP).transpose(0, 2, 1, 3).reshape(EXPERTS, FF, D)

    def one_expert(expert):
        place_index = jnp.where(flat_ids == expert, target, N_EXPERT * CAP).astype(jnp.int32)
        chosen = jnp.full((N_EXPERT * CAP,), TOKENS, jnp.int32).at[place_index].set(token_index, mode='drop')
        is_valid = chosen < TOKENS
        safe_index = jnp.minimum(chosen, TOKENS - 1).astype(jnp.int32)
        expert_tokens = tokens[safe_index] * is_valid[:, None].astype(tokens.dtype)
        expert_cotangent = cotangent[safe_index] * is_valid[:, None].astype(cotangent.dtype)
        in_one = in_all[expert]
        out_one = out_all[expert]
        pre_act = jnp.dot(expert_tokens, in_one, preferred_element_type=jnp.float32)
        back_act = jnp.dot(expert_cotangent, out_one.T, preferred_element_type=jnp.float32)
        act_value, act_slope = gelu_pair(pre_act)
        hidden = act_value.astype(jnp.bfloat16)
        pre_grad = (back_act * act_slope).astype(jnp.bfloat16)
        grad_in = jnp.dot(expert_tokens.T, pre_grad, preferred_element_type=jnp.float32)
        grad_out = jnp.dot(hidden.T, expert_cotangent, preferred_element_type=jnp.float32)
        upd_in = factored(grad_in, width_states[0, expert], hidden_states[0, expert])
        upd_out = factored(grad_out, hidden_states[1, expert], width_states[1, expert])
        return (upd_in, upd_out)
    upd_in, upd_out = lax.map(one_expert, jnp.arange(EXPERTS, dtype=jnp.int32))
    update_in = upd_in.reshape(EXPERTS * GROUP, D // GROUP, FF)
    update_out = upd_out.reshape(EXPERTS, FF, GROUP, D // GROUP).transpose(0, 2, 1, 3).reshape(EXPERTS * GROUP, FF, D // GROUP)
    return (update_in, update_out)
```

```python
import math

import jax
import jax.numpy as jnp
from jax import lax
from jax.sharding import PartitionSpec as P

D = 4096
FF = 5120
GROUP = 8


DECAY_RATE = 0.9
EPS_ONE = 1e-30
ROOT_COEF = math.sqrt(2.0 / math.pi)
CUBIC_COEF = 0.044715

PAIR, FIRST, SECOND = 1, 2, 4


def swap(value, mask, axis="expert"):
    pairs = [(source, source ^ mask) for source in range(lax.axis_size(axis))]
    return lax.ppermute(value, axis, pairs)


def gelu_pair(inputs):
    inner = ROOT_COEF * (inputs + CUBIC_COEF * inputs * inputs * inputs)
    tangent = jnp.tanh(inner)
    act_value = 0.5 * inputs * (1.0 + tangent)
    act_slope = 0.5 * (1.0 + tangent) + 0.5 * inputs * (1.0 - tangent * tangent) * ROOT_COEF * (
        1.0 + 3.0 * CUBIC_COEF * inputs * inputs
    )
    return (act_value, act_slope)


def dot(left, right, left_dim, right_dim):
    return lax.dot_general(
        left, right, (((left_dim,), (right_dim,)), ((), ())), preferred_element_type=jnp.float32
    )


def scalar_total(values):
    first = values
    for mask in (FIRST, SECOND, FIRST | SECOND):
        first = first + swap(values, mask)
    second = first + swap(first, PAIR)
    return lax.psum(second, "ffn")


def shards(tokens, cotangent, expert_ids, in_weight, out_weight, width_states, hidden_states):
    bf16 = jnp.bfloat16
    experts = width_states.shape[1]
    tok_rows, width = tokens.shape
    capacity = 5 * tok_rows // (4 * experts)
    part_cap = capacity // 2
    places = lax.axis_size("expert")
    block_width = width // GROUP
    hidden_part = in_weight.shape[2] // 2
    position = lax.axis_index("expert")
    expert = position // GROUP
    block_index = position % GROUP
    part = lax.axis_index("ffn") % 2
    pair_bit = position & 1
    first_bit = position >> 1 & 1
    second_bit = position >> 2 & 1

    local_in = in_weight[0]
    local_out = out_weight[0]
    keep_at = pair_bit * hidden_part
    send_at = (1 - pair_bit) * hidden_part
    in_keep = lax.dynamic_slice_in_dim(local_in, keep_at, hidden_part, 1)
    in_got = swap(lax.dynamic_slice_in_dim(local_in, send_at, hidden_part, 1), PAIR)
    out_keep = lax.dynamic_slice_in_dim(local_out, keep_at, hidden_part, 0)
    out_got = swap(lax.dynamic_slice_in_dim(local_out, send_at, hidden_part, 0), PAIR)

    route_ids = expert_ids[:, 0]
    onehot = (route_ids[:, None] == jnp.arange(experts, dtype=jnp.int32)[None, :]).astype(jnp.int32)
    before = jnp.cumsum(onehot, axis=0) - onehot
    slot_index = jnp.sum(before * onehot, axis=1) - part * part_cap
    valid = (slot_index >= 0) & (slot_index < part_cap)
    target = jnp.where(valid, route_ids * part_cap + slot_index, -1)
    select = (jnp.arange(experts * part_cap, dtype=jnp.int32)[:, None] == target[None, :]).astype(bf16)

    def dispatch(values):
        routed = dot(select, values, 1, 0).astype(bf16)
        routed = routed.reshape(experts, part_cap, GROUP, block_width).transpose(0, 2, 1, 3)
        routed = routed.reshape(places, part_cap, block_width)
        got = lax.all_to_all(routed, "expert", split_axis=0, concat_axis=0, tiled=True)
        got = got.reshape(places // GROUP, 2, 2, 2 * part_cap, block_width)
        got = jnp.where(second_bit == 1, got[:, ::-1], got)
        got = jnp.where(first_bit == 1, got[:, :, ::-1], got)
        got = got.transpose(1, 2, 0, 3, 4).reshape(4, -1, block_width)
        wide = jnp.concatenate([got, swap(got, PAIR)], axis=2)
        rows = jnp.concatenate([wide, swap(wide, 1, "ffn")], axis=1)
        return rows.reshape(2, 2, -1, 2 * block_width)

    expert_tokens = dispatch(tokens)
    expert_cotangent = dispatch(cotangent)
    in_pair = jnp.concatenate([in_keep, in_got], axis=0)
    out_pair = jnp.concatenate([out_keep, out_got], axis=1)

    middle = (hidden_part // 128 + 1) // 2 * 128 if hidden_part >= 256 else hidden_part // 2
    bounds = ((0, middle), (middle, hidden_part))
    orders = ((FIRST, SECOND, 1), (SECOND, FIRST, 0))

    def scatter_sum(rows, weights, contract, order):
        mask_one, mask_two, dim = order
        kept_rows = lax.index_in_dim(rows, 0, dim, keepdims=False)
        sent_rows = lax.index_in_dim(rows, 1, dim, keepdims=False)
        got = swap(dot(sent_rows, weights, 2, contract).astype(bf16), mask_one)
        total = dot(kept_rows, weights, 2, contract) + got.astype(jnp.float32)
        got = swap(total[1].astype(bf16), mask_two)
        return total[0] + got.astype(jnp.float32)

    def gather(own, order):
        mask_one, mask_two, dim = order
        both = jnp.stack([own, swap(own, mask_two)])
        whole = jnp.stack([both, swap(both, mask_one)], axis=dim)
        return whole.reshape(-1, own.shape[-1])

    pre = [
        scatter_sum(expert_tokens, in_pair[:, low:high], 0, order)
        for (low, high), order in zip(bounds, orders)
    ]
    back = [
        scatter_sum(expert_cotangent, out_pair[low:high], 1, order)
        for (low, high), order in zip(bounds, orders)
    ]
    acts = [gelu_pair(value) for value in pre]
    hidden = [gather(act[0].astype(bf16), order) for act, order in zip(acts, orders)]
    pre_grad = [
        gather((value * act[1]).astype(bf16), order) for value, act, order in zip(back, acts, orders)
    ]
    token_rows = expert_tokens.reshape(-1, 2 * block_width)
    cotangent_rows = expert_cotangent.reshape(-1, 2 * block_width)

    width_pick = lax.dynamic_index_in_dim(width_states, expert, 1, keepdims=False)
    width_pair = jnp.concatenate(
        [
            lax.dynamic_slice_in_dim(width_pick, block_index * block_width, block_width, 1),
            lax.dynamic_slice_in_dim(width_pick, (block_index ^ 1) * block_width, block_width, 1),
        ],
        axis=1,
    )
    hidden_pick = lax.dynamic_index_in_dim(hidden_states, expert, 1, keepdims=False)
    hidden_own = lax.dynamic_slice_in_dim(hidden_pick, keep_at, hidden_part, 1)
    hidden_mean = lax.psum(jnp.sum(hidden_pick[1]), "ffn") / FF
    width_mean = jnp.mean(width_pick[0])

    def sums_width(partial):
        got = swap(partial, PAIR)
        total = partial + jnp.concatenate([got[block_width:], got[:block_width]])
        return lax.psum(total, "ffn")

    def sums_hidden(partial):
        total = partial
        for mask in (FIRST, SECOND, FIRST | SECOND):
            total = total + swap(partial, mask)
        return total

    whole_count = float(D) * float(FF)

    grad_out = jnp.concatenate([dot(value, cotangent_rows, 0, 0) for value in hidden], axis=0)
    out_received = swap(grad_out[:, block_width:].astype(bf16), PAIR)
    square_out = grad_out * grad_out + EPS_ONE
    row_out = jnp.sum(square_out, axis=1)
    col_out = jnp.sum(square_out, axis=0)
    rows_out = DECAY_RATE * hidden_own[1] + (1.0 - DECAY_RATE) * sums_hidden(row_out) / D
    cols_out = DECAY_RATE * width_pair[1] + (1.0 - DECAY_RATE) * sums_width(col_out) / FF
    norm_out = jnp.sum(square_out_scaled(grad_out, rows_out, cols_out))
    total_out, norm_out = scalar_total(jnp.stack([jnp.sum(row_out), norm_out]))
    mean_out = DECAY_RATE * hidden_mean + (1.0 - DECAY_RATE) * total_out / whole_count
    clip_out = jnp.maximum(1.0, jnp.sqrt(mean_out * norm_out / whole_count))
    factor_out = jnp.sqrt(mean_out) / clip_out
    rows_out_got = swap(rows_out, PAIR)

    grad_in = jnp.concatenate([dot(token_rows, value, 0, 0) for value in pre_grad], axis=1)
    in_received = swap(grad_in[block_width:].astype(bf16), PAIR)
    square_in = grad_in * grad_in + EPS_ONE
    row_in = jnp.sum(square_in, axis=1)
    col_in = jnp.sum(square_in, axis=0)
    rows_in = DECAY_RATE * width_pair[0] + (1.0 - DECAY_RATE) * sums_width(row_in) / FF
    cols_in = DECAY_RATE * hidden_own[0] + (1.0 - DECAY_RATE) * sums_hidden(col_in) / D
    norm_in = jnp.sum(square_out_scaled(grad_in, rows_in, cols_in))
    total_in, norm_in = scalar_total(jnp.stack([jnp.sum(row_in), norm_in]))
    mean_in = DECAY_RATE * width_mean + (1.0 - DECAY_RATE) * total_in / whole_count
    clip_in = jnp.maximum(1.0, jnp.sqrt(mean_in * norm_in / whole_count))
    factor_in = jnp.sqrt(mean_in) / clip_in
    cols_in_got = swap(cols_in, PAIR)

    def finish(grad, rows, cols, factor):
        scale = lax.rsqrt(rows)[:, None] * lax.rsqrt(cols)[None, :] * factor
        return (grad.astype(jnp.float32) * scale).astype(bf16)

    in_own = finish(grad_in[:block_width], rows_in[:block_width], cols_in, factor_in)
    in_other = finish(in_received, rows_in[:block_width], cols_in_got, factor_in)
    update_in = jnp.where(
        pair_bit == 1,
        jnp.concatenate([in_other, in_own], axis=1),
        jnp.concatenate([in_own, in_other], axis=1),
    )
    out_own = finish(grad_out[:, :block_width], rows_out, cols_out[:block_width], factor_out)
    out_other = finish(out_received, rows_out_got, cols_out[:block_width], factor_out)
    update_out = jnp.where(
        pair_bit == 1,
        jnp.concatenate([out_other, out_own], axis=0),
        jnp.concatenate([out_own, out_other], axis=0),
    )
    return (update_in[None], update_out[None])


def square_out_scaled(grad, rows, cols):
    return grad * grad * (1.0 / rows)[:, None] * (1.0 / cols)[None, :]


def solution(mesh):
    return jax.shard_map(
        shards,
        mesh=mesh,
        in_specs=(
            P("expert", None),
            P("expert", None),
            P("expert", None),
            P("expert", None, "ffn"),
            P("expert", "ffn", None),
            P(),
            P(None, None, "ffn"),
        ),
        out_specs=(P("expert", None, "ffn"), P("expert", "ffn", None)),
        check_vma=False,
    )
```

```python
import math

import jax
import jax.numpy as jnp
from jax import lax
from jax.sharding import PartitionSpec as P

D = 4096
FF = 5120
GROUP = 8


DECAY_RATE = 0.9
EPS_ONE = 1e-30
ROOT_COEF = math.sqrt(2.0 / math.pi)
CUBIC_COEF = 0.044715

MASKS = (1, 2, 4)


def swap(value, mask, axis="expert"):
    pairs = [(source, source ^ mask) for source in range(lax.axis_size(axis))]
    return lax.ppermute(value, axis, pairs)


def gelu_pair(inputs):
    inner = ROOT_COEF * (inputs + CUBIC_COEF * inputs * inputs * inputs)
    tangent = jnp.tanh(inner)
    act_value = 0.5 * inputs * (1.0 + tangent)
    act_slope = 0.5 * (1.0 + tangent) + 0.5 * inputs * (1.0 - tangent * tangent) * ROOT_COEF * (
        1.0 + 3.0 * CUBIC_COEF * inputs * inputs
    )
    return (act_value, act_slope)


def dot(left, right, left_dim, right_dim):
    return lax.dot_general(
        left, right, (((left_dim,), (right_dim,)), ((), ())), preferred_element_type=jnp.float32
    )


def pick(value, index, dim):
    return lax.index_in_dim(value, index, dim, keepdims=False)


def ffn_total(values):
    mask = 1
    while mask < lax.axis_size("ffn"):
        values = values + swap(values, mask, "ffn")
        mask *= 2
    return values


def set_bounds(hidden):
    unit = next(unit for unit in (256, 128, 2) if hidden % unit == 0 and hidden // unit >= 3)
    units = hidden // unit
    bounds, low = [], 0
    for k in range(3):
        high = low + (units // 3 + (k < units % 3)) * unit
        bounds.append((low, high))
        low = high
    return bounds


def shards(tokens, cotangent, expert_ids, in_weight, out_weight, width_states, hidden_states):
    bf16 = jnp.bfloat16
    experts = width_states.shape[1]
    tok_rows, width = tokens.shape
    capacity = 5 * tok_rows // (4 * experts)
    part_cap = capacity // 2
    places = lax.axis_size("expert")
    block_width = width // GROUP
    position = lax.axis_index("expert")
    expert = position // GROUP
    block_index = position % GROUP
    part = lax.axis_index("ffn") % 2
    bits = [position >> k & 1 for k in range(3)]
    bounds = set_bounds(in_weight.shape[2])
    halves = [(high - low) // 2 for low, high in bounds]
    sets = range(3)
    firsts = [(k + 1) % 3 for k in sets]
    seconds = [(k + 2) % 3 for k in sets]

    def side(values, k, dim, own):
        place = bits[k] if own else 1 - bits[k]
        return lax.dynamic_slice_in_dim(values, bounds[k][0] + place * halves[k], halves[k], dim)

    local_in = in_weight[0]
    local_out = out_weight[0]
    in_got = [swap(side(local_in, k, 1, False), MASKS[k]) for k in sets]
    out_got = [swap(side(local_out, k, 0, False), MASKS[k]) for k in sets]

    route_ids = expert_ids[:, 0]
    onehot = (route_ids[:, None] == jnp.arange(experts, dtype=jnp.int32)[None, :]).astype(jnp.int32)
    before = jnp.cumsum(onehot, axis=0) - onehot
    slot_index = jnp.sum(before * onehot, axis=1) - part * part_cap
    valid = (slot_index >= 0) & (slot_index < part_cap)
    target = jnp.where(valid, route_ids * part_cap + slot_index, -1)
    select = (jnp.arange(experts * part_cap, dtype=jnp.int32)[:, None] == target[None, :]).astype(bf16)

    def route(values):
        routed = dot(select, values, 1, 0).astype(bf16)
        routed = routed.reshape(experts, part_cap, GROUP, block_width).transpose(0, 2, 1, 3)
        return routed.reshape(places, part_cap, block_width)

    def deliver(routed):
        got = lax.all_to_all(routed, "expert", split_axis=0, concat_axis=0, tiled=True)
        got = got.reshape(places // GROUP, 2, 2, 2, part_cap, block_width)
        for k in sets:
            got = jnp.where(bits[k] == 1, jnp.flip(got, 3 - k), got)
        return got.transpose(1, 2, 3, 0, 4, 5).reshape(2, 2, 2, -1, block_width)

    def both_cores(got):
        return jnp.concatenate([got, swap(got, 1, "ffn")], axis=3)

    got_tokens = deliver(route(tokens))
    routed_cotangent, in_got, out_got = lax.optimization_barrier((route(cotangent), in_got, out_got))
    pair_tokens = [swap(got_tokens, MASKS[k]) for k in sets]
    got_cotangent = deliver(routed_cotangent)
    pair_cotangent = [swap(got_cotangent, MASKS[k]) for k in sets]

    def widen(got, others):
        own = both_cores(got)
        return [
            jnp.concatenate([own, jnp.flip(both_cores(others[k]), 2 - k)], axis=4) for k in sets
        ]

    set_tokens = widen(got_tokens, pair_tokens)
    set_cotangent = widen(got_cotangent, pair_cotangent)
    set_in = [jnp.concatenate([side(local_in, k, 1, True), in_got[k]], axis=0) for k in sets]
    set_out = [jnp.concatenate([side(local_out, k, 0, True), out_got[k]], axis=1) for k in sets]

    def second_dim(k):
        return 2 - seconds[k] - (seconds[k] < firsts[k])

    def scatter_sum(rows, weights, contract):
        sent = [
            swap(dot(pick(rows[k], 1, 2 - firsts[k]), weights[k], 3, contract).astype(bf16), MASKS[firsts[k]])
            for k in sets
        ]
        totals = [
            dot(pick(rows[k], 0, 2 - firsts[k]), weights[k], 3, contract) + sent[k].astype(jnp.float32)
            for k in sets
        ]
        sent = [
            swap(pick(totals[k], 1, second_dim(k)).astype(bf16), MASKS[seconds[k]]) for k in sets
        ]
        return [pick(totals[k], 0, second_dim(k)) + sent[k].astype(jnp.float32) for k in sets]

    def gather(owns):
        boths = [
            jnp.stack([owns[k], swap(owns[k], MASKS[seconds[k]])], axis=second_dim(k)) for k in sets
        ]
        wholes = [
            jnp.stack([boths[k], swap(boths[k], MASKS[firsts[k]])], axis=2 - firsts[k]) for k in sets
        ]
        return [wholes[k].reshape(-1, halves[k]) for k in sets]

    pre = scatter_sum(set_tokens, set_in, 0)
    back = scatter_sum(set_cotangent, set_out, 1)
    acts = [gelu_pair(value) for value in pre]
    hidden = gather([act[0].astype(bf16) for act in acts])
    pre_grad = gather([(value * act[1]).astype(bf16) for value, act in zip(back, acts)])

    width_pick = lax.dynamic_index_in_dim(width_states, expert, 1, keepdims=False)
    width_own = lax.dynamic_slice_in_dim(width_pick, block_index * block_width, block_width, 1)
    hidden_pick = lax.dynamic_index_in_dim(hidden_states, expert, 1, keepdims=False)
    hidden_own = [side(hidden_pick, k, 1, True) for k in sets]
    hidden_mean = ffn_total(jnp.sum(hidden_pick[1])[None])[0] / FF
    width_mean = jnp.mean(width_pick[0])
    whole_count = float(D) * float(FF)

    def along(values, dim):
        return values[:, None] if dim == 0 else values[None, :]

    def factors(grads, which, width_dim, mean_prev):
        hidden_dim = 1 - width_dim
        squares = [grad * grad + EPS_ONE for grad in grads]
        by_width = [jnp.sum(square, axis=hidden_dim) for square in squares]
        by_hidden = [jnp.sum(square, axis=width_dim) for square in squares]
        total = sum(jnp.sum(value) for value in by_hidden)
        got = [
            swap(jnp.concatenate([by_width[j][block_width:], by_hidden[j - 1]]), MASKS[j]) for j in sets
        ]
        width_sum = sum(by_width[j][:block_width] + got[j][:block_width] for j in sets)
        by_hidden = [by_hidden[k] + got[firsts[k]][block_width:] for k in sets]
        width_sum = ffn_total(width_sum)
        by_hidden = [by_hidden[k] + swap(by_hidden[k], MASKS[seconds[k]]) for k in sets]
        width_factor = DECAY_RATE * width_own[which] + (1.0 - DECAY_RATE) * width_sum / FF
        hidden_factor = [
            DECAY_RATE * hidden_own[k][which] + (1.0 - DECAY_RATE) * by_hidden[k] / D for k in sets
        ]
        parts = [
            jnp.sum(grad * grad * along(1.0 / factor, hidden_dim), axis=hidden_dim)
            for grad, factor in zip(grads, hidden_factor)
        ]
        got = [
            swap(jnp.concatenate([parts[k][block_width:], hidden_factor[k]]), MASKS[k]) for k in sets
        ]
        scaled = sum(parts[k][:block_width] + got[k][:block_width] for k in sets)
        sums = jnp.stack([total, jnp.sum(scaled / width_factor)])
        for mask in MASKS:
            sums = sums + swap(sums, mask)
        sums = ffn_total(sums)
        mean = DECAY_RATE * mean_prev + (1.0 - DECAY_RATE) * sums[0] / whole_count
        clip = jnp.maximum(1.0, jnp.sqrt(mean * sums[1] / whole_count))
        width_scale = lax.rsqrt(width_factor) * (jnp.sqrt(mean) / clip)
        hidden_scale = [
            (lax.rsqrt(hidden_factor[k]), lax.rsqrt(got[k][block_width:])) for k in sets
        ]
        return width_scale, hidden_scale

    def finish(owns, others, scales, width_dim):
        hidden_dim = 1 - width_dim
        width_scale, hidden_scale = scales
        pieces = []
        for k in sets:
            own = owns[k] * along(width_scale, width_dim) * along(hidden_scale[k][0], hidden_dim)
            other = others[k].astype(jnp.float32) * along(width_scale, width_dim) * along(
                hidden_scale[k][1], hidden_dim
            )
            own, other = own.astype(bf16), other.astype(bf16)
            pieces.append(jnp.where(bits[k] == 1, other, own))
            pieces.append(jnp.where(bits[k] == 1, own, other))
        return jnp.concatenate(pieces, axis=hidden_dim)

    grad_out = [
        dot(hidden[k], set_cotangent[k].reshape(-1, 2 * block_width), 0, 0) for k in sets
    ]
    out_sent = [grad[:, block_width:].astype(bf16) for grad in grad_out]
    pre_grad, out_sent = lax.optimization_barrier((pre_grad, out_sent))
    out_others = [swap(out_sent[k], MASKS[k]) for k in sets]
    grad_in = [dot(set_tokens[k].reshape(-1, 2 * block_width), pre_grad[k], 0, 0) for k in sets]
    in_others = [swap(grad_in[k][block_width:].astype(bf16), MASKS[k]) for k in sets]

    out_scales = factors(grad_out, 1, 1, hidden_mean)
    in_scales = factors(grad_in, 0, 0, width_mean)
    update_in = finish([grad[:block_width] for grad in grad_in], in_others, in_scales, 0)
    update_out = finish([grad[:, :block_width] for grad in grad_out], out_others, out_scales, 1)
    return (update_in[None], update_out[None])


def solution(mesh):
    return jax.shard_map(
        shards,
        mesh=mesh,
        in_specs=(
            P("expert", None),
            P("expert", None),
            P("expert", None),
            P("expert", None, "ffn"),
            P("expert", "ffn", None),
            P(),
            P(None, None, "ffn"),
        ),
        out_specs=(P("expert", None, "ffn"), P("expert", "ffn", None)),
        check_vma=False,
    )
```

```python
import functools
import math

import jax
import jax.numpy as jnp
from jax import lax
from jax.experimental import pallas as pl
from jax.experimental.pallas import tpu as pltpu
from jax.sharding import PartitionSpec as P

D = 4096
FF = 5120
GROUP = 8


DECAY_RATE = 0.9
EPS_ONE = 1e-30
ROOT_COEF = math.sqrt(2.0 / math.pi)
CUBIC_COEF = 0.044715

MASKS = (1, 2, 4)

VMEM_BYTES = 48 * 1024 * 1024


def swap(value, mask, axis="expert"):
    pairs = [(source, source ^ mask) for source in range(lax.axis_size(axis))]
    return lax.ppermute(value, axis, pairs)


def gelu_pair(inputs):
    inner = ROOT_COEF * (inputs + CUBIC_COEF * inputs * inputs * inputs)
    tangent = jnp.tanh(inner)
    act_value = 0.5 * inputs * (1.0 + tangent)
    act_slope = 0.5 * (1.0 + tangent) + 0.5 * inputs * (1.0 - tangent * tangent) * ROOT_COEF * (
        1.0 + 3.0 * CUBIC_COEF * inputs * inputs
    )
    return (act_value, act_slope)


def ffn_total(values):
    mask = 1
    while mask < lax.axis_size("ffn"):
        values = values + swap(values, mask, "ffn")
        mask *= 2
    return values


def set_bounds(hidden):
    unit = next(unit for unit in (256, 128, 2) if hidden % unit == 0 and hidden // unit >= 3)
    units = hidden // unit
    bounds, low = [], 0
    for k in range(3):
        high = low + (units // 3 + (k < units % 3)) * unit
        bounds.append((low, high))
        low = high
    return bounds


def dot(left, right, left_dim, right_dim):
    return lax.dot_general(
        left, right, (((left_dim,), (right_dim,)), ((), ())), preferred_element_type=jnp.float32
    )


def call(kernel, out_shape, *operands):
    return pl.pallas_call(
        kernel,
        out_shape=out_shape,
        in_specs=[pl.BlockSpec(memory_space=pltpu.VMEM)] * len(operands),
        out_specs=jax.tree.map(lambda _: pl.BlockSpec(memory_space=pltpu.VMEM), out_shape),
        compiler_params=pltpu.CompilerParams(vmem_limit_bytes=VMEM_BYTES),
    )(*operands)


def place_in_group():
    return lax.rem(lax.axis_index("expert"), GROUP)


def bit(place, k):
    return lax.rem(lax.div(place, 1 << k), 2)


def flipped(place, mask):
    for k in range(3):
        if mask >> k & 1:
            place = place + (1 - 2 * bit(place, k)) * (1 << k)
    return place


def weight_part(weight_ref, k, low, half, by_row):
    side = bit(place_in_group(), k)
    if by_row:
        return weight_ref[pl.ds(pl.multiple_of(low + side * half, math.gcd(low, half)), half), :]
    if half % 128 == 0:
        return weight_ref[:, pl.ds(pl.multiple_of(low + side * half, 128), half)]
    return jnp.where(side == 1, weight_ref[:, low + half : low + 2 * half], weight_ref[:, low : low + half])


def partial_sum(rows, own_weight, got_weight, by_row):
    width = rows.shape[1] // 2
    contract = 1 if by_row else 0
    return dot(rows[:, :width], own_weight, 1, contract) + dot(rows[:, width:], got_weight, 1, contract)


def sent_kernel(k, low, half, by_row, *refs):
    own, own_other, pair, pair_other, weight, got_weight, rows_out, sent_out = refs
    count, width = own.shape[1], own.shape[2]
    first, second = 1 << (k + 1) % 3, 1 << (k + 2) % 3
    for i in range(2):
        for j in range(2):
            for l in range(2):
                chunk = flipped(place_in_group(), i * first + j * second + l * (1 << k))
                at = (j * 2 + l) * 2 * count
                rows_out[i, at : at + count, :width] = own[chunk]
                rows_out[i, at : at + count, width:] = pair[chunk]
                rows_out[i, at + count : at + 2 * count, :width] = own_other[chunk]
                rows_out[i, at + count : at + 2 * count, width:] = pair_other[chunk]
    own_weight = weight_part(weight, k, low, half, by_row)
    sent_out[...] = partial_sum(rows_out[1], own_weight, got_weight[...], by_row).astype(sent_out.dtype)


def kept_kernel(k, low, half, by_row, rows, weight, got_weight, received, kept_out, sent_out):
    own_weight = weight_part(weight, k, low, half, by_row)
    total = partial_sum(rows[0], own_weight, got_weight[...], by_row) + received[...].astype(jnp.float32)
    middle = total.shape[0] // 2
    kept_out[...] = total[:middle]
    sent_out[...] = total[middle:].astype(sent_out.dtype)


def gradient_kernel(hidden_first, rows, near, far, grad_out, sent_out, by_width_out, by_hidden_out):
    width = rows.shape[2] // 2
    if hidden_first:
        grad = dot(near[...], rows[0], 0, 0) + dot(far[...], rows[1], 0, 0)
        sent_out[...] = grad[:, width:].astype(sent_out.dtype)
    else:
        grad = dot(rows[0], near[...], 0, 0) + dot(rows[1], far[...], 0, 0)
        sent_out[...] = grad[width:].astype(sent_out.dtype)
    grad_out[...] = grad
    square = grad * grad + EPS_ONE
    down = jnp.sum(square, axis=0, keepdims=True)
    across = dot(jnp.ones((8, square.shape[1]), jnp.float32), square, 1, 1)
    down = jnp.broadcast_to(down, (8, square.shape[1]))
    by_width_out[...] = down if hidden_first else across
    by_hidden_out[...] = across if hidden_first else down


IN_WIDTH, OUT_WIDTH, IN_HIDDEN, OUT_HIDDEN, TOTALS, STAT_ROWS = 0, 8, 16, 22, 28, 32


def collect_kernel(hidden_prev, *refs):
    stats_out = refs[-1]
    place = place_in_group()
    stats_out[...] = jnp.zeros_like(stats_out)
    lanes = stats_out.shape[1]
    for which in range(2):
        by_width, by_hidden = refs[which * 6 : which * 6 + 3], refs[which * 6 + 3 : which * 6 + 6]
        width_row, hidden_row = (IN_WIDTH, OUT_WIDTH)[which], (IN_HIDDEN, OUT_HIDDEN)[which]
        width = by_width[0].shape[1] // 2
        own = sum(ref[0:1, :width] for ref in by_width)
        stats_out[pl.ds(width_row + place, 1), :width] = own
        total = 0.0
        for k in range(3):
            stats_out[pl.ds(width_row + flipped(place, 1 << k), 1), :width] = by_width[k][0:1, width:]
            half = by_hidden[k].shape[1]
            row = by_hidden[k][0:1, :]
            stats_out[pl.ds(hidden_row + 2 * k + bit(place, k), 1), :half] = row
            total = total + jnp.sum(row, axis=1, keepdims=True)
        stats_out[TOTALS + which : TOTALS + which + 1, :] = jnp.broadcast_to(total, (1, lanes))
    previous = jnp.sum(hidden_prev[...], axis=1, keepdims=True)
    stats_out[TOTALS + 2 : TOTALS + 3, :] = jnp.broadcast_to(previous, (1, lanes))


def stat_row(stats_ref, index):
    return stats_ref[pl.ds(index, 1), :]


def upright(row):
    return jnp.transpose(jnp.broadcast_to(row, (8, row.shape[1])))[:, 0:1]


def norm_kernel(prev, group_sums, whole_sums, *refs):
    grads_in, grads_out, factors_out, norms_out = refs[:3], refs[3:6], refs[6], refs[7]
    place = place_in_group()
    width = grads_in[0].shape[0] // 2
    row = lax.broadcasted_iota(jnp.int32, prev.shape, 0)
    by_width = row < IN_HIDDEN
    mean = jnp.where(by_width, whole_sums[...] / FF, group_sums[...] / D)
    factors_out[...] = DECAY_RATE * prev[...] + (1.0 - DECAY_RATE) * mean
    norm_in, norm_out = 0.0, 0.0
    for k in range(3):
        half = grads_in[k].shape[1]
        partner = flipped(place, 1 << k)
        own_row = stat_row(factors_out, IN_WIDTH + place)[:, :width]
        pair_row = stat_row(factors_out, IN_WIDTH + partner)[:, :width]
        hidden_row = stat_row(factors_out, IN_HIDDEN + 2 * k + bit(place, k))[:, :half]
        down = jnp.sum(grads_in[k][:width] * grads_in[k][:width] * upright(1.0 / own_row), axis=0, keepdims=True)
        down = down + jnp.sum(
            grads_in[k][width:] * grads_in[k][width:] * upright(1.0 / pair_row), axis=0, keepdims=True
        )
        norm_in = norm_in + jnp.sum(down / hidden_row, axis=1, keepdims=True)
        own_row = stat_row(factors_out, OUT_WIDTH + place)[:, :width]
        pair_row = stat_row(factors_out, OUT_WIDTH + partner)[:, :width]
        hidden_row = stat_row(factors_out, OUT_HIDDEN + 2 * k + bit(place, k))[:, :half]
        down = jnp.sum(grads_out[k][...] * grads_out[k][...] * upright(1.0 / hidden_row), axis=0, keepdims=True)
        norm_out = norm_out + jnp.sum(down[:, :width] / own_row, axis=1, keepdims=True)
        norm_out = norm_out + jnp.sum(down[:, width:] / pair_row, axis=1, keepdims=True)
    row = lax.broadcasted_iota(jnp.int32, norms_out.shape, 0)
    norms_out[...] = jnp.where(row == 0, norm_in, norm_out)


def final_kernel(bounds, prev, factors, whole_sums, norms, *refs):
    grads_in, grads_out, got_in, got_out = refs[:3], refs[3:6], refs[6:9], refs[9:12]
    update_in, update_out = refs[12:]
    place = place_in_group()
    width = update_in.shape[0]
    count = float(D) * float(FF)
    mean_in = DECAY_RATE * jnp.mean(prev[IN_WIDTH : IN_WIDTH + 8, :width], keepdims=True)
    mean_in = mean_in + (1.0 - DECAY_RATE) * whole_sums[TOTALS : TOTALS + 1, 0:1] / count
    mean_out = DECAY_RATE * whole_sums[TOTALS + 2 : TOTALS + 3, 0:1] / (FF * GROUP)
    mean_out = mean_out + (1.0 - DECAY_RATE) * whole_sums[TOTALS + 1 : TOTALS + 2, 0:1] / count
    factor_in = jnp.sqrt(mean_in) / jnp.maximum(1.0, jnp.sqrt(mean_in * norms[0:1, 0:1] / count))
    factor_out = jnp.sqrt(mean_out) / jnp.maximum(1.0, jnp.sqrt(mean_out * norms[1:2, 0:1] / count))
    width_in = upright(lax.rsqrt(stat_row(factors, IN_WIDTH + place)[:, :width]) * factor_in)
    width_out = lax.rsqrt(stat_row(factors, OUT_WIDTH + place)[:, :width]) * factor_out
    for k in range(3):
        low, half = bounds[k][0], (bounds[k][1] - bounds[k][0]) // 2
        own_bit = bit(place, k)
        if half % 128:
            width_scaled = (grads_in[k][:width] * width_in, got_in[k][...].astype(jnp.float32) * width_in)
            for side in range(2):
                hidden_in = lax.rsqrt(factors[IN_HIDDEN + 2 * k + side : IN_HIDDEN + 2 * k + side + 1, :half])
                value = jnp.where(own_bit == side, *width_scaled) * hidden_in
                update_in[:, low + side * half : low + side * half + half] = value.astype(update_in.dtype)
        for own in (True, False):
            side = own_bit if own else 1 - own_bit
            start = pl.multiple_of(low + side * half, math.gcd(low, half))
            hidden_out = upright(lax.rsqrt(stat_row(factors, OUT_HIDDEN + 2 * k + side)[:, :half]))
            if half % 128 == 0:
                hidden_in = lax.rsqrt(stat_row(factors, IN_HIDDEN + 2 * k + side)[:, :half])
                value = grads_in[k][:width] if own else got_in[k][...].astype(jnp.float32)
                update_in[:, pl.ds(start, half)] = (value * width_in * hidden_in).astype(update_in.dtype)
            value = grads_out[k][:, :width] if own else got_out[k][...].astype(jnp.float32)
            update_out[pl.ds(start, half), :] = (value * hidden_out * width_out).astype(update_out.dtype)


def shards(tokens, cotangent, expert_ids, in_weight, out_weight, width_states, hidden_states):
    bf16, f32 = jnp.bfloat16, jnp.float32
    shape = jax.ShapeDtypeStruct
    experts = width_states.shape[1]
    tok_rows, width = tokens.shape
    capacity = 5 * tok_rows // (4 * experts)
    part_cap = capacity // 2
    places = lax.axis_size("expert")
    block_width = width // GROUP
    position = lax.axis_index("expert")
    expert = position // GROUP
    part = lax.axis_index("ffn") % 2
    bits = [position >> k & 1 for k in range(3)]
    bounds = set_bounds(in_weight.shape[2])
    halves = [(high - low) // 2 for low, high in bounds]
    sets = range(3)
    firsts = [MASKS[(k + 1) % 3] for k in sets]
    seconds = [MASKS[(k + 2) % 3] for k in sets]
    local_in = in_weight[0]
    local_out = out_weight[0]

    def pair_side(values, k, dim):
        return lax.dynamic_slice_in_dim(values, bounds[k][0] + (1 - bits[k]) * halves[k], halves[k], dim)

    in_got = [swap(pair_side(local_in, k, 1), MASKS[k]) for k in sets]
    out_got = [swap(pair_side(local_out, k, 0), MASKS[k]) for k in sets]

    route_ids = expert_ids[:, 0]
    onehot = (route_ids[:, None] == jnp.arange(experts, dtype=jnp.int32)[None, :]).astype(jnp.int32)
    before = jnp.cumsum(onehot, axis=0) - onehot
    slot_index = jnp.sum(before * onehot, axis=1) - part * part_cap
    valid = (slot_index >= 0) & (slot_index < part_cap)
    target = jnp.where(valid, route_ids * part_cap + slot_index, -1)
    select = (jnp.arange(experts * part_cap, dtype=jnp.int32)[:, None] == target[None, :]).astype(bf16)

    def route(values):
        routed = dot(select, values, 1, 0).astype(bf16)
        routed = routed.reshape(experts, part_cap, GROUP, block_width).transpose(0, 2, 1, 3)
        return routed.reshape(places, part_cap, block_width)

    routed = jnp.concatenate([route(tokens), route(cotangent)], axis=2)
    got = lax.all_to_all(routed, "expert", split_axis=0, concat_axis=0, tiled=True)
    got = got.reshape(places // GROUP, GROUP, part_cap, 2 * block_width).transpose(1, 0, 2, 3)
    got = got.reshape(GROUP, -1, 2 * block_width)

    def exchanged(own):
        pairs = [swap(own, MASKS[k]) for k in sets]
        return (own, swap(own, 1, "ffn")), [(pair, swap(pair, 1, "ffn")) for pair in pairs]

    got_tokens, got_cotangent = got[:, :, :block_width], got[:, :, block_width:]
    own_tokens, pair_tokens = exchanged(got_tokens)
    own_cotangent, pair_cotangent = exchanged(got_cotangent)

    def scatter_sum(own, pairs, weight, got_weights, by_row):
        results, rows, kept = [], [], []
        received = []
        for k in sets:
            count = own[0].shape[1] * 2 * 4
            args = (k, bounds[k][0], halves[k], by_row)
            row, sent = call(
                functools.partial(sent_kernel, *args),
                (shape((2, count, 2 * block_width), bf16), shape((count, halves[k]), bf16)),
                *own, *pairs[k], weight, got_weights[k],
            )
            rows.append(row)
            received.append(swap(sent, firsts[k]))
        for k in sets:
            count = rows[k].shape[1] // 2
            args = (k, bounds[k][0], halves[k], by_row)
            keep, sent = call(
                functools.partial(kept_kernel, *args),
                (shape((count, halves[k]), f32), shape((count, halves[k]), bf16)),
                rows[k], weight, got_weights[k], received[k],
            )
            kept.append((keep, swap(sent, seconds[k])))
        return rows, [keep + got.astype(f32) for keep, got in kept]

    def gather(owns):
        near = [jnp.concatenate([owns[k], swap(owns[k], seconds[k])]) for k in sets]
        return [(near[k], swap(near[k], firsts[k])) for k in sets]

    token_rows, pre = scatter_sum(own_tokens, pair_tokens, local_in, in_got, False)
    cotangent_rows, back = scatter_sum(own_cotangent, pair_cotangent, local_out, out_got, True)
    acts = [gelu_pair(value) for value in pre]
    hidden = gather([act[0].astype(bf16) for act in acts])
    pre_grad = gather([(value * act[1]).astype(bf16) for value, act in zip(back, acts)])

    def gradient(rows, values, hidden_first):
        half, wide = values[0].shape[1], 2 * block_width
        grad_shape = (half, wide) if hidden_first else (wide, half)
        sent_shape = (half, block_width) if hidden_first else (block_width, half)
        return call(
            functools.partial(gradient_kernel, hidden_first),
            (shape(grad_shape, f32), shape(sent_shape, bf16), shape((8, wide), f32), shape((8, half), f32)),
            rows, *values,
        )

    out_results = [gradient(cotangent_rows[k], hidden[k], True) for k in sets]
    out_sent = [result[1] for result in out_results]
    pre_grad, out_sent = lax.optimization_barrier((pre_grad, out_sent))
    got_out = [swap(out_sent[k], MASKS[k]) for k in sets]
    in_results = [gradient(token_rows[k], pre_grad[k], False) for k in sets]
    got_in = [swap(in_results[k][1], MASKS[k]) for k in sets]

    lanes = max(block_width, *halves)
    width_pick = lax.dynamic_index_in_dim(width_states, expert, 1, keepdims=False)
    hidden_pick = lax.dynamic_index_in_dim(hidden_states, expert, 1, keepdims=False)

    def padded(values):
        return jnp.pad(values, ((0, 0), (0, lanes - values.shape[1])), constant_values=1.0)

    prev = [padded(width_pick.reshape(2 * GROUP, block_width))]
    for which in range(2):
        for k in sets:
            low, high = bounds[k]
            prev.append(padded(hidden_pick[which, low:high].reshape(2, halves[k])))
    prev.append(jnp.ones((STAT_ROWS - TOTALS, lanes), f32))
    prev = jnp.concatenate(prev)

    def cube_total(values):
        values = values + swap(values, 1) + swap(values, 2) + swap(values, 3)
        return values + swap(values, 4)

    def whole_tiles(values):
        return values if values.shape[1] > 128 else jnp.pad(values, ((0, 0), (0, lanes - values.shape[1])))

    sums = []
    for results in (in_results, out_results):
        sums += [result[2] for result in results] + [whole_tiles(result[3]) for result in results]
    stats = call(collect_kernel, shape((STAT_ROWS, lanes), f32), hidden_pick[1:2], *sums)
    group_sums = cube_total(stats)
    whole_sums = ffn_total(group_sums)
    grads = [result[0] for result in in_results] + [result[0] for result in out_results]
    factors, norms = call(
        norm_kernel,
        (shape((STAT_ROWS, lanes), f32), shape((8, 128), f32)),
        prev, group_sums, whole_sums, *grads,
    )
    norms = ffn_total(cube_total(norms))
    update_in, update_out = call(
        functools.partial(final_kernel, bounds),
        (shape(local_in.shape, bf16), shape(local_out.shape, bf16)),
        prev, factors, whole_sums, norms, *grads, *got_in, *got_out,
    )
    return (update_in[None], update_out[None])


def solution(mesh):
    return jax.shard_map(
        shards,
        mesh=mesh,
        in_specs=(
            P("expert", None),
            P("expert", None),
            P("expert", None),
            P("expert", None, "ffn"),
            P("expert", "ffn", None),
            P(),
            P(None, None, "ffn"),
        ),
        out_specs=(P("expert", None, "ffn"), P("expert", "ffn", None)),
        check_vma=False,
    )
```

```python
import functools
import math

import jax
import jax.numpy as jnp
from jax import lax
from jax.experimental import pallas as pl
from jax.experimental.pallas import tpu as pltpu
from jax.sharding import PartitionSpec as P

D = 4096
FF = 5120
GROUP = 8


DECAY_RATE = 0.9
EPS_ONE = 1e-30
ROOT_COEF = math.sqrt(2.0 / math.pi)
CUBIC_COEF = 0.044715

MASKS = (1, 2, 4)

MIB = 1024 * 1024


def swap(value, mask, axis="expert"):
    pairs = [(source, source ^ mask) for source in range(lax.axis_size(axis))]
    return lax.ppermute(value, axis, pairs)


def gelu_pair(inputs):
    inner = ROOT_COEF * (inputs + CUBIC_COEF * inputs * inputs * inputs)
    tangent = jnp.tanh(inner)
    act_value = 0.5 * inputs * (1.0 + tangent)
    act_slope = 0.5 * (1.0 + tangent) + 0.5 * inputs * (1.0 - tangent * tangent) * ROOT_COEF * (
        1.0 + 3.0 * CUBIC_COEF * inputs * inputs
    )
    return (act_value, act_slope)


def ffn_total(values):
    mask = 1
    while mask < lax.axis_size("ffn"):
        values = values + swap(values, mask, "ffn")
        mask *= 2
    return values


def set_bounds(hidden):
    unit = next(unit for unit in (256, 128, 2) if hidden % unit == 0 and hidden // unit >= 3)
    units = hidden // unit
    bounds, low = [], 0
    for k in range(3):
        high = low + (units // 3 + (k < units % 3)) * unit
        bounds.append((low, high))
        low = high
    return bounds


def dot(left, right, left_dim, right_dim):
    return lax.dot_general(
        left, right, (((left_dim,), (right_dim,)), ((), ())), preferred_element_type=jnp.float32
    )


def call(kernel, mib, out_shape, *operands):
    return pl.pallas_call(
        kernel,
        out_shape=out_shape,
        in_specs=[pl.BlockSpec(memory_space=pltpu.VMEM)] * len(operands),
        out_specs=jax.tree.map(lambda _: pl.BlockSpec(memory_space=pltpu.VMEM), out_shape),
        compiler_params=pltpu.CompilerParams(vmem_limit_bytes=mib * MIB),
    )(*operands)


def place_in_group():
    return lax.rem(lax.axis_index("expert"), GROUP)


def bit(place, k):
    return lax.rem(lax.div(place, 1 << k), 2)


def flipped(place, mask):
    for k in range(3):
        if mask >> k & 1:
            place = place + (1 - 2 * bit(place, k)) * (1 << k)
    return place


def weight_part(weight_ref, k, low, half, by_row):
    side = bit(place_in_group(), k)
    if by_row:
        return weight_ref[pl.ds(pl.multiple_of(low + side * half, math.gcd(low, half)), half), :]
    if half % 128 == 0:
        return weight_ref[:, pl.ds(pl.multiple_of(low + side * half, 128), half)]
    return jnp.where(side == 1, weight_ref[:, low + half : low + 2 * half], weight_ref[:, low : low + half])


def partial_sum(rows, own_weight, got_weight, by_row):
    width = rows.shape[1] // 2
    contract = 1 if by_row else 0
    return dot(rows[:, :width], own_weight, 1, contract) + dot(rows[:, width:], got_weight, 1, contract)


def sums_kernel(bounds, by_row, *refs):
    own, own_other, pairs, weight, got_weights = refs[0], refs[1], refs[2:8], refs[8], refs[9:12]
    rows_out, sent_out, kept_out = refs[12:15], refs[15:18], refs[18:21]
    count, width = own.shape[1], own.shape[2]
    for k in range(3):
        pair, pair_other = pairs[2 * k : 2 * k + 2]
        first, second = 1 << (k + 1) % 3, 1 << (k + 2) % 3
        for i in range(2):
            for j in range(2):
                for l in range(2):
                    chunk = flipped(place_in_group(), i * first + j * second + l * (1 << k))
                    at = (j * 2 + l) * 2 * count
                    rows_out[k][i, at : at + count, :width] = own[chunk]
                    rows_out[k][i, at : at + count, width:] = pair[chunk]
                    rows_out[k][i, at + count : at + 2 * count, :width] = own_other[chunk]
                    rows_out[k][i, at + count : at + 2 * count, width:] = pair_other[chunk]
        own_weight = weight_part(weight, k, bounds[k][0], (bounds[k][1] - bounds[k][0]) // 2, by_row)
        got_weight = got_weights[k][...]
        sent_out[k][...] = partial_sum(rows_out[k][1], own_weight, got_weight, by_row).astype(jnp.bfloat16)
        kept_out[k][...] = partial_sum(rows_out[k][0], own_weight, got_weight, by_row)


def add_kernel(*refs):
    kept, received, total_out, sent_out = refs[:3], refs[3:6], refs[6:9], refs[9:12]
    for k in range(3):
        middle = kept[k].shape[0] // 2
        total_out[k][...] = kept[k][:middle] + received[k][:middle].astype(jnp.float32)
        total = kept[k][middle:] + received[k][middle:].astype(jnp.float32)
        sent_out[k][...] = total.astype(jnp.bfloat16)


def hidden_kernel(*refs):
    kept, received, hidden_out, slope_out = refs[:3], refs[3:6], refs[6:9], refs[9:12]
    for k in range(3):
        act_value, act_slope = gelu_pair(kept[k][...] + received[k][...].astype(jnp.float32))
        hidden_out[k][...] = act_value.astype(jnp.bfloat16)
        slope_out[k][...] = act_slope


def pre_grad_kernel(*refs):
    kept, received, slope, pre_grad_out = refs[:3], refs[3:6], refs[6:9], refs[9:12]
    for k in range(3):
        value = (kept[k][...] + received[k][...].astype(jnp.float32)) * slope[k][...]
        pre_grad_out[k][...] = value.astype(jnp.bfloat16)


def gradient_kernel(hidden_first, *refs):
    all_rows, values, outs = refs[:3], refs[3:15], refs[15:]
    width = all_rows[0].shape[2] // 2
    for k in range(3):
        rows = all_rows[k]
        pieces = values[4 * k : 4 * k + 4]
        own_out, sent_out, by_width_out, by_hidden_out = outs[4 * k : 4 * k + 4]
        near = jnp.concatenate([pieces[0][...], pieces[1][...]])
        far = jnp.concatenate([pieces[2][...], pieces[3][...]])
        if hidden_first:
            grad = dot(near, rows[0], 0, 0) + dot(far, rows[1], 0, 0)
            own_out[...] = grad[:, :width]
            sent_out[...] = grad[:, width:].astype(sent_out.dtype)
        else:
            grad = dot(rows[0], near, 0, 0) + dot(rows[1], far, 0, 0)
            own_out[...] = grad[:width]
            sent_out[...] = grad[width:].astype(sent_out.dtype)
        square = grad * grad + EPS_ONE
        down = jnp.sum(square, axis=0, keepdims=True)
        across = dot(jnp.ones((8, square.shape[1]), jnp.float32), square, 1, 1)
        down = jnp.broadcast_to(down, (8, square.shape[1]))
        by_width_out[...] = down if hidden_first else across
        by_hidden_out[...] = across if hidden_first else down


IN_WIDTH, OUT_WIDTH, IN_HIDDEN, OUT_HIDDEN, TOTALS, STAT_ROWS = 0, 8, 16, 22, 28, 32


def collect_kernel(hidden_prev, *refs):
    stats_out = refs[-1]
    place = place_in_group()
    stats_out[...] = jnp.zeros_like(stats_out)
    lanes = stats_out.shape[1]
    for which in range(2):
        by_width, by_hidden = refs[which * 6 : which * 6 + 3], refs[which * 6 + 3 : which * 6 + 6]
        width_row, hidden_row = (IN_WIDTH, OUT_WIDTH)[which], (IN_HIDDEN, OUT_HIDDEN)[which]
        width = by_width[0].shape[1] // 2
        own = sum(ref[0:1, :width] for ref in by_width)
        stats_out[pl.ds(width_row + place, 1), :width] = own
        total = 0.0
        for k in range(3):
            stats_out[pl.ds(width_row + flipped(place, 1 << k), 1), :width] = by_width[k][0:1, width:]
            half = by_hidden[k].shape[1]
            row = by_hidden[k][0:1, :]
            stats_out[pl.ds(hidden_row + 2 * k + bit(place, k), 1), :half] = row
            total = total + jnp.sum(row, axis=1, keepdims=True)
        stats_out[TOTALS + which : TOTALS + which + 1, :] = jnp.broadcast_to(total, (1, lanes))
    previous = jnp.sum(hidden_prev[...], axis=1, keepdims=True)
    stats_out[TOTALS + 2 : TOTALS + 3, :] = jnp.broadcast_to(previous, (1, lanes))


def stat_row(stats_ref, index):
    return stats_ref[pl.ds(index, 1), :]


def upright(row):
    return jnp.transpose(jnp.broadcast_to(row, (8, row.shape[1])))[:, 0:1]


def norm_kernel(prev, group_sums, whole_sums, *refs):
    own_in, sent_in, own_out, sent_out = refs[:3], refs[3:6], refs[6:9], refs[9:12]
    factors_out, norms_out = refs[12], refs[13]
    place = place_in_group()
    width = own_in[0].shape[0]
    row = lax.broadcasted_iota(jnp.int32, prev.shape, 0)
    by_width = row < IN_HIDDEN
    mean = jnp.where(by_width, whole_sums[...] / FF, group_sums[...] / D)
    factors_out[...] = DECAY_RATE * prev[...] + (1.0 - DECAY_RATE) * mean
    norm_in, norm_out = 0.0, 0.0
    for k in range(3):
        half = own_in[k].shape[1]
        partner = flipped(place, 1 << k)
        own_row = stat_row(factors_out, IN_WIDTH + place)[:, :width]
        pair_row = stat_row(factors_out, IN_WIDTH + partner)[:, :width]
        hidden_row = stat_row(factors_out, IN_HIDDEN + 2 * k + bit(place, k))[:, :half]
        sent = sent_in[k][...].astype(jnp.float32)
        down = jnp.sum(own_in[k][...] * own_in[k][...] * upright(1.0 / own_row), axis=0, keepdims=True)
        down = down + jnp.sum(sent * sent * upright(1.0 / pair_row), axis=0, keepdims=True)
        norm_in = norm_in + jnp.sum(down / hidden_row, axis=1, keepdims=True)
        own_row = stat_row(factors_out, OUT_WIDTH + place)[:, :width]
        pair_row = stat_row(factors_out, OUT_WIDTH + partner)[:, :width]
        hidden_row = stat_row(factors_out, OUT_HIDDEN + 2 * k + bit(place, k))[:, :half]
        inverse = upright(1.0 / hidden_row)
        sent = sent_out[k][...].astype(jnp.float32)
        down = jnp.sum(own_out[k][...] * own_out[k][...] * inverse, axis=0, keepdims=True) / own_row
        down = down + jnp.sum(sent * sent * inverse, axis=0, keepdims=True) / pair_row
        norm_out = norm_out + jnp.sum(down, axis=1, keepdims=True)
    row = lax.broadcasted_iota(jnp.int32, norms_out.shape, 0)
    norms_out[...] = jnp.where(row == 0, norm_in, norm_out)


def final_kernel(bounds, prev, factors, whole_sums, norms, *refs):
    own_in, own_out, got_in, got_out = refs[:3], refs[3:6], refs[6:9], refs[9:12]
    update_in, update_out = refs[12:]
    place = place_in_group()
    width = update_in.shape[0]
    count = float(D) * float(FF)
    mean_in = DECAY_RATE * jnp.mean(prev[IN_WIDTH : IN_WIDTH + 8, :width], keepdims=True)
    mean_in = mean_in + (1.0 - DECAY_RATE) * whole_sums[TOTALS : TOTALS + 1, 0:1] / count
    mean_out = DECAY_RATE * whole_sums[TOTALS + 2 : TOTALS + 3, 0:1] / (FF * GROUP)
    mean_out = mean_out + (1.0 - DECAY_RATE) * whole_sums[TOTALS + 1 : TOTALS + 2, 0:1] / count
    factor_in = jnp.sqrt(mean_in) / jnp.maximum(1.0, jnp.sqrt(mean_in * norms[0:1, 0:1] / count))
    factor_out = jnp.sqrt(mean_out) / jnp.maximum(1.0, jnp.sqrt(mean_out * norms[1:2, 0:1] / count))
    width_in = upright(lax.rsqrt(stat_row(factors, IN_WIDTH + place)[:, :width]) * factor_in)
    width_out = lax.rsqrt(stat_row(factors, OUT_WIDTH + place)[:, :width]) * factor_out
    for k in range(3):
        low, half = bounds[k][0], (bounds[k][1] - bounds[k][0]) // 2
        own_bit = bit(place, k)
        if half % 128:
            width_scaled = (own_in[k][...] * width_in, got_in[k][...].astype(jnp.float32) * width_in)
            for side in range(2):
                hidden_in = lax.rsqrt(factors[IN_HIDDEN + 2 * k + side : IN_HIDDEN + 2 * k + side + 1, :half])
                value = jnp.where(own_bit == side, *width_scaled) * hidden_in
                update_in[:, low + side * half : low + side * half + half] = value.astype(update_in.dtype)
        for own in (True, False):
            side = own_bit if own else 1 - own_bit
            start = pl.multiple_of(low + side * half, math.gcd(low, half))
            hidden_out = upright(lax.rsqrt(stat_row(factors, OUT_HIDDEN + 2 * k + side)[:, :half]))
            if half % 128 == 0:
                hidden_in = lax.rsqrt(stat_row(factors, IN_HIDDEN + 2 * k + side)[:, :half])
                value = own_in[k][...] if own else got_in[k][...].astype(jnp.float32)
                update_in[:, pl.ds(start, half)] = (value * width_in * hidden_in).astype(update_in.dtype)
            value = own_out[k][...] if own else got_out[k][...].astype(jnp.float32)
            update_out[pl.ds(start, half), :] = (value * hidden_out * width_out).astype(update_out.dtype)


def shards(tokens, cotangent, expert_ids, in_weight, out_weight, width_states, hidden_states):
    bf16, f32 = jnp.bfloat16, jnp.float32
    shape = jax.ShapeDtypeStruct
    experts = width_states.shape[1]
    tok_rows, width = tokens.shape
    capacity = 5 * tok_rows // (4 * experts)
    part_cap = capacity // 2
    places = lax.axis_size("expert")
    block_width = width // GROUP
    position = lax.axis_index("expert")
    expert = position // GROUP
    part = lax.axis_index("ffn") % 2
    bits = [position >> k & 1 for k in range(3)]
    bounds = set_bounds(in_weight.shape[2])
    halves = [(high - low) // 2 for low, high in bounds]
    sets = range(3)
    firsts = [MASKS[(k + 1) % 3] for k in sets]
    seconds = [MASKS[(k + 2) % 3] for k in sets]
    local_in = in_weight[0]
    local_out = out_weight[0]

    def pair_side(values, k, dim):
        return lax.dynamic_slice_in_dim(values, bounds[k][0] + (1 - bits[k]) * halves[k], halves[k], dim)

    in_got = [swap(pair_side(local_in, k, 1), MASKS[k]) for k in sets]
    out_got = [swap(pair_side(local_out, k, 0), MASKS[k]) for k in sets]

    route_ids = expert_ids[:, 0]
    onehot = (route_ids[:, None] == jnp.arange(experts, dtype=jnp.int32)[None, :]).astype(jnp.int32)
    before = jnp.cumsum(onehot, axis=0) - onehot
    slot_index = jnp.sum(before * onehot, axis=1) - part * part_cap
    valid = (slot_index >= 0) & (slot_index < part_cap)
    target = jnp.where(valid, route_ids * part_cap + slot_index, -1)
    select = (jnp.arange(experts * part_cap, dtype=jnp.int32)[:, None] == target[None, :]).astype(bf16)

    def route(values):
        routed = dot(select, values, 1, 0).astype(bf16)
        routed = routed.reshape(experts, part_cap, GROUP, block_width).transpose(0, 2, 1, 3)
        return routed.reshape(places, part_cap, block_width)

    routed = jnp.concatenate([route(tokens), route(cotangent)], axis=2)
    routed, in_got, out_got = lax.optimization_barrier((routed, in_got, out_got))
    got = lax.all_to_all(routed, "expert", split_axis=0, concat_axis=0, tiled=True)
    got = got.reshape(places // GROUP, GROUP, part_cap, 2 * block_width).transpose(1, 0, 2, 3)
    got = got.reshape(GROUP, -1, 2 * block_width)

    def exchanged(own):
        pairs = [swap(own, MASKS[k]) for k in sets]
        return (own, swap(own, 1, "ffn")), [(pair, swap(pair, 1, "ffn")) for pair in pairs]

    got_tokens, got_cotangent = got[:, :, :block_width], got[:, :, block_width:]
    own_tokens, pair_tokens = exchanged(got_tokens)
    own_cotangent, pair_cotangent = exchanged(got_cotangent)

    def shapes(rows, dtype):
        return [shape((rows, half), dtype) for half in halves]

    count = got.shape[1] * 8
    wide = 2 * block_width

    def scatter_sum(own, pairs, weight, got_weights, by_row):
        outs = call(
            functools.partial(sums_kernel, bounds, by_row), 40,
            [shape((2, count, wide), bf16)] * 3 + shapes(count, bf16) + shapes(count, f32),
            *own, *pairs[0], *pairs[1], *pairs[2], weight, *got_weights,
        )
        rows, sent, kept = outs[:3], outs[3:6], outs[6:]
        received = [swap(sent[k], firsts[k]) for k in sets]
        outs = call(add_kernel, 16, shapes(count // 2, f32) + shapes(count // 2, bf16), *kept, *received)
        kept, sent = outs[:3], outs[3:]
        return rows, kept, [swap(sent[k], seconds[k]) for k in sets]

    def gather(owns):
        pieces = []
        for k in sets:
            near = swap(owns[k], seconds[k])
            pieces += [owns[k], near, swap(owns[k], firsts[k]), swap(near, firsts[k])]
        return pieces

    token_rows, *pre = scatter_sum(own_tokens, pair_tokens, local_in, in_got, False)
    cotangent_rows, *back = scatter_sum(own_cotangent, pair_cotangent, local_out, out_got, True)
    outs = call(hidden_kernel, 16, shapes(count // 2, bf16) + shapes(count // 2, f32), *pre[0], *pre[1])
    hidden, slope = gather(outs[:3]), outs[3:]
    outs = call(pre_grad_kernel, 16, shapes(count // 2, bf16), *back[0], *back[1], *slope)
    pre_grad = gather(outs)

    def gradient(rows, values, hidden_first):
        out_shapes = []
        for half in halves:
            part = (half, block_width) if hidden_first else (block_width, half)
            out_shapes += [shape(part, f32), shape(part, bf16), shape((8, wide), f32), shape((8, half), f32)]
        outs = call(functools.partial(gradient_kernel, hidden_first), 40, out_shapes, *rows, *values)
        return outs[0::4], outs[1::4], outs[2::4], outs[3::4]

    out_own, out_sent, *out_sums = gradient(cotangent_rows, hidden, True)
    got_out = [swap(out_sent[k], MASKS[k]) for k in sets]
    pre_grad, got_out = lax.optimization_barrier((pre_grad, got_out))
    in_own, in_sent, *in_sums = gradient(token_rows, pre_grad, False)
    got_in = [swap(in_sent[k], MASKS[k]) for k in sets]

    lanes = max(block_width, *halves)
    width_pick = lax.dynamic_index_in_dim(width_states, expert, 1, keepdims=False)
    hidden_pick = lax.dynamic_index_in_dim(hidden_states, expert, 1, keepdims=False)

    def padded(values):
        return jnp.pad(values, ((0, 0), (0, lanes - values.shape[1])), constant_values=1.0)

    prev = [padded(width_pick.reshape(2 * GROUP, block_width))]
    for which in range(2):
        for k in sets:
            low, high = bounds[k]
            prev.append(padded(hidden_pick[which, low:high].reshape(2, halves[k])))
    prev.append(jnp.ones((STAT_ROWS - TOTALS, lanes), f32))
    prev = jnp.concatenate(prev)

    def cube_total(values):
        values = values + swap(values, 1) + swap(values, 2) + swap(values, 3)
        return values + swap(values, 4)

    def whole_tiles(values):
        return values if values.shape[1] > 128 else jnp.pad(values, ((0, 0), (0, lanes - values.shape[1])))

    sums = []
    for by_width, by_hidden in (in_sums, out_sums):
        sums += [*by_width, *map(whole_tiles, by_hidden)]
    stats = call(collect_kernel, 4, shape((STAT_ROWS, lanes), f32), hidden_pick[1:2], *sums)
    group_sums = cube_total(stats)
    whole_sums = ffn_total(group_sums)
    whole_sums, got_in = lax.optimization_barrier((whole_sums, got_in))
    factors, norms = call(
        norm_kernel, 20,
        (shape((STAT_ROWS, lanes), f32), shape((8, 128), f32)),
        prev, group_sums, whole_sums, *in_own, *in_sent, *out_own, *out_sent,
    )
    norms = ffn_total(cube_total(norms))
    update_in, update_out = call(
        functools.partial(final_kernel, bounds), 24,
        (shape(local_in.shape, bf16), shape(local_out.shape, bf16)),
        prev, factors, whole_sums, norms, *in_own, *out_own, *got_in, *got_out,
    )
    return (update_in[None], update_out[None])


def solution(mesh):
    return jax.shard_map(
        shards,
        mesh=mesh,
        in_specs=(
            P("expert", None),
            P("expert", None),
            P("expert", None),
            P("expert", None, "ffn"),
            P("expert", "ffn", None),
            P(),
            P(None, None, "ffn"),
        ),
        out_specs=(P("expert", None, "ffn"), P("expert", "ffn", None)),
        check_vma=False,
    )
```

```python
import functools
import math

import jax
import jax.numpy as jnp
from jax import lax
from jax.experimental import pallas as pl
from jax.experimental.pallas import tpu as pltpu
from jax.sharding import PartitionSpec as P

D = 4096
FF = 5120
GROUP = 8


DECAY_RATE = 0.9
EPS_ONE = 1e-30
ROOT_COEF = math.sqrt(2.0 / math.pi)
CUBIC_COEF = 0.044715

MASKS = (1, 2, 4)

MIB = 1024 * 1024


def swap(value, mask, axis="expert"):
    pairs = [(source, source ^ mask) for source in range(lax.axis_size(axis))]
    return lax.ppermute(value, axis, pairs)


def gelu_pair(inputs):
    inner = ROOT_COEF * (inputs + CUBIC_COEF * inputs * inputs * inputs)
    tangent = jnp.tanh(inner)
    act_value = 0.5 * inputs * (1.0 + tangent)
    act_slope = 0.5 * (1.0 + tangent) + 0.5 * inputs * (1.0 - tangent * tangent) * ROOT_COEF * (
        1.0 + 3.0 * CUBIC_COEF * inputs * inputs
    )
    return (act_value, act_slope)


def ffn_total(values):
    mask = 1
    while mask < lax.axis_size("ffn"):
        values = values + swap(values, mask, "ffn")
        mask *= 2
    return values


def set_bounds(hidden):
    unit = next(unit for unit in (256, 128, 2) if hidden % unit == 0 and hidden // unit >= 3)
    units = hidden // unit
    bounds, low = [], 0
    for k in range(3):
        high = low + (units // 3 + (k < units % 3)) * unit
        bounds.append((low, high))
        low = high
    return bounds


def dot(left, right, left_dim, right_dim):
    return lax.dot_general(
        left, right, (((left_dim,), (right_dim,)), ((), ())), preferred_element_type=jnp.float32
    )


def call(kernel, mib, out_shape, *operands, scratch=(), whole=False):
    space = pl.ANY if whole else pltpu.VMEM
    return pl.pallas_call(
        kernel,
        out_shape=out_shape,
        in_specs=[pl.BlockSpec(memory_space=space)] * len(operands),
        out_specs=jax.tree.map(lambda _: pl.BlockSpec(memory_space=pltpu.VMEM), out_shape),
        scratch_shapes=list(scratch),
        compiler_params=pltpu.CompilerParams(vmem_limit_bytes=mib * MIB),
    )(*operands)


def place_in_group():
    return lax.rem(lax.axis_index("expert"), GROUP)


def bit(place, k):
    return lax.rem(lax.div(place, 1 << k), 2)


def flipped(place, mask):
    for k in range(3):
        if mask >> k & 1:
            place = place + (1 - 2 * bit(place, k)) * (1 << k)
    return place


def partial_sum(rows, own_weight, got_weight, by_row):
    width = rows.shape[1] // 2
    contract = 1 if by_row else 0
    return dot(rows[:, :width], own_weight, 1, contract) + dot(rows[:, width:], got_weight, 1, contract)


def cut_kernel(bounds, weight_in, weight_out, *refs):
    cuts, sems = refs[:12], refs[12]
    copies = []
    for k in range(3):
        low, half = bounds[k][0], (bounds[k][1] - bounds[k][0]) // 2
        side = bit(place_in_group(), k)
        for taken in range(2):
            at = (1 - side) if taken else side
            part = pl.ds(pl.multiple_of(low + at * half, 128), half)
            n = 6 * taken + k
            copies.append(pltpu.make_async_copy(weight_in.at[:, part], cuts[n], sems.at[n]))
            copies.append(pltpu.make_async_copy(weight_out.at[part, :], cuts[n + 3], sems.at[n + 3]))
    for copy in copies:
        copy.start()
    for copy in copies:
        copy.wait()


def sums_kernel(side, by_row, *refs):
    own, own_other, pairs, own_weights, got_weights = refs[0], refs[1], refs[2:8], refs[8:11], refs[11:14]
    rows_out, sums_out = refs[14:17], refs[17:20]
    count, width = own.shape[1], own.shape[2]
    for k in range(3):
        pair, pair_other = pairs[2 * k : 2 * k + 2]
        first, second = 1 << (k + 1) % 3, 1 << (k + 2) % 3
        for j in range(2):
            for l in range(2):
                chunk = flipped(place_in_group(), side * first + j * second + l * (1 << k))
                at = (j * 2 + l) * 2 * count
                rows_out[k][at : at + count, :width] = own[chunk]
                rows_out[k][at : at + count, width:] = pair[chunk]
                rows_out[k][at + count : at + 2 * count, :width] = own_other[chunk]
                rows_out[k][at + count : at + 2 * count, width:] = pair_other[chunk]
        sums = partial_sum(rows_out[k][...], own_weights[k][...], got_weights[k][...], by_row)
        sums_out[k][...] = sums.astype(sums_out[k].dtype)


def add_kernel(*refs):
    kept, received, total_out, sent_out = refs[:3], refs[3:6], refs[6:9], refs[9:12]
    for k in range(3):
        middle = kept[k].shape[0] // 2
        total_out[k][...] = kept[k][:middle] + received[k][:middle].astype(jnp.float32)
        total = kept[k][middle:] + received[k][middle:].astype(jnp.float32)
        sent_out[k][...] = total.astype(jnp.bfloat16)


def hidden_kernel(*refs):
    kept, received, hidden_out, slope_out = refs[:3], refs[3:6], refs[6:9], refs[9:12]
    for k in range(3):
        act_value, act_slope = gelu_pair(kept[k][...] + received[k][...].astype(jnp.float32))
        hidden_out[k][...] = act_value.astype(jnp.bfloat16)
        slope_out[k][...] = act_slope


def pre_grad_kernel(*refs):
    kept, received, slope, pre_grad_out = refs[:3], refs[3:6], refs[6:9], refs[9:12]
    for k in range(3):
        value = (kept[k][...] + received[k][...].astype(jnp.float32)) * slope[k][...]
        pre_grad_out[k][...] = value.astype(jnp.bfloat16)


def gradients(hidden_first, near_rows, far_rows, values, own_out, sent_out, sums_out):
    width = near_rows[0].shape[1] // 2
    for k in range(3):
        pieces = values[4 * k : 4 * k + 4]
        near = jnp.concatenate([pieces[0][...], pieces[1][...]])
        far = jnp.concatenate([pieces[2][...], pieces[3][...]])
        if hidden_first:
            grad = dot(near, near_rows[k][...], 0, 0) + dot(far, far_rows[k][...], 0, 0)
            own_out[k][...] = grad[:, :width]
            sent_out[k][...] = grad[:, width:].astype(jnp.bfloat16)
        else:
            grad = dot(near_rows[k][...], near, 0, 0) + dot(far_rows[k][...], far, 0, 0)
            own_out[k][...] = grad[:width]
            sent_out[k][...] = grad[width:].astype(jnp.bfloat16)
        square = grad * grad + EPS_ONE
        down = jnp.sum(square, axis=0, keepdims=True)
        across = dot(jnp.ones((8, square.shape[1]), jnp.float32), square, 1, 1)
        down = jnp.broadcast_to(down, (8, square.shape[1]))
        by_width, by_hidden = (down, across) if hidden_first else (across, down)
        sums_out[k] = by_width
        sums_out[3 + k] = jnp.zeros(sums_out.shape[1:], jnp.float32)
        sums_out[3 + k, :, : by_hidden.shape[1]] = by_hidden


def grad_out_kernel(*refs):
    gradients(True, refs[:3], refs[3:6], refs[6:18], refs[18:21], refs[21:24], refs[24])


def grad_in_kernel(*refs):
    other_sums, hidden_prev, stats_out, sums = refs[18], refs[19], refs[26], refs[27]
    gradients(False, refs[:3], refs[3:6], refs[6:18], refs[20:23], refs[23:26], sums)
    collect(hidden_prev, (sums, other_sums), stats_out)


IN_WIDTH, OUT_WIDTH, IN_HIDDEN, OUT_HIDDEN, TOTALS, STAT_ROWS = 0, 8, 16, 22, 28, 32


def collect(hidden_prev, all_sums, stats_out):
    place = place_in_group()
    stats_out[...] = jnp.zeros_like(stats_out)
    lanes = stats_out.shape[1]
    for which in range(2):
        sums = all_sums[which]
        width_row, hidden_row = (IN_WIDTH, OUT_WIDTH)[which], (IN_HIDDEN, OUT_HIDDEN)[which]
        width = sums.shape[2] // 2
        stats_out[pl.ds(width_row + place, 1), :] = sum(sums[k, 0:1, :width] for k in range(3))
        total = 0.0
        for k in range(3):
            stats_out[pl.ds(width_row + flipped(place, 1 << k), 1), :] = sums[k, 0:1, width:]
            row = sums[3 + k, 0:1, :lanes]
            stats_out[pl.ds(hidden_row + 2 * k + bit(place, k), 1), :] = row
            total = total + jnp.sum(row, axis=1, keepdims=True)
        stats_out[TOTALS + which : TOTALS + which + 1, :] = jnp.broadcast_to(total, (1, lanes))
    previous = jnp.sum(hidden_prev[...], axis=1, keepdims=True)
    stats_out[TOTALS + 2 : TOTALS + 3, :] = jnp.broadcast_to(previous, (1, lanes))


def stat_row(stats_ref, index):
    return stats_ref[pl.ds(index, 1), :]


def upright(row):
    return jnp.transpose(jnp.broadcast_to(row, (8, row.shape[1])))[:, 0:1]


def norm_kernel(prev, group_sums, whole_sums, *refs):
    own_in, sent_in, own_out, sent_out = refs[:3], refs[3:6], refs[6:9], refs[9:12]
    factors_out, norms_out = refs[12], refs[13]
    place = place_in_group()
    width = own_in[0].shape[0]
    row = lax.broadcasted_iota(jnp.int32, prev.shape, 0)
    by_width = row < IN_HIDDEN
    mean = jnp.where(by_width, whole_sums[...] / FF, group_sums[...] / D)
    factors_out[...] = DECAY_RATE * prev[...] + (1.0 - DECAY_RATE) * mean
    norm_in, norm_out = 0.0, 0.0
    for k in range(3):
        half = own_in[k].shape[1]
        partner = flipped(place, 1 << k)
        own_row = stat_row(factors_out, IN_WIDTH + place)[:, :width]
        pair_row = stat_row(factors_out, IN_WIDTH + partner)[:, :width]
        hidden_row = stat_row(factors_out, IN_HIDDEN + 2 * k + bit(place, k))[:, :half]
        sent = sent_in[k][...].astype(jnp.float32)
        down = jnp.sum(own_in[k][...] * own_in[k][...] * upright(1.0 / own_row), axis=0, keepdims=True)
        down = down + jnp.sum(sent * sent * upright(1.0 / pair_row), axis=0, keepdims=True)
        norm_in = norm_in + jnp.sum(down / hidden_row, axis=1, keepdims=True)
        own_row = stat_row(factors_out, OUT_WIDTH + place)[:, :width]
        pair_row = stat_row(factors_out, OUT_WIDTH + partner)[:, :width]
        hidden_row = stat_row(factors_out, OUT_HIDDEN + 2 * k + bit(place, k))[:, :half]
        inverse = upright(1.0 / hidden_row)
        sent = sent_out[k][...].astype(jnp.float32)
        down = jnp.sum(own_out[k][...] * own_out[k][...] * inverse, axis=0, keepdims=True) / own_row
        down = down + jnp.sum(sent * sent * inverse, axis=0, keepdims=True) / pair_row
        norm_out = norm_out + jnp.sum(down, axis=1, keepdims=True)
    row = lax.broadcasted_iota(jnp.int32, norms_out.shape, 0)
    norms_out[...] = jnp.where(row == 0, norm_in, norm_out)


def final_kernel(bounds, prev, factors, whole_sums, norms, *refs):
    own_in, own_out, got_in, got_out = refs[:3], refs[3:6], refs[6:9], refs[9:12]
    update_in, update_out = refs[12:]
    place = place_in_group()
    width = update_in.shape[0]
    count = float(D) * float(FF)
    mean_in = DECAY_RATE * jnp.mean(prev[IN_WIDTH : IN_WIDTH + 8, :width], keepdims=True)
    mean_in = mean_in + (1.0 - DECAY_RATE) * whole_sums[TOTALS : TOTALS + 1, 0:1] / count
    mean_out = DECAY_RATE * whole_sums[TOTALS + 2 : TOTALS + 3, 0:1] / (FF * GROUP)
    mean_out = mean_out + (1.0 - DECAY_RATE) * whole_sums[TOTALS + 1 : TOTALS + 2, 0:1] / count
    factor_in = jnp.sqrt(mean_in) / jnp.maximum(1.0, jnp.sqrt(mean_in * norms[0:1, 0:1] / count))
    factor_out = jnp.sqrt(mean_out) / jnp.maximum(1.0, jnp.sqrt(mean_out * norms[1:2, 0:1] / count))
    width_in = upright(lax.rsqrt(stat_row(factors, IN_WIDTH + place)[:, :width]) * factor_in)
    width_out = lax.rsqrt(stat_row(factors, OUT_WIDTH + place)[:, :width]) * factor_out
    for k in range(3):
        low, half = bounds[k][0], (bounds[k][1] - bounds[k][0]) // 2
        own_bit = bit(place, k)
        if half % 128:
            width_scaled = (own_in[k][...] * width_in, got_in[k][...].astype(jnp.float32) * width_in)
            for side in range(2):
                hidden_in = lax.rsqrt(factors[IN_HIDDEN + 2 * k + side : IN_HIDDEN + 2 * k + side + 1, :half])
                value = jnp.where(own_bit == side, *width_scaled) * hidden_in
                update_in[:, low + side * half : low + side * half + half] = value.astype(update_in.dtype)
        for own in (True, False):
            side = own_bit if own else 1 - own_bit
            start = pl.multiple_of(low + side * half, math.gcd(low, half))
            hidden_out = upright(lax.rsqrt(stat_row(factors, OUT_HIDDEN + 2 * k + side)[:, :half]))
            if half % 128 == 0:
                hidden_in = lax.rsqrt(stat_row(factors, IN_HIDDEN + 2 * k + side)[:, :half])
                value = own_in[k][...] if own else got_in[k][...].astype(jnp.float32)
                update_in[:, pl.ds(start, half)] = (value * width_in * hidden_in).astype(update_in.dtype)
            value = own_out[k][...] if own else got_out[k][...].astype(jnp.float32)
            update_out[pl.ds(start, half), :] = (value * hidden_out * width_out).astype(update_out.dtype)


def shards(tokens, cotangent, expert_ids, in_weight, out_weight, width_states, hidden_states):
    bf16, f32 = jnp.bfloat16, jnp.float32
    shape = jax.ShapeDtypeStruct
    experts = width_states.shape[1]
    tok_rows, width = tokens.shape
    capacity = 5 * tok_rows // (4 * experts)
    part_cap = capacity // 2
    places = lax.axis_size("expert")
    block_width = width // GROUP
    position = lax.axis_index("expert")
    expert = position // GROUP
    part = lax.axis_index("ffn") % 2
    bits = [position >> k & 1 for k in range(3)]
    bounds = set_bounds(in_weight.shape[2])
    halves = [(high - low) // 2 for low, high in bounds]
    sets = range(3)
    firsts = [MASKS[(k + 1) % 3] for k in sets]
    seconds = [MASKS[(k + 2) % 3] for k in sets]
    local_in = in_weight[0]
    local_out = out_weight[0]

    if all(half % 128 == 0 for half in halves):
        cut_shapes = [shape((block_width, half), bf16) for half in halves]
        cut_shapes += [shape((half, block_width), bf16) for half in halves]
        cuts = call(
            functools.partial(cut_kernel, bounds), 48, cut_shapes * 2, local_in, local_out,
            scratch=[pltpu.SemaphoreType.DMA((12,))], whole=True,
        )
    else:
        cuts = []
        for taken in range(2):
            at = [bounds[k][0] + (1 - bits[k] if taken else bits[k]) * halves[k] for k in sets]
            cuts += [lax.dynamic_slice_in_dim(local_in, at[k], halves[k], 1) for k in sets]
            cuts += [lax.dynamic_slice_in_dim(local_out, at[k], halves[k], 0) for k in sets]
    in_own_weights, out_own_weights = cuts[:3], cuts[3:6]
    in_got = [swap(cuts[6 + k], MASKS[k]) for k in sets]
    out_got = [swap(cuts[9 + k], MASKS[k]) for k in sets]

    route_ids = expert_ids[:, 0]
    onehot = (route_ids[:, None] == jnp.arange(experts, dtype=jnp.int32)[None, :]).astype(jnp.int32)
    before = jnp.cumsum(onehot, axis=0) - onehot
    slot_index = jnp.sum(before * onehot, axis=1) - part * part_cap
    valid = (slot_index >= 0) & (slot_index < part_cap)
    target = jnp.where(valid, route_ids * part_cap + slot_index, -1)
    select = (jnp.arange(experts * part_cap, dtype=jnp.int32)[:, None] == target[None, :]).astype(bf16)

    def route(values):
        routed = dot(select, values, 1, 0).astype(bf16)
        routed = routed.reshape(experts, part_cap, GROUP, block_width).transpose(0, 2, 1, 3)
        return routed.reshape(places, part_cap, block_width)

    routed = jnp.concatenate([route(tokens), route(cotangent)], axis=2)
    got = lax.all_to_all(routed, "expert", split_axis=0, concat_axis=0, tiled=True)
    got, in_got, out_got = lax.optimization_barrier((got, in_got, out_got))
    got = got.reshape(places // GROUP, GROUP, part_cap, 2 * block_width).transpose(1, 0, 2, 3)
    got = got.reshape(GROUP, -1, 2 * block_width)

    def exchanged(own):
        pairs = [swap(own, MASKS[k]) for k in sets]
        return (own, swap(own, 1, "ffn")), [(pair, swap(pair, 1, "ffn")) for pair in pairs]

    got_tokens, got_cotangent = got[:, :, :block_width], got[:, :, block_width:]
    own_tokens, pair_tokens = exchanged(got_tokens)
    own_cotangent, pair_cotangent = exchanged(got_cotangent)

    def shapes(rows, dtype):
        return [shape((rows, half), dtype) for half in halves]

    count = got.shape[1] * 8
    wide = 2 * block_width

    def scatter_sum(own, pairs, own_weights, got_weights, by_row):
        operands = (*own, *pairs[0], *pairs[1], *pairs[2], *own_weights, *got_weights)
        row_shapes = [shape((count, wide), bf16)] * 3
        outs = call(functools.partial(sums_kernel, 1, by_row), 24, row_shapes + shapes(count, bf16), *operands)
        far_rows, received = outs[:3], [swap(outs[3 + k], firsts[k]) for k in sets]
        outs = call(functools.partial(sums_kernel, 0, by_row), 24, row_shapes + shapes(count, f32), *operands)
        near_rows, kept = outs[:3], outs[3:]
        outs = call(add_kernel, 12, shapes(count // 2, f32) + shapes(count // 2, bf16), *kept, *received)
        return near_rows + far_rows, outs[:3], [swap(outs[3 + k], seconds[k]) for k in sets]

    def gather(owns):
        pieces = []
        for k in sets:
            near = swap(owns[k], seconds[k])
            pieces += [owns[k], near, swap(owns[k], firsts[k]), swap(near, firsts[k])]
        return pieces

    token_rows, *pre = scatter_sum(own_tokens, pair_tokens, in_own_weights, in_got, False)
    cotangent_rows, *back = scatter_sum(own_cotangent, pair_cotangent, out_own_weights, out_got, True)
    outs = call(hidden_kernel, 12, shapes(count // 2, bf16) + shapes(count // 2, f32), *pre[0], *pre[1])
    hidden, slope = gather(outs[:3]), outs[3:]
    outs = call(pre_grad_kernel, 12, shapes(count // 2, bf16), *back[0], *back[1], *slope)
    pre_grad = gather(outs)

    hidden, near = lax.optimization_barrier((hidden, pre_grad[1::4]))
    pre_grad[1::4] = near
    lanes = max(block_width, *halves)
    hidden_pick = lax.dynamic_index_in_dim(hidden_states, expert, 1, keepdims=False)
    sums_shape = (6, 8, wide)
    outs = call(
        grad_out_kernel, 24,
        [shape((half, block_width), f32) for half in halves]
        + [shape((half, block_width), bf16) for half in halves]
        + [shape(sums_shape, f32)],
        *cotangent_rows, *hidden,
    )
    out_own, out_sent, out_sums = outs[:3], outs[3:6], outs[6]
    got_out = [swap(out_sent[k], MASKS[k]) for k in sets]
    pre_grad, got_out = lax.optimization_barrier((pre_grad, got_out))
    outs = call(
        grad_in_kernel, 24,
        [shape((block_width, half), f32) for half in halves]
        + [shape((block_width, half), bf16) for half in halves]
        + [shape((STAT_ROWS, lanes), f32)],
        *token_rows, *pre_grad, out_sums, hidden_pick[1:2],
        scratch=[pltpu.VMEM(sums_shape, f32)],
    )
    in_own, in_sent, stats = outs[:3], outs[3:6], outs[6]
    got_in = [swap(in_sent[k], MASKS[k]) for k in sets]

    width_pick = lax.dynamic_index_in_dim(width_states, expert, 1, keepdims=False)

    def padded(values):
        return jnp.pad(values, ((0, 0), (0, lanes - values.shape[1])), constant_values=1.0)

    prev = [padded(width_pick.reshape(2 * GROUP, block_width))]
    for which in range(2):
        for k in sets:
            low, high = bounds[k]
            prev.append(padded(hidden_pick[which, low:high].reshape(2, halves[k])))
    prev.append(jnp.ones((STAT_ROWS - TOTALS, lanes), f32))
    prev = jnp.concatenate(prev)

    def cube_total(values):
        values = values + swap(values, 1) + swap(values, 2) + swap(values, 3)
        return values + swap(values, 4)

    group_sums = cube_total(stats)
    whole_sums = ffn_total(group_sums)
    whole_sums, got_in = lax.optimization_barrier((whole_sums, got_in))
    factors, norms = call(
        norm_kernel, 12,
        (shape((STAT_ROWS, lanes), f32), shape((8, 128), f32)),
        prev, group_sums, whole_sums, *in_own, *in_sent, *out_own, *out_sent,
    )
    norms = ffn_total(cube_total(norms))
    update_in, update_out = call(
        functools.partial(final_kernel, bounds), 18,
        (shape(local_in.shape, bf16), shape(local_out.shape, bf16)),
        prev, factors, whole_sums, norms, *in_own, *out_own, *got_in, *got_out,
    )
    return (update_in[None], update_out[None])


def solution(mesh):
    return jax.shard_map(
        shards,
        mesh=mesh,
        in_specs=(
            P("expert", None),
            P("expert", None),
            P("expert", None),
            P("expert", None, "ffn"),
            P("expert", "ffn", None),
            P(),
            P(None, None, "ffn"),
        ),
        out_specs=(P("expert", None, "ffn"), P("expert", "ffn", None)),
        check_vma=False,
    )
```

```python
import functools
import math

import jax
import jax.numpy as jnp
from jax import lax
from jax.experimental import pallas as pl
from jax.experimental.pallas import tpu as pltpu
from jax.sharding import PartitionSpec as P

D = 4096
FF = 5120
GROUP = 8


DECAY_RATE = 0.9
EPS_ONE = 1e-30
ROOT_COEF = math.sqrt(2.0 / math.pi)
CUBIC_COEF = 0.044715

MASKS = (1, 2, 4)

MIB = 1024 * 1024
CUT_MIB = 14


def swap(value, mask, axis="expert"):
    pairs = [(source, source ^ mask) for source in range(lax.axis_size(axis))]
    return lax.ppermute(value, axis, pairs)


def gelu_pair(inputs):
    inner = ROOT_COEF * (inputs + CUBIC_COEF * inputs * inputs * inputs)
    tangent = jnp.tanh(inner)
    act_value = 0.5 * inputs * (1.0 + tangent)
    act_slope = 0.5 * (1.0 + tangent) + 0.5 * inputs * (1.0 - tangent * tangent) * ROOT_COEF * (
        1.0 + 3.0 * CUBIC_COEF * inputs * inputs
    )
    return (act_value, act_slope)


def ffn_total(values):
    mask = 1
    while mask < lax.axis_size("ffn"):
        values = values + swap(values, mask, "ffn")
        mask *= 2
    return values


def set_bounds(hidden):
    unit = next(unit for unit in (256, 128, 2) if hidden % unit == 0 and hidden // unit >= 3)
    units = hidden // unit
    bounds, low = [], 0
    for k in range(3):
        high = low + (units // 3 + (k < units % 3)) * unit
        bounds.append((low, high))
        low = high
    return bounds


def dot(left, right, left_dim, right_dim):
    return lax.dot_general(
        left, right, (((left_dim,), (right_dim,)), ((), ())), preferred_element_type=jnp.float32
    )


def call(kernel, mib, out_shape, *operands, scratch=(), whole=False):
    space = pl.ANY if whole else pltpu.VMEM
    return pl.pallas_call(
        kernel,
        out_shape=out_shape,
        in_specs=[pl.BlockSpec(memory_space=space)] * len(operands),
        out_specs=jax.tree.map(lambda _: pl.BlockSpec(memory_space=pltpu.VMEM), out_shape),
        scratch_shapes=list(scratch),
        compiler_params=pltpu.CompilerParams(vmem_limit_bytes=mib * MIB),
    )(*operands)


def place_in_group():
    return lax.rem(lax.axis_index("expert"), GROUP)


def bit(place, k):
    return lax.rem(lax.div(place, 1 << k), 2)


def flipped(place, mask):
    for k in range(3):
        if mask >> k & 1:
            place = place + (1 - 2 * bit(place, k)) * (1 << k)
    return place


def partial_sum(rows, own_weight, got_weight, by_row):
    width = rows.shape[1] // 2
    contract = 1 if by_row else 0
    return dot(rows[:, :width], own_weight, 1, contract) + dot(rows[:, width:], got_weight, 1, contract)


def cut_kernel(bounds, weight_in, weight_out, *refs):
    kept_in, kept_out, packed, sems = refs[:3], refs[3:6], refs[6:9], refs[9]
    copies = []
    width = weight_in.shape[0]
    for k in range(3):
        low, half = bounds[k][0], (bounds[k][1] - bounds[k][0]) // 2
        side = bit(place_in_group(), k)
        kept = pl.ds(pl.multiple_of(low + side * half, 128), half)
        copies.append((weight_in.at[:, kept], kept_in[k], 3 * k))
        copies.append((weight_out.at[kept, :], kept_out[k], 3 * k + 1))
        start = low + (1 - side) * half
        at = 0
        for n in range(half // 128):
            part = pl.ds(pl.multiple_of(start + n * 128, 128), 128)
            copies.append((weight_in.at[:, part], packed[k].at[at : at + width], 3 * k + 2))
            at += width
        for n in range(width // 128):
            part = pl.ds(pl.multiple_of(start, 128), half)
            source = weight_out.at[part, n * 128 : n * 128 + 128]
            copies.append((source, packed[k].at[at : at + half], 3 * k + 2))
            at += half
    copies = [pltpu.make_async_copy(source, target, sems.at[n]) for n, (source, target, _) in enumerate(copies)]
    for copy in copies:
        copy.start()
    for copy in copies:
        copy.wait()


def got_weight(ref, by_row, half, width):
    at = half // 128 * width if by_row else 0
    rows = half if by_row else width
    blocks = (width if by_row else half) // 128
    return jnp.concatenate([ref[at + n * rows : at + (n + 1) * rows, :] for n in range(blocks)], axis=1)


def sums_kernel(side, by_row, is_packed, *refs):
    own, own_other, pairs, pairs_other = refs[:4]
    own_weights, got_weights, rows_out, sums_out = refs[4:7], refs[7:10], refs[10:13], refs[13:16]
    count, width = own.shape[1], own.shape[2]
    for k in range(3):
        first, second = 1 << (k + 1) % 3, 1 << (k + 2) % 3
        for j in range(2):
            for l in range(2):
                chunk = flipped(place_in_group(), side * first + j * second + l * (1 << k))
                at = (j * 2 + l) * 2 * count
                rows_out[k][at : at + count, :width] = own[chunk]
                rows_out[k][at : at + count, width:] = pairs[k, chunk]
                rows_out[k][at + count : at + 2 * count, :width] = own_other[chunk]
                rows_out[k][at + count : at + 2 * count, width:] = pairs_other[k, chunk]
        half = sums_out[k].shape[1]
        got = got_weight(got_weights[k], by_row, half, width) if is_packed else got_weights[k][...]
        sums = partial_sum(rows_out[k][...], own_weights[k][...], got, by_row)
        sums_out[k][...] = sums.astype(sums_out[k].dtype)


def add_kernel(*refs):
    kept, received, total_out, sent_out = refs[:3], refs[3:6], refs[6:9], refs[9:12]
    for k in range(3):
        middle = kept[k].shape[0] // 2
        total_out[k][...] = kept[k][:middle] + received[k][:middle].astype(jnp.float32)
        total = kept[k][middle:] + received[k][middle:].astype(jnp.float32)
        sent_out[k][...] = total.astype(jnp.bfloat16)


def hidden_kernel(*refs):
    kept, received, hidden_out, slope_out = refs[:3], refs[3:6], refs[6:9], refs[9:12]
    for k in range(3):
        act_value, act_slope = gelu_pair(kept[k][...] + received[k][...].astype(jnp.float32))
        hidden_out[k][...] = act_value.astype(jnp.bfloat16)
        slope_out[k][...] = act_slope


def pre_grad_kernel(*refs):
    kept, received, slope, pre_grad_out = refs[:3], refs[3:6], refs[6:9], refs[9:12]
    for k in range(3):
        value = (kept[k][...] + received[k][...].astype(jnp.float32)) * slope[k][...]
        pre_grad_out[k][...] = value.astype(jnp.bfloat16)


def join_kernel(*refs):
    for k in range(3):
        own, got, joined = refs[k], refs[3 + k], refs[6 + k]
        joined[: own.shape[0]] = own[...]
        joined[own.shape[0] :] = got[...]


def gradients(hidden_first, near_rows, far_rows, values, own_out, sent_out, sums_out):
    width = near_rows[0].shape[1] // 2
    for k in range(3):
        near, far = values[2 * k][...], values[2 * k + 1][...]
        if hidden_first:
            grad = dot(near, near_rows[k][...], 0, 0) + dot(far, far_rows[k][...], 0, 0)
            own_out[k][...] = grad[:, :width]
            sent_out[k][...] = grad[:, width:].astype(jnp.bfloat16)
        else:
            grad = dot(near_rows[k][...], near, 0, 0) + dot(far_rows[k][...], far, 0, 0)
            own_out[k][...] = grad[:width]
            sent_out[k][...] = grad[width:].astype(jnp.bfloat16)
        square = grad * grad + EPS_ONE
        down = jnp.sum(square, axis=0, keepdims=True)
        across = dot(jnp.ones((8, square.shape[1]), jnp.float32), square, 1, 1)
        down = jnp.broadcast_to(down, (8, square.shape[1]))
        by_width, by_hidden = (down, across) if hidden_first else (across, down)
        sums_out[k] = by_width
        sums_out[3 + k] = jnp.zeros(sums_out.shape[1:], jnp.float32)
        sums_out[3 + k, :, : by_hidden.shape[1]] = by_hidden


def grad_out_kernel(*refs):
    gradients(True, refs[:3], refs[3:6], refs[6:12], refs[12:15], refs[15:18], refs[18])


def grad_in_kernel(*refs):
    other_sums, hidden_prev, stats_out, sums = refs[12], refs[13], refs[20], refs[21]
    gradients(False, refs[:3], refs[3:6], refs[6:12], refs[14:17], refs[17:20], sums)
    collect(hidden_prev, (sums, other_sums), stats_out)


IN_WIDTH, OUT_WIDTH, IN_HIDDEN, OUT_HIDDEN, TOTALS, STAT_ROWS = 0, 8, 16, 22, 28, 32


def collect(hidden_prev, all_sums, stats_out):
    place = place_in_group()
    stats_out[...] = jnp.zeros_like(stats_out)
    lanes = stats_out.shape[1]
    for which in range(2):
        sums = all_sums[which]
        width_row, hidden_row = (IN_WIDTH, OUT_WIDTH)[which], (IN_HIDDEN, OUT_HIDDEN)[which]
        width = sums.shape[2] // 2
        stats_out[pl.ds(width_row + place, 1), :] = sum(sums[k, 0:1, :width] for k in range(3))
        total = 0.0
        for k in range(3):
            stats_out[pl.ds(width_row + flipped(place, 1 << k), 1), :] = sums[k, 0:1, width:]
            row = sums[3 + k, 0:1, :lanes]
            stats_out[pl.ds(hidden_row + 2 * k + bit(place, k), 1), :] = row
            total = total + jnp.sum(row, axis=1, keepdims=True)
        stats_out[TOTALS + which : TOTALS + which + 1, :] = jnp.broadcast_to(total, (1, lanes))
    previous = jnp.sum(hidden_prev[...], axis=1, keepdims=True)
    stats_out[TOTALS + 2 : TOTALS + 3, :] = jnp.broadcast_to(previous, (1, lanes))


def stat_row(stats_ref, index):
    return stats_ref[pl.ds(index, 1), :]


def upright(row):
    return jnp.transpose(jnp.broadcast_to(row, (8, row.shape[1])))[:, 0:1]


def norm_kernel(prev, group_sums, whole_sums, *refs):
    own_in, sent_in, own_out, sent_out = refs[:3], refs[3:6], refs[6:9], refs[9:12]
    factors_out, norms_out = refs[12], refs[13]
    place = place_in_group()
    width = own_in[0].shape[0]
    row = lax.broadcasted_iota(jnp.int32, prev.shape, 0)
    by_width = row < IN_HIDDEN
    mean = jnp.where(by_width, whole_sums[...] / FF, group_sums[...] / D)
    factors_out[...] = DECAY_RATE * prev[...] + (1.0 - DECAY_RATE) * mean
    norm_in, norm_out = 0.0, 0.0
    for k in range(3):
        half = own_in[k].shape[1]
        partner = flipped(place, 1 << k)
        own_row = stat_row(factors_out, IN_WIDTH + place)[:, :width]
        pair_row = stat_row(factors_out, IN_WIDTH + partner)[:, :width]
        hidden_row = stat_row(factors_out, IN_HIDDEN + 2 * k + bit(place, k))[:, :half]
        sent = sent_in[k][...].astype(jnp.float32)
        down = jnp.sum(own_in[k][...] * own_in[k][...] * upright(1.0 / own_row), axis=0, keepdims=True)
        down = down + jnp.sum(sent * sent * upright(1.0 / pair_row), axis=0, keepdims=True)
        norm_in = norm_in + jnp.sum(down / hidden_row, axis=1, keepdims=True)
        own_row = stat_row(factors_out, OUT_WIDTH + place)[:, :width]
        pair_row = stat_row(factors_out, OUT_WIDTH + partner)[:, :width]
        hidden_row = stat_row(factors_out, OUT_HIDDEN + 2 * k + bit(place, k))[:, :half]
        inverse = upright(1.0 / hidden_row)
        sent = sent_out[k][...].astype(jnp.float32)
        down = jnp.sum(own_out[k][...] * own_out[k][...] * inverse, axis=0, keepdims=True) / own_row
        down = down + jnp.sum(sent * sent * inverse, axis=0, keepdims=True) / pair_row
        norm_out = norm_out + jnp.sum(down, axis=1, keepdims=True)
    row = lax.broadcasted_iota(jnp.int32, norms_out.shape, 0)
    norms_out[...] = jnp.where(row == 0, norm_in, norm_out)


def final_kernel(bounds, prev, factors, whole_sums, norms, *refs):
    own_in, own_out, got_in, got_out = refs[:3], refs[3:6], refs[6:9], refs[9:12]
    update_in, update_out = refs[12:]
    place = place_in_group()
    width = update_in.shape[0]
    count = float(D) * float(FF)
    mean_in = DECAY_RATE * jnp.mean(prev[IN_WIDTH : IN_WIDTH + 8, :width], keepdims=True)
    mean_in = mean_in + (1.0 - DECAY_RATE) * whole_sums[TOTALS : TOTALS + 1, 0:1] / count
    mean_out = DECAY_RATE * whole_sums[TOTALS + 2 : TOTALS + 3, 0:1] / (FF * GROUP)
    mean_out = mean_out + (1.0 - DECAY_RATE) * whole_sums[TOTALS + 1 : TOTALS + 2, 0:1] / count
    factor_in = jnp.sqrt(mean_in) / jnp.maximum(1.0, jnp.sqrt(mean_in * norms[0:1, 0:1] / count))
    factor_out = jnp.sqrt(mean_out) / jnp.maximum(1.0, jnp.sqrt(mean_out * norms[1:2, 0:1] / count))
    width_in = upright(lax.rsqrt(stat_row(factors, IN_WIDTH + place)[:, :width]) * factor_in)
    width_out = lax.rsqrt(stat_row(factors, OUT_WIDTH + place)[:, :width]) * factor_out
    for k in range(3):
        low, half = bounds[k][0], (bounds[k][1] - bounds[k][0]) // 2
        own_bit = bit(place, k)
        if half % 128:
            width_scaled = (own_in[k][...] * width_in, got_in[k][...].astype(jnp.float32) * width_in)
            for side in range(2):
                hidden_in = lax.rsqrt(factors[IN_HIDDEN + 2 * k + side : IN_HIDDEN + 2 * k + side + 1, :half])
                value = jnp.where(own_bit == side, *width_scaled) * hidden_in
                update_in[:, low + side * half : low + side * half + half] = value.astype(update_in.dtype)
        for own in (True, False):
            side = own_bit if own else 1 - own_bit
            start = pl.multiple_of(low + side * half, math.gcd(low, half))
            hidden_out = upright(lax.rsqrt(stat_row(factors, OUT_HIDDEN + 2 * k + side)[:, :half]))
            if half % 128 == 0:
                hidden_in = lax.rsqrt(stat_row(factors, IN_HIDDEN + 2 * k + side)[:, :half])
                value = own_in[k][...] if own else got_in[k][...].astype(jnp.float32)
                update_in[:, pl.ds(start, half)] = (value * width_in * hidden_in).astype(update_in.dtype)
            value = own_out[k][...] if own else got_out[k][...].astype(jnp.float32)
            update_out[pl.ds(start, half), :] = (value * hidden_out * width_out).astype(update_out.dtype)


def shards(tokens, cotangent, expert_ids, in_weight, out_weight, width_states, hidden_states):
    bf16, f32 = jnp.bfloat16, jnp.float32
    shape = jax.ShapeDtypeStruct
    experts = width_states.shape[1]
    tok_rows, width = tokens.shape
    capacity = 5 * tok_rows // (4 * experts)
    part_cap = capacity // 2
    places = lax.axis_size("expert")
    block_width = width // GROUP
    position = lax.axis_index("expert")
    expert = position // GROUP
    part = lax.axis_index("ffn") % 2
    bits = [position >> k & 1 for k in range(3)]
    bounds = set_bounds(in_weight.shape[2])
    halves = [(high - low) // 2 for low, high in bounds]
    sets = range(3)
    firsts = [MASKS[(k + 1) % 3] for k in sets]
    seconds = [MASKS[(k + 2) % 3] for k in sets]
    local_in = in_weight[0]
    local_out = out_weight[0]

    is_packed = all(half % 128 == 0 for half in halves) and block_width % 128 == 0
    if is_packed:
        kept_shapes = [shape((block_width, half), bf16) for half in halves]
        kept_shapes += [shape((half, block_width), bf16) for half in halves]
        packed_shapes = [shape((2 * half * block_width // 128, 128), bf16) for half in halves]
        copies = 6 + sum(half + block_width for half in halves) // 128
        cuts = call(
            functools.partial(cut_kernel, bounds), CUT_MIB, kept_shapes + packed_shapes, local_in, local_out,
            scratch=[pltpu.SemaphoreType.DMA((copies,))], whole=True,
        )
        own_weights = cuts[:3], cuts[3:6]
        got_weights = [swap(cuts[6 + k], MASKS[k]) for k in sets]
        got_weights = (got_weights, got_weights)
    else:
        cuts = []
        for taken in range(2):
            at = [bounds[k][0] + (1 - bits[k] if taken else bits[k]) * halves[k] for k in sets]
            cuts += [lax.dynamic_slice_in_dim(local_in, at[k], halves[k], 1) for k in sets]
            cuts += [lax.dynamic_slice_in_dim(local_out, at[k], halves[k], 0) for k in sets]
        own_weights = cuts[:3], cuts[3:6]
        got_weights = tuple([swap(cuts[n + k], MASKS[k]) for k in sets] for n in (6, 9))

    route_ids = expert_ids[:, 0]
    onehot = (route_ids[:, None] == jnp.arange(experts, dtype=jnp.int32)[None, :]).astype(jnp.int32)
    before = jnp.cumsum(onehot, axis=0) - onehot
    slot_index = jnp.sum(before * onehot, axis=1) - part * part_cap
    valid = (slot_index >= 0) & (slot_index < part_cap)
    target = jnp.where(valid, route_ids * part_cap + slot_index, -1)
    select = (jnp.arange(experts * part_cap, dtype=jnp.int32)[:, None] == target[None, :]).astype(bf16)

    def route(values):
        routed = dot(select, values, 1, 0).astype(bf16)
        routed = routed.reshape(experts, part_cap, GROUP, block_width).transpose(0, 2, 1, 3)
        return routed.reshape(places, part_cap, block_width)

    routed = jnp.concatenate([route(tokens), route(cotangent)], axis=2)
    got = lax.all_to_all(routed, "expert", split_axis=0, concat_axis=0, tiled=True)
    got, got_weights = lax.optimization_barrier((got, got_weights))
    got = got.reshape(places // GROUP, GROUP, part_cap, 2 * block_width).transpose(1, 0, 2, 3)
    got = got.reshape(GROUP, -1, 2 * block_width)

    def both_cores(own, pairs):
        pairs = jnp.stack(pairs)
        return own, swap(own, 1, "ffn"), pairs, swap(pairs, 1, "ffn")

    got_tokens, got_cotangent = got[:, :, :block_width], got[:, :, block_width:]
    token_pairs = [swap(got_tokens, MASKS[k]) for k in sets]
    cotangent_pairs = [swap(got_cotangent, MASKS[k]) for k in sets]

    def shapes(rows, dtype):
        return [shape((rows, half), dtype) for half in halves]

    count = got.shape[1] * 8
    wide = 2 * block_width

    def far_sums(blocks, which):
        kernel = functools.partial(sums_kernel, 1, which == 1, is_packed)
        operands = (*blocks, *own_weights[which], *got_weights[which])
        outs = call(kernel, 14, [shape((count, wide), bf16)] * 3 + shapes(count, bf16), *operands)
        return operands, outs[:3], outs[3:]

    def scatter_sum(operands, far_rows, sent, which):
        received = [swap(sent[k], firsts[k]) for k in sets]
        kernel = functools.partial(sums_kernel, 0, which == 1, is_packed)
        outs = call(kernel, 14, [shape((count, wide), bf16)] * 3 + shapes(count, f32), *operands)
        near_rows, kept = outs[:3], outs[3:]
        outs = call(add_kernel, 8, shapes(count // 2, f32) + shapes(count // 2, bf16), *kept, *received)
        return near_rows + far_rows, outs[:3], [swap(outs[3 + k], seconds[k]) for k in sets]

    def gather(near):
        values = []
        for k in sets:
            values += [near[k], swap(near[k], firsts[k])]
        return values

    def join(owns, got):
        return call(join_kernel, 8, shapes(count, bf16), *owns, *got)

    token_operands, far_tokens, token_sums = far_sums(both_cores(got_tokens, token_pairs), 0)
    far_tokens, cotangent_pairs = lax.optimization_barrier((far_tokens, cotangent_pairs))
    cotangent_operands, far_cotangent, cotangent_sums = far_sums(both_cores(got_cotangent, cotangent_pairs), 1)
    token_rows, *pre = scatter_sum(token_operands, far_tokens, token_sums, 0)
    cotangent_rows, *back = scatter_sum(cotangent_operands, far_cotangent, cotangent_sums, 1)
    outs = call(hidden_kernel, 8, shapes(count // 2, bf16) + shapes(count // 2, f32), *pre[0], *pre[1])
    hidden, slope = outs[:3], outs[3:]
    hidden_got = [swap(hidden[k], seconds[k]) for k in sets]
    pre_grad = call(pre_grad_kernel, 8, shapes(count // 2, bf16), *back[0], *back[1], *slope)
    pre_grad_got = [swap(pre_grad[k], seconds[k]) for k in sets]
    hidden = gather(join(hidden, hidden_got))
    pre_grad_near = join(pre_grad, pre_grad_got)
    pre_grad = gather(pre_grad_near)

    hidden, pre_grad[0::2] = lax.optimization_barrier((hidden, pre_grad[0::2]))
    lanes = max(block_width, *halves)
    hidden_pick = lax.dynamic_index_in_dim(hidden_states, expert, 1, keepdims=False)
    sums_shape = (6, 8, wide)
    outs = call(
        grad_out_kernel, 14,
        [shape((half, block_width), f32) for half in halves]
        + [shape((half, block_width), bf16) for half in halves]
        + [shape(sums_shape, f32)],
        *cotangent_rows, *hidden,
    )
    out_own, out_sent, out_sums = outs[:3], outs[3:6], outs[6]
    got_out = [swap(out_sent[k], MASKS[k]) for k in sets]
    pre_grad, got_out = lax.optimization_barrier((pre_grad, got_out))
    outs = call(
        grad_in_kernel, 14,
        [shape((block_width, half), f32) for half in halves]
        + [shape((block_width, half), bf16) for half in halves]
        + [shape((STAT_ROWS, lanes), f32)],
        *token_rows, *pre_grad, out_sums, hidden_pick[1:2],
        scratch=[pltpu.VMEM(sums_shape, f32)],
    )
    in_own, in_sent, stats = outs[:3], outs[3:6], outs[6]
    got_in = [swap(in_sent[k], MASKS[k]) for k in sets]

    width_pick = lax.dynamic_index_in_dim(width_states, expert, 1, keepdims=False)

    def padded(values):
        return jnp.pad(values, ((0, 0), (0, lanes - values.shape[1])), constant_values=1.0)

    prev = [padded(width_pick.reshape(2 * GROUP, block_width))]
    for which in range(2):
        for k in sets:
            low, high = bounds[k]
            prev.append(padded(hidden_pick[which, low:high].reshape(2, halves[k])))
    prev.append(jnp.ones((STAT_ROWS - TOTALS, lanes), f32))
    prev = jnp.concatenate(prev)

    def cube_total(values):
        values = values + swap(values, 1) + swap(values, 2) + swap(values, 3)
        return values + swap(values, 4)

    group_sums = cube_total(stats)
    whole_sums = ffn_total(group_sums)
    whole_sums, got_in = lax.optimization_barrier((whole_sums, got_in))
    factors, norms = call(
        norm_kernel, 12,
        (shape((STAT_ROWS, lanes), f32), shape((8, 128), f32)),
        prev, group_sums, whole_sums, *in_own, *in_sent, *out_own, *out_sent,
    )
    norms = ffn_total(cube_total(norms))
    update_in, update_out = call(
        functools.partial(final_kernel, bounds), 12,
        (shape(local_in.shape, bf16), shape(local_out.shape, bf16)),
        prev, factors, whole_sums, norms, *in_own, *out_own, *got_in, *got_out,
    )
    return (update_in[None], update_out[None])


def solution(mesh):
    return jax.shard_map(
        shards,
        mesh=mesh,
        in_specs=(
            P("expert", None),
            P("expert", None),
            P("expert", None),
            P("expert", None, "ffn"),
            P("expert", "ffn", None),
            P(),
            P(None, None, "ffn"),
        ),
        out_specs=(P("expert", None, "ffn"), P("expert", "ffn", None)),
        check_vma=False,
    )
```

```python
import functools
import math

import jax
import jax.numpy as jnp
from jax import lax
from jax.experimental import pallas as pl
from jax.experimental.pallas import tpu as pltpu
from jax.sharding import PartitionSpec as P

D = 4096
FF = 5120
GROUP = 8


DECAY_RATE = 0.9
EPS_ONE = 1e-30
ROOT_COEF = math.sqrt(2.0 / math.pi)
CUBIC_COEF = 0.044715

MASKS = (1, 2, 4)

MIB = 1024 * 1024
CUT_MIB = 14


def swap(value, mask, axis="expert"):
    pairs = [(source, source ^ mask) for source in range(lax.axis_size(axis))]
    return lax.ppermute(value, axis, pairs)


def gelu_pair(inputs):
    inner = ROOT_COEF * (inputs + CUBIC_COEF * inputs * inputs * inputs)
    tangent = jnp.tanh(inner)
    act_value = 0.5 * inputs * (1.0 + tangent)
    act_slope = 0.5 * (1.0 + tangent) + 0.5 * inputs * (1.0 - tangent * tangent) * ROOT_COEF * (
        1.0 + 3.0 * CUBIC_COEF * inputs * inputs
    )
    return (act_value, act_slope)


def ffn_total(values):
    mask = 1
    while mask < lax.axis_size("ffn"):
        values = values + swap(values, mask, "ffn")
        mask *= 2
    return values


def set_bounds(hidden):
    unit = next(unit for unit in (256, 128, 2) if hidden % unit == 0 and hidden // unit >= 3)
    units = hidden // unit
    bounds, low = [], 0
    for k in range(3):
        high = low + (units // 3 + (k < units % 3)) * unit
        bounds.append((low, high))
        low = high
    return bounds


def dot(left, right, left_dim, right_dim):
    return lax.dot_general(
        left, right, (((left_dim,), (right_dim,)), ((), ())), preferred_element_type=jnp.float32
    )


def call(kernel, mib, out_shape, *operands, scratch=(), streamed=(), streamed_out=(), whole=()):
    def spec(value, n, blocks, refs):
        if n in refs:
            return pl.BlockSpec(memory_space=pl.ANY)
        if n in blocks:
            return pl.BlockSpec(value.shape, lambda: (0,) * len(value.shape))
        return pl.BlockSpec(memory_space=pltpu.VMEM)

    return pl.pallas_call(
        kernel,
        out_shape=out_shape,
        in_specs=[spec(value, n, streamed, whole) for n, value in enumerate(operands)],
        out_specs=[spec(value, n, streamed_out, ()) for n, value in enumerate(out_shape)],
        scratch_shapes=list(scratch),
        compiler_params=pltpu.CompilerParams(vmem_limit_bytes=mib * MIB),
    )(*operands)


def padded_width(half):
    return -(-half // 128) * 128


def packed_place(step, matrix, k, halves):
    axis = (k + 1 + (step + matrix) % 2) % 3
    return axis, padded_width(halves[(axis + 2 - step) % 3]) if matrix else 0


def packed_widths(step, halves):
    return [padded_width(halves[(axis + 2 - step) % 3]) + halves[(axis + 1 + step) % 3] for axis in range(3)]


def place_in_group():
    return lax.rem(lax.axis_index("expert"), GROUP)


def bit(place, k):
    return lax.rem(lax.div(place, 1 << k), 2)


def flipped(place, mask):
    for k in range(3):
        if mask >> k & 1:
            place = place + (1 - 2 * bit(place, k)) * (1 << k)
    return place


def partial_sum(rows, own_weight, got_weight, by_row):
    width = rows.shape[1] // 2
    contract = 1 if by_row else 0
    return dot(rows[:, :width], own_weight, 1, contract) + dot(rows[:, width:], got_weight, 1, contract)


def cut_kernel(bounds, weight_in, weight_out, *refs):
    kept_in, kept_out, packed, sems = refs[:3], refs[3:6], refs[6:9], refs[9]
    copies = []
    width = weight_in.shape[0]
    for k in range(3):
        low, half = bounds[k][0], (bounds[k][1] - bounds[k][0]) // 2
        side = bit(place_in_group(), k)
        kept = pl.ds(pl.multiple_of(low + side * half, 128), half)
        copies.append((weight_in.at[:, kept], kept_in[k], 3 * k))
        copies.append((weight_out.at[kept, :], kept_out[k], 3 * k + 1))
        start = low + (1 - side) * half
        at = 0
        for n in range(half // 128):
            part = pl.ds(pl.multiple_of(start + n * 128, 128), 128)
            copies.append((weight_in.at[:, part], packed[k].at[at : at + width], 3 * k + 2))
            at += width
        for n in range(width // 128):
            part = pl.ds(pl.multiple_of(start, 128), half)
            source = weight_out.at[part, n * 128 : n * 128 + 128]
            copies.append((source, packed[k].at[at : at + half], 3 * k + 2))
            at += half
    copies = [pltpu.make_async_copy(source, target, sems.at[n]) for n, (source, target, _) in enumerate(copies)]
    for copy in copies:
        copy.start()
    for copy in copies:
        copy.wait()


def got_weight(ref, by_row, half, width):
    at = half // 128 * width if by_row else 0
    rows = half if by_row else width
    blocks = (width if by_row else half) // 128
    return jnp.concatenate([ref[at + n * rows : at + (n + 1) * rows, :] for n in range(blocks)], axis=1)


def sums_kernel(side, halves, is_packed, *refs):
    own, pairs, own_weights, got_weights = refs[0], refs[1], refs[2:8], refs[8:14]
    rows_out, sums_out = refs[14:20], refs[20:]
    count, width = own.shape[1], own.shape[2] // 2
    for matrix in range(2):
        lanes = slice(matrix * width, (matrix + 1) * width)
        for k in range(3):
            n, half = 3 * matrix + k, halves[k]
            axis = packed_place(0, matrix, k, halves)[0]
            first, second = 1 << axis, 1 << (3 - axis - k)
            for j in range(2):
                for l in range(2):
                    chunk = flipped(place_in_group(), side * first + j * second + l * (1 << k))
                    at = (j * 2 + l) * count
                    rows_out[n][at : at + count, :width] = own[chunk, :, lanes]
                    rows_out[n][at : at + count, width:] = pairs[k, chunk, :, lanes]
            by_row = matrix == 1
            got = got_weight(got_weights[n], by_row, half, width) if is_packed else got_weights[n][...]
            sums = partial_sum(rows_out[n][...], own_weights[n][...], got, by_row)
            if side:
                at = packed_place(0, matrix, k, halves)[1]
                sums_out[axis][:, at : at + half] = sums.astype(jnp.bfloat16)
            else:
                sums_out[n][...] = sums


def add_kernel(halves, *refs):
    kept, received, total_out, sent_out = refs[:6], refs[6:9], refs[9:15], refs[15:18]
    for matrix in range(2):
        for k in range(3):
            n, half = 3 * matrix + k, halves[k]
            middle = kept[n].shape[0] // 2
            axis, at = packed_place(0, matrix, k, halves)
            total = kept[n][...] + received[axis][:, at : at + half].astype(jnp.float32)
            total_out[n][...] = total[:middle]
            axis, at = packed_place(1, matrix, k, halves)
            sent_out[axis][:, at : at + half] = total[middle:].astype(jnp.bfloat16)


def act_kernel(halves, *refs):
    kept, received, outs = refs[:6], refs[6:9], refs[9:12]
    for k in range(3):
        values = []
        for matrix in range(2):
            axis, at = packed_place(1, matrix, k, halves)
            values.append(kept[3 * matrix + k][...] + received[axis][:, at : at + halves[k]].astype(jnp.float32))
        act_value, act_slope = gelu_pair(values[0])
        for matrix, value in enumerate((act_value, values[1] * act_slope)):
            axis, at = packed_place(0, matrix, k, halves)
            outs[axis][:, at : at + halves[k]] = value.astype(jnp.bfloat16)


def join_kernel(halves, *refs):
    own, got, outs = refs[:3], refs[3:6], refs[6:9]
    for matrix in range(2):
        for k in range(3):
            source, start = packed_place(0, matrix, k, halves)
            axis, at = packed_place(1, matrix, k, halves)
            rows = own[source].shape[0]
            outs[axis][:rows, at : at + halves[k]] = own[source][:, start : start + halves[k]]
            outs[axis][rows:, at : at + halves[k]] = got[source][:, start : start + halves[k]]


def gradients(hidden_first, halves, rows, values, row_buffers, value_buffers, sems, own_out, sent_out, sums_out):
    matrix = 0 if hidden_first else 1
    part = row_buffers.shape[1] // 4
    width = row_buffers.shape[2] // 2

    def copies(n, parts, buffer):
        return [
            pltpu.make_async_copy(parts[i], buffer.at[pl.ds(i * part, part)], sems.at[n * 4 + i]) for i in range(4)
        ]

    value_copies, row_copies = {}, {}
    for k in range(3):
        axis = packed_place(1, matrix, k, halves)[0]
        row_copies[k] = copies(k, rows[4 * k : 4 * k + 4], row_buffers.at[k])
        value_copies[k] = copies(3 + axis, values[4 * axis : 4 * axis + 4], value_buffers[axis])
        for copy in row_copies[k] + value_copies[k]:
            copy.start()
    for k in range(3):
        for copy in row_copies[k] + value_copies[k]:
            copy.wait()
        axis, at = packed_place(1, matrix, k, halves)
        value = value_buffers[axis][:, at : at + halves[k]]
        if hidden_first:
            grad = dot(value, row_buffers[k], 0, 0)
            own_out[k][...] = grad[:, :width]
            sent_out[k][...] = grad[:, width:].astype(jnp.bfloat16)
        else:
            grad = dot(row_buffers[k], value, 0, 0)
            own_out[k][...] = grad[:width]
            sent_out[k][...] = grad[width:].astype(jnp.bfloat16)
        square = grad * grad + EPS_ONE
        down = jnp.sum(square, axis=0, keepdims=True)
        down = jnp.broadcast_to(down, (8, square.shape[1]))
        if square.shape[1] % 128 == 0:
            square = sum(square[:, n : n + 128] for n in range(0, square.shape[1], 128))
        across = dot(jnp.ones((8, square.shape[1]), jnp.float32), square, 1, 1)
        by_width, by_hidden = (down, across) if hidden_first else (across, down)
        sums_out[k] = by_width
        sums_out[3 + k] = jnp.zeros(sums_out.shape[1:], jnp.float32)
        sums_out[3 + k, :, : by_hidden.shape[1]] = by_hidden


def grad_out_kernel(halves, *refs):
    rows, values, outs, buffers = refs[:12], refs[12:24], refs[24:31], refs[31:]
    gradients(True, halves, rows, values, buffers[0], buffers[1:4], buffers[4], outs[:3], outs[3:6], outs[6])


def grad_in_kernel(halves, *refs):
    rows, values, other_sums, hidden_prev, outs, buffers = (
        refs[:12], refs[12:24], refs[24], refs[25], refs[26:33], refs[33:]
    )
    sums = buffers[5]
    gradients(False, halves, rows, values, buffers[0], buffers[1:4], buffers[4], outs[:3], outs[3:6], sums)
    collect(hidden_prev, (sums, other_sums), outs[6])


IN_WIDTH, OUT_WIDTH, IN_HIDDEN, OUT_HIDDEN, TOTALS, STAT_ROWS = 0, 8, 16, 22, 28, 32


def collect(hidden_prev, all_sums, stats_out):
    place = place_in_group()
    stats_out[...] = jnp.zeros_like(stats_out)
    lanes = stats_out.shape[1]
    for which in range(2):
        sums = all_sums[which]
        width_row, hidden_row = (IN_WIDTH, OUT_WIDTH)[which], (IN_HIDDEN, OUT_HIDDEN)[which]
        width = sums.shape[2] // 2
        stats_out[pl.ds(width_row + place, 1), :] = sum(sums[k, 0:1, :width] for k in range(3))
        total = 0.0
        for k in range(3):
            stats_out[pl.ds(width_row + flipped(place, 1 << k), 1), :] = sums[k, 0:1, width:]
            row = sums[3 + k, 0:1, :lanes]
            stats_out[pl.ds(hidden_row + 2 * k + bit(place, k), 1), :] = row
            total = total + jnp.sum(row, axis=1, keepdims=True)
        stats_out[TOTALS + which : TOTALS + which + 1, :] = jnp.broadcast_to(total, (1, lanes))
    previous = jnp.sum(hidden_prev[...], axis=1, keepdims=True)
    stats_out[TOTALS + 2 : TOTALS + 3, :] = jnp.broadcast_to(previous, (1, lanes))


def stat_row(stats_ref, index):
    return stats_ref[pl.ds(index, 1), :]


def upright(row):
    return jnp.transpose(jnp.broadcast_to(row, (8, row.shape[1])))[:, 0:1]


def norm_kernel(prev, group_sums, whole_sums, *refs):
    own_in, sent_in, own_out, sent_out = refs[:3], refs[3:6], refs[6:9], refs[9:12]
    factors_out, norms_out = refs[12], refs[13]
    place = place_in_group()
    width = own_in[0].shape[0]
    row = lax.broadcasted_iota(jnp.int32, prev.shape, 0)
    by_width = row < IN_HIDDEN
    mean = jnp.where(by_width, whole_sums[...] / FF, group_sums[...] / D)
    factors_out[...] = DECAY_RATE * prev[...] + (1.0 - DECAY_RATE) * mean
    norm_in, norm_out = 0.0, 0.0
    for k in range(3):
        half = own_in[k].shape[1]
        partner = flipped(place, 1 << k)
        own_row = stat_row(factors_out, IN_WIDTH + place)[:, :width]
        pair_row = stat_row(factors_out, IN_WIDTH + partner)[:, :width]
        hidden_row = stat_row(factors_out, IN_HIDDEN + 2 * k + bit(place, k))[:, :half]
        sent = sent_in[k][...].astype(jnp.float32)
        down = jnp.sum(own_in[k][...] * own_in[k][...] * upright(1.0 / own_row), axis=0, keepdims=True)
        down = down + jnp.sum(sent * sent * upright(1.0 / pair_row), axis=0, keepdims=True)
        norm_in = norm_in + jnp.sum(down / hidden_row, axis=1, keepdims=True)
        own_row = stat_row(factors_out, OUT_WIDTH + place)[:, :width]
        pair_row = stat_row(factors_out, OUT_WIDTH + partner)[:, :width]
        hidden_row = stat_row(factors_out, OUT_HIDDEN + 2 * k + bit(place, k))[:, :half]
        inverse = upright(1.0 / hidden_row)
        sent = sent_out[k][...].astype(jnp.float32)
        down = jnp.sum(own_out[k][...] * own_out[k][...] * inverse, axis=0, keepdims=True) / own_row
        down = down + jnp.sum(sent * sent * inverse, axis=0, keepdims=True) / pair_row
        norm_out = norm_out + jnp.sum(down, axis=1, keepdims=True)
    row = lax.broadcasted_iota(jnp.int32, norms_out.shape, 0)
    norms_out[...] = jnp.where(row == 0, norm_in, norm_out)


def final_kernel(bounds, prev, factors, whole_sums, norms, *refs):
    own_in, own_out, got_in, got_out = refs[:3], refs[3:6], refs[6:9], refs[9:12]
    update_in, update_out = refs[12:]
    place = place_in_group()
    width = update_in.shape[0]
    count = float(D) * float(FF)
    mean_in = DECAY_RATE * jnp.mean(prev[IN_WIDTH : IN_WIDTH + 8, :width], keepdims=True)
    mean_in = mean_in + (1.0 - DECAY_RATE) * whole_sums[TOTALS : TOTALS + 1, 0:1] / count
    mean_out = DECAY_RATE * whole_sums[TOTALS + 2 : TOTALS + 3, 0:1] / (FF * GROUP)
    mean_out = mean_out + (1.0 - DECAY_RATE) * whole_sums[TOTALS + 1 : TOTALS + 2, 0:1] / count
    factor_in = jnp.sqrt(mean_in) / jnp.maximum(1.0, jnp.sqrt(mean_in * norms[0:1, 0:1] / count))
    factor_out = jnp.sqrt(mean_out) / jnp.maximum(1.0, jnp.sqrt(mean_out * norms[1:2, 0:1] / count))
    width_in = upright(lax.rsqrt(stat_row(factors, IN_WIDTH + place)[:, :width]) * factor_in)
    width_out = lax.rsqrt(stat_row(factors, OUT_WIDTH + place)[:, :width]) * factor_out
    for k in range(3):
        low, half = bounds[k][0], (bounds[k][1] - bounds[k][0]) // 2
        own_bit = bit(place, k)
        if half % 128:
            width_scaled = (own_in[k][...] * width_in, got_in[k][...].astype(jnp.float32) * width_in)
            for side in range(2):
                hidden_in = lax.rsqrt(factors[IN_HIDDEN + 2 * k + side : IN_HIDDEN + 2 * k + side + 1, :half])
                value = jnp.where(own_bit == side, *width_scaled) * hidden_in
                update_in[:, low + side * half : low + side * half + half] = value.astype(update_in.dtype)
        for own in (True, False):
            side = own_bit if own else 1 - own_bit
            start = pl.multiple_of(low + side * half, math.gcd(low, half))
            hidden_out = upright(lax.rsqrt(stat_row(factors, OUT_HIDDEN + 2 * k + side)[:, :half]))
            if half % 128 == 0:
                hidden_in = lax.rsqrt(stat_row(factors, IN_HIDDEN + 2 * k + side)[:, :half])
                value = own_in[k][...] if own else got_in[k][...].astype(jnp.float32)
                update_in[:, pl.ds(start, half)] = (value * width_in * hidden_in).astype(update_in.dtype)
            value = own_out[k][...] if own else got_out[k][...].astype(jnp.float32)
            update_out[pl.ds(start, half), :] = (value * hidden_out * width_out).astype(update_out.dtype)


def shards(tokens, cotangent, expert_ids, in_weight, out_weight, width_states, hidden_states):
    bf16, f32 = jnp.bfloat16, jnp.float32
    shape = jax.ShapeDtypeStruct
    experts = width_states.shape[1]
    tok_rows, width = tokens.shape
    capacity = 5 * tok_rows // (4 * experts)
    part_cap = capacity // 2
    places = lax.axis_size("expert")
    block_width = width // GROUP
    position = lax.axis_index("expert")
    expert = position // GROUP
    part = lax.axis_index("ffn") % 2
    bits = [position >> k & 1 for k in range(3)]
    bounds = set_bounds(in_weight.shape[2])
    halves = [(high - low) // 2 for low, high in bounds]
    sets = range(3)
    local_in = in_weight[0]
    local_out = out_weight[0]

    is_packed = all(half % 128 == 0 for half in halves) and block_width % 128 == 0
    if is_packed:
        kept_shapes = [shape((block_width, half), bf16) for half in halves]
        kept_shapes += [shape((half, block_width), bf16) for half in halves]
        packed_shapes = [shape((2 * half * block_width // 128, 128), bf16) for half in halves]
        copies = 6 + sum(half + block_width for half in halves) // 128
        cuts = call(
            functools.partial(cut_kernel, bounds), CUT_MIB, kept_shapes + packed_shapes, local_in, local_out,
            scratch=[pltpu.SemaphoreType.DMA((copies,))], whole=(0, 1),
        )
        got_weights = [swap(cuts[6 + k], MASKS[k]) for k in sets] * 2
    else:
        cuts = []
        for taken in range(2):
            at = [bounds[k][0] + (1 - bits[k] if taken else bits[k]) * halves[k] for k in sets]
            cuts += [lax.dynamic_slice_in_dim(local_in, at[k], halves[k], 1) for k in sets]
            cuts += [lax.dynamic_slice_in_dim(local_out, at[k], halves[k], 0) for k in sets]
        got_weights = [swap(cuts[6 + n], MASKS[n % 3]) for n in range(6)]

    route_ids = expert_ids[:, 0]
    onehot = (route_ids[:, None] == jnp.arange(experts, dtype=jnp.int32)[None, :]).astype(jnp.int32)
    before = jnp.cumsum(onehot, axis=0) - onehot
    slot_index = jnp.sum(before * onehot, axis=1) - part * part_cap
    valid = (slot_index >= 0) & (slot_index < part_cap)
    target = jnp.where(valid, route_ids * part_cap + slot_index, -1)
    select = (jnp.arange(experts * part_cap, dtype=jnp.int32)[:, None] == target[None, :]).astype(bf16)

    def route(values):
        routed = dot(select, values, 1, 0).astype(bf16)
        routed = routed.reshape(experts, part_cap, GROUP, block_width).transpose(0, 2, 1, 3)
        return routed.reshape(places, part_cap, block_width)

    routed = jnp.concatenate([route(tokens), route(cotangent)], axis=2)
    routed, own_weights = lax.optimization_barrier((routed, cuts[:6]))
    got = lax.all_to_all(routed, "expert", split_axis=0, concat_axis=0, tiled=True)
    got, got_weights = lax.optimization_barrier((got, got_weights))
    got = got.reshape(places // GROUP, GROUP, part_cap, 2 * block_width).transpose(1, 0, 2, 3)
    got = got.reshape(GROUP, -1, 2 * block_width)

    count = got.shape[1] * 4
    wide = 2 * block_width
    first_widths, second_widths = packed_widths(0, halves), packed_widths(1, halves)

    def shapes(rows, widths, dtype):
        return [shape((rows, width), dtype) for width in widths]

    def along_axes(values):
        return [swap(value, mask) for value, mask in zip(values, MASKS)]

    pairs = jnp.stack([swap(got, MASKS[k]) for k in sets])
    blocks = [(got, pairs), (swap(got, 1, "ffn"), swap(pairs, 1, "ffn"))]
    chains = range(2)
    row_shapes = [shape((count, wide), bf16)] * 6

    def sums(chain, side, out_shapes):
        kernel = functools.partial(sums_kernel, side, halves, is_packed)
        outs = call(
            kernel, 20, row_shapes + out_shapes, *blocks[chain], *own_weights, *got_weights,
            streamed_out=range(6),
        )
        return outs[:6], outs[6:]

    far_rows, received, near_rows, kept = [None] * 2, [None] * 2, [None] * 2, [None] * 2
    for c in chains:
        far_rows[c], sent = sums(c, 1, shapes(count, first_widths, bf16))
        received[c] = along_axes(sent)
    for c in chains:
        near_rows[c], kept[c] = sums(c, 0, shapes(count, halves * 2, f32))
    for c in chains:
        out_shapes = shapes(count // 2, halves * 2, f32) + shapes(count // 2, second_widths, bf16)
        outs = call(functools.partial(add_kernel, halves), 8, out_shapes, *kept[c], *received[c])
        kept[c], received[c] = outs[:6], along_axes(outs[6:])
    owns, nears, fars = [None] * 2, [None] * 2, [None] * 2
    for c in chains:
        out_shapes = shapes(count // 2, first_widths, bf16)
        owns[c] = call(functools.partial(act_kernel, halves), 8, out_shapes, *kept[c], *received[c])
        received[c] = along_axes(owns[c])
    for c in chains:
        out_shapes = shapes(count, second_widths, bf16)
        nears[c] = call(functools.partial(join_kernel, halves), 8, out_shapes, *owns[c], *received[c])
        fars[c] = along_axes(nears[c])

    def parts(near, far):
        return [value[n] for n in range(3) for chain in chains for value in (near[chain], far[chain])]

    token_rows = parts([rows[:3] for rows in near_rows], [rows[:3] for rows in far_rows])
    cotangent_rows = parts([rows[3:] for rows in near_rows], [rows[3:] for rows in far_rows])
    values = parts(nears, fars)
    buffers = [pltpu.VMEM((3, 4 * count, wide), bf16)]
    buffers += [pltpu.VMEM((4 * count, width), bf16) for width in second_widths]
    buffers += [pltpu.SemaphoreType.DMA((24,))]

    lanes = max(block_width, *halves)
    hidden_pick = lax.dynamic_index_in_dim(hidden_states, expert, 1, keepdims=False)
    sums_shape = (6, 8, wide)
    outs = call(
        functools.partial(grad_out_kernel, halves), 28,
        [shape((half, block_width), f32) for half in halves]
        + [shape((half, block_width), bf16) for half in halves]
        + [shape(sums_shape, f32)],
        *cotangent_rows, *values,
        scratch=buffers, whole=range(24), streamed_out=range(3),
    )
    out_own, out_sent, out_sums = outs[:3], outs[3:6], outs[6]
    got_out = along_axes(out_sent)
    outs = call(
        functools.partial(grad_in_kernel, halves), 28,
        [shape((block_width, half), f32) for half in halves]
        + [shape((block_width, half), bf16) for half in halves]
        + [shape((STAT_ROWS, lanes), f32)],
        *token_rows, *values, out_sums, hidden_pick[1:2],
        scratch=buffers + [pltpu.VMEM(sums_shape, f32)], whole=range(24), streamed_out=range(3),
    )
    in_own, in_sent, stats = outs[:3], outs[3:6], outs[6]
    got_in = along_axes(in_sent)

    width_pick = lax.dynamic_index_in_dim(width_states, expert, 1, keepdims=False)

    def padded(values):
        return jnp.pad(values, ((0, 0), (0, lanes - values.shape[1])), constant_values=1.0)

    prev = [padded(width_pick.reshape(2 * GROUP, block_width))]
    for which in range(2):
        for k in sets:
            low, high = bounds[k]
            prev.append(padded(hidden_pick[which, low:high].reshape(2, halves[k])))
    prev.append(jnp.ones((STAT_ROWS - TOTALS, lanes), f32))
    prev = jnp.concatenate(prev)

    def totals(values):
        values = values + swap(values, 1) + swap(values, 2) + swap(values, 3)
        if lax.axis_size("ffn") > 2:
            values = values + swap(values, 4)
            return values, ffn_total(values)
        ends = [(e, f) for e in range(places) for f in range(2)]

        def other(expert_mask, ffn_mask):
            moves = [(e * 2 + f, (e ^ expert_mask) * 2 + (f ^ ffn_mask)) for e, f in ends]
            return lax.ppermute(values, ("expert", "ffn"), moves)

        cube = values + swap(values, 4)
        return cube, cube + (other(0, 1) + other(4, 1))

    group_sums, whole_sums = totals(stats)
    whole_sums, got_in, got_out = lax.optimization_barrier((whole_sums, got_in, got_out))
    factors, norms = call(
        norm_kernel, 20,
        [shape((STAT_ROWS, lanes), f32), shape((8, 128), f32)],
        prev, group_sums, whole_sums, *in_own, *in_sent, *out_own, *out_sent,
        streamed=range(3, 15),
    )
    norms = totals(norms)[1]
    update_in, update_out = call(
        functools.partial(final_kernel, bounds), 24,
        [shape(local_in.shape, bf16), shape(local_out.shape, bf16)],
        prev, factors, whole_sums, norms, *in_own, *out_own, *got_in, *got_out,
        streamed=range(4, 16), streamed_out=range(2),
    )
    return (update_in[None], update_out[None])


def solution(mesh):
    return jax.shard_map(
        shards,
        mesh=mesh,
        in_specs=(
            P("expert", None),
            P("expert", None),
            P("expert", None),
            P("expert", None, "ffn"),
            P("expert", "ffn", None),
            P(),
            P(None, None, "ffn"),
        ),
        out_specs=(P("expert", None, "ffn"), P("expert", "ffn", None)),
        check_vma=False,
    )
```

```python
import functools
import math

import jax
import jax.numpy as jnp
from jax import lax
from jax.experimental import pallas as pl
from jax.experimental.pallas import tpu as pltpu
from jax.sharding import PartitionSpec as P

D = 4096
FF = 5120
GROUP = 8


DECAY_RATE = 0.9
EPS_ONE = 1e-30
ROOT_COEF = math.sqrt(2.0 / math.pi)
CUBIC_COEF = 0.044715

MASKS = (1, 2, 4)

MIB = 1024 * 1024
CUT_MIB = 44


def swap(value, mask, axis="expert"):
    pairs = [(source, source ^ mask) for source in range(lax.axis_size(axis))]
    return lax.ppermute(value, axis, pairs)


def gelu_pair(inputs):
    inner = ROOT_COEF * (inputs + CUBIC_COEF * inputs * inputs * inputs)
    tangent = jnp.tanh(inner)
    act_value = 0.5 * inputs * (1.0 + tangent)
    act_slope = 0.5 * (1.0 + tangent) + 0.5 * inputs * (1.0 - tangent * tangent) * ROOT_COEF * (
        1.0 + 3.0 * CUBIC_COEF * inputs * inputs
    )
    return (act_value, act_slope)


def ffn_total(values):
    mask = 1
    while mask < lax.axis_size("ffn"):
        values = values + swap(values, mask, "ffn")
        mask *= 2
    return values


def set_bounds(hidden):
    unit = next(unit for unit in (256, 128, 2) if hidden % unit == 0 and hidden // unit >= 3)
    units = hidden // unit
    bounds, low = [], 0
    for k in range(3):
        high = low + (units // 3 + (k < units % 3)) * unit
        bounds.append((low, high))
        low = high
    return bounds


def dot(left, right, left_dim, right_dim):
    return lax.dot_general(
        left, right, (((left_dim,), (right_dim,)), ((), ())), preferred_element_type=jnp.float32
    )


def call(kernel, mib, out_shape, *operands, scratch=(), streamed=(), streamed_out=(), whole=()):
    def spec(value, n, blocks, refs):
        if n in refs:
            return pl.BlockSpec(memory_space=pl.ANY)
        if n in blocks:
            return pl.BlockSpec(value.shape, lambda: (0,) * len(value.shape))
        return pl.BlockSpec(memory_space=pltpu.VMEM)

    return pl.pallas_call(
        kernel,
        out_shape=out_shape,
        in_specs=[spec(value, n, streamed, whole) for n, value in enumerate(operands)],
        out_specs=[spec(value, n, streamed_out, ()) for n, value in enumerate(out_shape)],
        scratch_shapes=list(scratch),
        compiler_params=pltpu.CompilerParams(vmem_limit_bytes=mib * MIB),
    )(*operands)


def padded_width(half):
    return -(-half // 128) * 128


def packed_place(step, matrix, k, halves):
    axis = (k + 1 + (step + matrix) % 2) % 3
    return axis, padded_width(halves[(axis + 2 - step) % 3]) if matrix else 0


def packed_widths(step, halves):
    return [padded_width(halves[(axis + 2 - step) % 3]) + halves[(axis + 1 + step) % 3] for axis in range(3)]


def place_in_group():
    return lax.rem(lax.axis_index("expert"), GROUP)


def bit(place, k):
    return lax.rem(lax.div(place, 1 << k), 2)


def flipped(place, mask):
    for k in range(3):
        if mask >> k & 1:
            place = place + (1 - 2 * bit(place, k)) * (1 << k)
    return place


def partial_sum(rows, own_weight, got_weight, by_row):
    width = rows.shape[1] // 2
    contract = 1 if by_row else 0
    return dot(rows[:, :width], own_weight, 1, contract) + dot(rows[:, width:], got_weight, 1, contract)


def cut_kernel(bounds, weight_in, weight_out, *refs):
    kept_in, kept_out, packed, sems = refs[:3], refs[3:6], refs[6:9], refs[9]
    copies = []
    width = weight_in.shape[0]
    for k in range(3):
        low, half = bounds[k][0], (bounds[k][1] - bounds[k][0]) // 2
        side = bit(place_in_group(), k)
        kept = pl.ds(pl.multiple_of(low + side * half, 128), half)
        copies.append((weight_in.at[:, kept], kept_in[k], 3 * k))
        copies.append((weight_out.at[kept, :], kept_out[k], 3 * k + 1))
        start = low + (1 - side) * half
        at = 0
        for n in range(half // 128):
            part = pl.ds(pl.multiple_of(start + n * 128, 128), 128)
            copies.append((weight_in.at[:, part], packed[k].at[at : at + width], 3 * k + 2))
            at += width
        for n in range(width // 128):
            part = pl.ds(pl.multiple_of(start, 128), half)
            source = weight_out.at[part, n * 128 : n * 128 + 128]
            copies.append((source, packed[k].at[at : at + half], 3 * k + 2))
            at += half
    copies = [pltpu.make_async_copy(source, target, sems.at[n]) for n, (source, target, _) in enumerate(copies)]
    for copy in copies:
        copy.start()
    for copy in copies:
        copy.wait()


def got_weight(ref, by_row, half, width):
    at = half // 128 * width if by_row else 0
    rows = half if by_row else width
    blocks = (width if by_row else half) // 128
    return jnp.concatenate([ref[at + n * rows : at + (n + 1) * rows, :] for n in range(blocks)], axis=1)


def sums_kernel(side, halves, is_packed, *refs):
    own, pairs, own_weights, got_weights = refs[0], refs[1], refs[2:8], refs[8:14]
    rows_out, sums_out = refs[14:20], refs[20:]
    count, width = own.shape[1], own.shape[2] // 2
    for matrix in range(2):
        lanes = slice(matrix * width, (matrix + 1) * width)
        for k in range(3):
            n, half = 3 * matrix + k, halves[k]
            axis = packed_place(0, matrix, k, halves)[0]
            first, second = 1 << axis, 1 << (3 - axis - k)
            for j in range(2):
                for l in range(2):
                    chunk = flipped(place_in_group(), side * first + j * second + l * (1 << k))
                    at = (j * 2 + l) * count
                    rows_out[n][at : at + count, :width] = own[chunk, :, lanes]
                    rows_out[n][at : at + count, width:] = pairs[k, chunk, :, lanes]
            by_row = matrix == 1
            got = got_weight(got_weights[n], by_row, half, width) if is_packed else got_weights[n][...]
            sums = partial_sum(rows_out[n][...], own_weights[n][...], got, by_row)
            if side:
                at = packed_place(0, matrix, k, halves)[1]
                sums_out[axis][:, at : at + half] = sums.astype(jnp.bfloat16)
            else:
                sums_out[n][...] = sums


def add_kernel(halves, *refs):
    kept, received, total_out, sent_out = refs[:6], refs[6:9], refs[9:15], refs[15:18]
    for matrix in range(2):
        for k in range(3):
            n, half = 3 * matrix + k, halves[k]
            middle = kept[n].shape[0] // 2
            axis, at = packed_place(0, matrix, k, halves)
            total = kept[n][...] + received[axis][:, at : at + half].astype(jnp.float32)
            total_out[n][...] = total[:middle]
            axis, at = packed_place(1, matrix, k, halves)
            sent_out[axis][:, at : at + half] = total[middle:].astype(jnp.bfloat16)


def act_kernel(halves, *refs):
    kept, received, outs = refs[:6], refs[6:9], refs[9:12]
    for k in range(3):
        values = []
        for matrix in range(2):
            axis, at = packed_place(1, matrix, k, halves)
            values.append(kept[3 * matrix + k][...] + received[axis][:, at : at + halves[k]].astype(jnp.float32))
        act_value, act_slope = gelu_pair(values[0])
        for matrix, value in enumerate((act_value, values[1] * act_slope)):
            axis, at = packed_place(0, matrix, k, halves)
            outs[axis][:, at : at + halves[k]] = value.astype(jnp.bfloat16)


def join_kernel(halves, *refs):
    own, got, outs = refs[:3], refs[3:6], refs[6:9]
    for matrix in range(2):
        for k in range(3):
            source, start = packed_place(0, matrix, k, halves)
            axis, at = packed_place(1, matrix, k, halves)
            rows = own[source].shape[0]
            outs[axis][:rows, at : at + halves[k]] = own[source][:, start : start + halves[k]]
            outs[axis][rows:, at : at + halves[k]] = got[source][:, start : start + halves[k]]


def gradients(hidden_first, halves, rows, values, row_buffers, value_buffers, sems, own_out, sent_out, sums_out):
    matrix = 0 if hidden_first else 1
    part = row_buffers.shape[1] // 4
    width = row_buffers.shape[2] // 2

    def copies(n, parts, buffer):
        return [
            pltpu.make_async_copy(parts[i], buffer.at[pl.ds(i * part, part)], sems.at[n * 4 + i]) for i in range(4)
        ]

    value_copies, row_copies = {}, {}
    for k in range(3):
        axis, at = packed_place(1, matrix, k, halves)
        row_copies[k] = copies(k, rows[4 * k : 4 * k + 4], row_buffers.at[k])
        parts, buffer = values[4 * axis : 4 * axis + 4], value_buffers[axis]
        if all(half % 128 == 0 for half in halves):
            parts = [value.at[:, at : at + halves[k]] for value in parts]
            buffer = buffer.at[:, at : at + halves[k]]
        value_copies[k] = copies(3 + axis, parts, buffer)
        for copy in row_copies[k] + value_copies[k]:
            copy.start()
    for k in range(3):
        for copy in row_copies[k] + value_copies[k]:
            copy.wait()
        axis, at = packed_place(1, matrix, k, halves)
        value = value_buffers[axis][:, at : at + halves[k]]
        if hidden_first:
            grad = dot(value, row_buffers[k], 0, 0)
            own_out[k][...] = grad[:, :width]
            sent_out[k][...] = grad[:, width:].astype(jnp.bfloat16)
        else:
            grad = dot(row_buffers[k], value, 0, 0)
            own_out[k][...] = grad[:width]
            sent_out[k][...] = grad[width:].astype(jnp.bfloat16)
        square = grad * grad + EPS_ONE
        down = jnp.sum(square, axis=0, keepdims=True)
        down = jnp.broadcast_to(down, (8, square.shape[1]))
        if square.shape[1] % 128 == 0:
            square = sum(square[:, n : n + 128] for n in range(0, square.shape[1], 128))
        across = dot(jnp.ones((8, square.shape[1]), jnp.float32), square, 1, 1)
        by_width, by_hidden = (down, across) if hidden_first else (across, down)
        sums_out[k] = by_width
        sums_out[3 + k] = jnp.zeros(sums_out.shape[1:], jnp.float32)
        sums_out[3 + k, :, : by_hidden.shape[1]] = by_hidden


def grad_out_kernel(halves, *refs):
    rows, values, outs, buffers = refs[:12], refs[12:24], refs[24:31], refs[31:]
    gradients(True, halves, rows, values, buffers[0], buffers[1:4], buffers[4], outs[:3], outs[3:6], outs[6])


def grad_in_kernel(halves, *refs):
    rows, values, other_sums, hidden_prev, outs, buffers = (
        refs[:12], refs[12:24], refs[24], refs[25], refs[26:33], refs[33:]
    )
    sums = buffers[5]
    gradients(False, halves, rows, values, buffers[0], buffers[1:4], buffers[4], outs[:3], outs[3:6], sums)
    collect(hidden_prev, (sums, other_sums), outs[6])


IN_WIDTH, OUT_WIDTH, IN_HIDDEN, OUT_HIDDEN, TOTALS, STAT_ROWS = 0, 8, 16, 22, 28, 32


def collect(hidden_prev, all_sums, stats_out):
    place = place_in_group()
    stats_out[...] = jnp.zeros_like(stats_out)
    lanes = stats_out.shape[1]
    for which in range(2):
        sums = all_sums[which]
        width_row, hidden_row = (IN_WIDTH, OUT_WIDTH)[which], (IN_HIDDEN, OUT_HIDDEN)[which]
        width = sums.shape[2] // 2
        stats_out[pl.ds(width_row + place, 1), :] = sum(sums[k, 0:1, :width] for k in range(3))
        total = 0.0
        for k in range(3):
            stats_out[pl.ds(width_row + flipped(place, 1 << k), 1), :] = sums[k, 0:1, width:]
            row = sums[3 + k, 0:1, :lanes]
            stats_out[pl.ds(hidden_row + 2 * k + bit(place, k), 1), :] = row
            total = total + jnp.sum(row, axis=1, keepdims=True)
        stats_out[TOTALS + which : TOTALS + which + 1, :] = jnp.broadcast_to(total, (1, lanes))
    previous = jnp.sum(hidden_prev[...], axis=1, keepdims=True)
    stats_out[TOTALS + 2 : TOTALS + 3, :] = jnp.broadcast_to(previous, (1, lanes))


def stat_row(stats_ref, index):
    return stats_ref[pl.ds(index, 1), :]


def upright(row):
    return jnp.transpose(jnp.broadcast_to(row, (8, row.shape[1])))[:, 0:1]


def norm_kernel(prev, group_sums, whole_sums, *refs):
    own_in, sent_in, own_out, sent_out = refs[:3], refs[3:6], refs[6:9], refs[9:12]
    factors_out, norms_out = refs[12], refs[13]
    place = place_in_group()
    width = own_in[0].shape[0]
    row = lax.broadcasted_iota(jnp.int32, prev.shape, 0)
    by_width = row < IN_HIDDEN
    mean = jnp.where(by_width, whole_sums[...] / FF, group_sums[...] / D)
    factors_out[...] = DECAY_RATE * prev[...] + (1.0 - DECAY_RATE) * mean
    norm_in, norm_out = 0.0, 0.0
    for k in range(3):
        half = own_in[k].shape[1]
        partner = flipped(place, 1 << k)
        own_row = stat_row(factors_out, IN_WIDTH + place)[:, :width]
        pair_row = stat_row(factors_out, IN_WIDTH + partner)[:, :width]
        hidden_row = stat_row(factors_out, IN_HIDDEN + 2 * k + bit(place, k))[:, :half]
        sent = sent_in[k][...].astype(jnp.float32)
        down = jnp.sum(own_in[k][...] * own_in[k][...] * upright(1.0 / own_row), axis=0, keepdims=True)
        down = down + jnp.sum(sent * sent * upright(1.0 / pair_row), axis=0, keepdims=True)
        norm_in = norm_in + jnp.sum(down / hidden_row, axis=1, keepdims=True)
        own_row = stat_row(factors_out, OUT_WIDTH + place)[:, :width]
        pair_row = stat_row(factors_out, OUT_WIDTH + partner)[:, :width]
        hidden_row = stat_row(factors_out, OUT_HIDDEN + 2 * k + bit(place, k))[:, :half]
        inverse = upright(1.0 / hidden_row)
        sent = sent_out[k][...].astype(jnp.float32)
        down = jnp.sum(own_out[k][...] * own_out[k][...] * inverse, axis=0, keepdims=True) / own_row
        down = down + jnp.sum(sent * sent * inverse, axis=0, keepdims=True) / pair_row
        norm_out = norm_out + jnp.sum(down, axis=1, keepdims=True)
    row = lax.broadcasted_iota(jnp.int32, norms_out.shape, 0)
    norms_out[...] = jnp.where(row == 0, norm_in, norm_out)


def final_kernel(bounds, prev, factors, whole_sums, norms, *refs):
    own_in, own_out, got_in, got_out = refs[:3], refs[3:6], refs[6:9], refs[9:12]
    update_in, update_out = refs[12:]
    place = place_in_group()
    width = update_in.shape[0]
    count = float(D) * float(FF)
    mean_in = DECAY_RATE * jnp.mean(prev[IN_WIDTH : IN_WIDTH + 8, :width], keepdims=True)
    mean_in = mean_in + (1.0 - DECAY_RATE) * whole_sums[TOTALS : TOTALS + 1, 0:1] / count
    mean_out = DECAY_RATE * whole_sums[TOTALS + 2 : TOTALS + 3, 0:1] / (FF * GROUP)
    mean_out = mean_out + (1.0 - DECAY_RATE) * whole_sums[TOTALS + 1 : TOTALS + 2, 0:1] / count
    factor_in = jnp.sqrt(mean_in) / jnp.maximum(1.0, jnp.sqrt(mean_in * norms[0:1, 0:1] / count))
    factor_out = jnp.sqrt(mean_out) / jnp.maximum(1.0, jnp.sqrt(mean_out * norms[1:2, 0:1] / count))
    width_in = upright(lax.rsqrt(stat_row(factors, IN_WIDTH + place)[:, :width]) * factor_in)
    width_out = lax.rsqrt(stat_row(factors, OUT_WIDTH + place)[:, :width]) * factor_out
    for k in range(3):
        low, half = bounds[k][0], (bounds[k][1] - bounds[k][0]) // 2
        own_bit = bit(place, k)
        if half % 128:
            width_scaled = (own_in[k][...] * width_in, got_in[k][...].astype(jnp.float32) * width_in)
            for side in range(2):
                hidden_in = lax.rsqrt(factors[IN_HIDDEN + 2 * k + side : IN_HIDDEN + 2 * k + side + 1, :half])
                value = jnp.where(own_bit == side, *width_scaled) * hidden_in
                update_in[:, low + side * half : low + side * half + half] = value.astype(update_in.dtype)
        for own in (True, False):
            side = own_bit if own else 1 - own_bit
            start = pl.multiple_of(low + side * half, math.gcd(low, half))
            hidden_out = upright(lax.rsqrt(stat_row(factors, OUT_HIDDEN + 2 * k + side)[:, :half]))
            if half % 128 == 0:
                hidden_in = lax.rsqrt(stat_row(factors, IN_HIDDEN + 2 * k + side)[:, :half])
                value = own_in[k][...] if own else got_in[k][...].astype(jnp.float32)
                update_in[:, pl.ds(start, half)] = (value * width_in * hidden_in).astype(update_in.dtype)
            value = own_out[k][...] if own else got_out[k][...].astype(jnp.float32)
            update_out[pl.ds(start, half), :] = (value * hidden_out * width_out).astype(update_out.dtype)


def shards(tokens, cotangent, expert_ids, in_weight, out_weight, width_states, hidden_states):
    bf16, f32 = jnp.bfloat16, jnp.float32
    shape = jax.ShapeDtypeStruct
    experts = width_states.shape[1]
    tok_rows, width = tokens.shape
    capacity = 5 * tok_rows // (4 * experts)
    part_cap = capacity // 2
    places = lax.axis_size("expert")
    block_width = width // GROUP
    position = lax.axis_index("expert")
    expert = position // GROUP
    part = lax.axis_index("ffn") % 2
    bits = [position >> k & 1 for k in range(3)]
    bounds = set_bounds(in_weight.shape[2])
    halves = [(high - low) // 2 for low, high in bounds]
    sets = range(3)
    local_in = in_weight[0]
    local_out = out_weight[0]

    is_packed = all(half % 128 == 0 for half in halves) and block_width % 128 == 0
    if is_packed:
        kept_shapes = [shape((block_width, half), bf16) for half in halves]
        kept_shapes += [shape((half, block_width), bf16) for half in halves]
        packed_shapes = [shape((2 * half * block_width // 128, 128), bf16) for half in halves]
        copies = 6 + sum(half + block_width for half in halves) // 128
        cuts = call(
            functools.partial(cut_kernel, bounds), CUT_MIB, kept_shapes + packed_shapes, local_in, local_out,
            scratch=[pltpu.SemaphoreType.DMA((copies,))], whole=(0, 1),
        )
        got_weights = [swap(cuts[6 + k], MASKS[k]) for k in sets] * 2
    else:
        cuts = []
        for taken in range(2):
            at = [bounds[k][0] + (1 - bits[k] if taken else bits[k]) * halves[k] for k in sets]
            cuts += [lax.dynamic_slice_in_dim(local_in, at[k], halves[k], 1) for k in sets]
            cuts += [lax.dynamic_slice_in_dim(local_out, at[k], halves[k], 0) for k in sets]
        got_weights = [swap(cuts[6 + n], MASKS[n % 3]) for n in range(6)]

    route_ids = expert_ids[:, 0]
    onehot = (route_ids[:, None] == jnp.arange(experts, dtype=jnp.int32)[None, :]).astype(jnp.int32)
    before = jnp.cumsum(onehot, axis=0) - onehot
    slot_index = jnp.sum(before * onehot, axis=1) - part * part_cap
    valid = (slot_index >= 0) & (slot_index < part_cap)
    target = jnp.where(valid, route_ids * part_cap + slot_index, -1)
    select = (jnp.arange(experts * part_cap, dtype=jnp.int32)[:, None] == target[None, :]).astype(bf16)

    def route(values):
        routed = dot(select, values, 1, 0).astype(bf16)
        routed = routed.reshape(experts, part_cap, GROUP, block_width).transpose(0, 2, 1, 3)
        return routed.reshape(places, part_cap, block_width)

    routed = jnp.concatenate([route(tokens), route(cotangent)], axis=2)
    got = lax.all_to_all(routed, "expert", split_axis=0, concat_axis=0, tiled=True)
    got, got_weights = lax.optimization_barrier((got, got_weights))
    got = got.reshape(places // GROUP, GROUP, part_cap, 2 * block_width).transpose(1, 0, 2, 3)
    got = got.reshape(GROUP, -1, 2 * block_width)

    count = got.shape[1] * 4
    wide = 2 * block_width
    first_widths, second_widths = packed_widths(0, halves), packed_widths(1, halves)

    def shapes(rows, widths, dtype):
        return [shape((rows, width), dtype) for width in widths]

    def along_axes(values):
        return [swap(value, mask) for value, mask in zip(values, MASKS)]

    pairs = jnp.stack([swap(got, MASKS[k]) for k in sets])
    blocks = [(got, pairs), (swap(got, 1, "ffn"), swap(pairs, 1, "ffn"))]
    chains = range(2)
    row_shapes = [shape((count, wide), bf16)] * 6

    def sums(chain, side, out_shapes):
        kernel = functools.partial(sums_kernel, side, halves, is_packed)
        outs = call(
            kernel, 40, row_shapes + out_shapes, *blocks[chain], *cuts[:6], *got_weights,
            streamed_out=range(6),
        )
        return outs[:6], outs[6:]

    far_rows, received, near_rows, kept = [None] * 2, [None] * 2, [None] * 2, [None] * 2
    for c in chains:
        far_rows[c], sent = sums(c, 1, shapes(count, first_widths, bf16))
        received[c] = along_axes(sent)
    for c in chains:
        near_rows[c], kept[c] = sums(c, 0, shapes(count, halves * 2, f32))
    for c in chains:
        out_shapes = shapes(count // 2, halves * 2, f32) + shapes(count // 2, second_widths, bf16)
        outs = call(functools.partial(add_kernel, halves), 8, out_shapes, *kept[c], *received[c])
        kept[c], received[c] = outs[:6], along_axes(outs[6:])
    owns, nears, fars = [None] * 2, [None] * 2, [None] * 2
    for c in chains:
        out_shapes = shapes(count // 2, first_widths, bf16)
        owns[c] = call(functools.partial(act_kernel, halves), 8, out_shapes, *kept[c], *received[c])
        received[c] = along_axes(owns[c])
    for c in chains:
        out_shapes = shapes(count, second_widths, bf16)
        nears[c] = call(functools.partial(join_kernel, halves), 8, out_shapes, *owns[c], *received[c])
        fars[c] = along_axes(nears[c])

    def parts(near, far):
        return [value[n] for n in range(3) for chain in chains for value in (near[chain], far[chain])]

    token_rows = parts([rows[:3] for rows in near_rows], [rows[:3] for rows in far_rows])
    cotangent_rows = parts([rows[3:] for rows in near_rows], [rows[3:] for rows in far_rows])
    values = parts(nears, fars)
    buffers = [pltpu.VMEM((3, 4 * count, wide), bf16)]
    buffers += [pltpu.VMEM((4 * count, width), bf16) for width in second_widths]
    buffers += [pltpu.SemaphoreType.DMA((24,))]

    lanes = max(block_width, *halves)
    hidden_pick = lax.dynamic_index_in_dim(hidden_states, expert, 1, keepdims=False)
    sums_shape = (6, 8, wide)
    outs = call(
        functools.partial(grad_out_kernel, halves), 56,
        [shape((half, block_width), f32) for half in halves]
        + [shape((half, block_width), bf16) for half in halves]
        + [shape(sums_shape, f32)],
        *cotangent_rows, *values,
        scratch=buffers, whole=range(24), streamed_out=range(3),
    )
    out_own, out_sent, out_sums = outs[:3], outs[3:6], outs[6]
    got_out = along_axes(out_sent)
    outs = call(
        functools.partial(grad_in_kernel, halves), 56,
        [shape((block_width, half), f32) for half in halves]
        + [shape((block_width, half), bf16) for half in halves]
        + [shape((STAT_ROWS, lanes), f32)],
        *token_rows, *values, out_sums, hidden_pick[1:2],
        scratch=buffers + [pltpu.VMEM(sums_shape, f32)], whole=range(24), streamed_out=range(3),
    )
    in_own, in_sent, stats = outs[:3], outs[3:6], outs[6]
    got_in = along_axes(in_sent)

    width_pick = lax.dynamic_index_in_dim(width_states, expert, 1, keepdims=False)

    def padded(values):
        return jnp.pad(values, ((0, 0), (0, lanes - values.shape[1])), constant_values=1.0)

    prev = [padded(width_pick.reshape(2 * GROUP, block_width))]
    for which in range(2):
        for k in sets:
            low, high = bounds[k]
            prev.append(padded(hidden_pick[which, low:high].reshape(2, halves[k])))
    prev.append(jnp.ones((STAT_ROWS - TOTALS, lanes), f32))
    prev = jnp.concatenate(prev)

    def totals(values):
        values = values + swap(values, 1) + swap(values, 2) + swap(values, 3)
        if lax.axis_size("ffn") > 2:
            values = values + swap(values, 4)
            return values, ffn_total(values)
        ends = [(e, f) for e in range(places) for f in range(2)]

        def other(expert_mask, ffn_mask):
            moves = [(e * 2 + f, (e ^ expert_mask) * 2 + (f ^ ffn_mask)) for e, f in ends]
            return lax.ppermute(values, ("expert", "ffn"), moves)

        cube = values + swap(values, 4)
        return cube, cube + (other(0, 1) + other(4, 1))

    stats, got_out = lax.optimization_barrier((stats, got_out))
    group_sums, whole_sums = totals(stats)
    whole_sums, got_in = lax.optimization_barrier((whole_sums, got_in))
    factors, norms = call(
        norm_kernel, 52,
        [shape((STAT_ROWS, lanes), f32), shape((8, 128), f32)],
        prev, group_sums, whole_sums, *in_own, *in_sent, *out_own, *out_sent,
        streamed=range(3, 15),
    )
    norms = totals(norms)[1]
    update_in, update_out = call(
        functools.partial(final_kernel, bounds), 52,
        [shape(local_in.shape, bf16), shape(local_out.shape, bf16)],
        prev, factors, whole_sums, norms, *in_own, *out_own, *got_in, *got_out,
        streamed=range(4, 16), streamed_out=range(2),
    )
    return (update_in[None], update_out[None])


def solution(mesh):
    return jax.shard_map(
        shards,
        mesh=mesh,
        in_specs=(
            P("expert", None),
            P("expert", None),
            P("expert", None),
            P("expert", None, "ffn"),
            P("expert", "ffn", None),
            P(),
            P(None, None, "ffn"),
        ),
        out_specs=(P("expert", None, "ffn"), P("expert", "ffn", None)),
        check_vma=False,
    )
```

```python
import functools
import math

import jax
import jax.numpy as jnp
from jax import lax
from jax.experimental import pallas as pl
from jax.experimental.pallas import tpu as pltpu
from jax.sharding import PartitionSpec as P

D = 4096
FF = 5120
GROUP = 8


DECAY_RATE = 0.9
EPS_ONE = 1e-30
ROOT_COEF = math.sqrt(2.0 / math.pi)
CUBIC_COEF = 0.044715

MASKS = (1, 2, 4)

MIB = 1024 * 1024
CUT_MIB = 8


def swap(value, mask, axis="expert"):
    pairs = [(source, source ^ mask) for source in range(lax.axis_size(axis))]
    return lax.ppermute(value, axis, pairs)


def gelu_pair(inputs):
    inner = ROOT_COEF * (inputs + CUBIC_COEF * inputs * inputs * inputs)
    tangent = jnp.tanh(inner)
    act_value = 0.5 * inputs * (1.0 + tangent)
    act_slope = 0.5 * (1.0 + tangent) + 0.5 * inputs * (1.0 - tangent * tangent) * ROOT_COEF * (
        1.0 + 3.0 * CUBIC_COEF * inputs * inputs
    )
    return (act_value, act_slope)


def ffn_total(values):
    mask = 1
    while mask < lax.axis_size("ffn"):
        values = values + swap(values, mask, "ffn")
        mask *= 2
    return values


def set_bounds(hidden):
    unit = next(unit for unit in (256, 128, 2) if hidden % unit == 0 and hidden // unit >= 3)
    units = hidden // unit
    bounds, low = [], 0
    for k in range(3):
        high = low + (units // 3 + (k < units % 3)) * unit
        bounds.append((low, high))
        low = high
    return bounds


def dot(left, right, left_dim, right_dim):
    return lax.dot_general(
        left, right, (((left_dim,), (right_dim,)), ((), ())), preferred_element_type=jnp.float32
    )


def call(kernel, mib, out_shape, *operands, scratch=(), streamed=(), streamed_out=(), whole=(), whole_out=()):
    def spec(value, n, blocks, refs):
        if n in refs:
            return pl.BlockSpec(memory_space=pltpu.HBM)
        if n in blocks:
            return pl.BlockSpec(value.shape, lambda: (0,) * len(value.shape))
        return pl.BlockSpec(memory_space=pltpu.VMEM)

    return pl.pallas_call(
        kernel,
        out_shape=out_shape,
        in_specs=[spec(value, n, streamed, whole) for n, value in enumerate(operands)],
        out_specs=[spec(value, n, streamed_out, whole_out) for n, value in enumerate(out_shape)],
        scratch_shapes=list(scratch),
        compiler_params=pltpu.CompilerParams(vmem_limit_bytes=mib * MIB),
    )(*operands)


def padded_width(half):
    return -(-half // 128) * 128


def packed_place(step, matrix, k, halves):
    axis = (k + 1 + (step + matrix) % 2) % 3
    return axis, padded_width(halves[(axis + 2 - step) % 3]) if matrix else 0


def packed_widths(step, halves):
    return [padded_width(halves[(axis + 2 - step) % 3]) + halves[(axis + 1 + step) % 3] for axis in range(3)]


def place_in_group():
    return lax.rem(lax.axis_index("expert"), GROUP)


def bit(place, k):
    return lax.rem(lax.div(place, 1 << k), 2)


def flipped(place, mask):
    for k in range(3):
        if mask >> k & 1:
            place = place + (1 - 2 * bit(place, k)) * (1 << k)
    return place


def partial_sum(rows, own_weight, got_weight, by_row):
    width = rows.shape[1] // 2
    contract = 1 if by_row else 0
    return dot(rows[:, :width], own_weight, 1, contract) + dot(rows[:, width:], got_weight, 1, contract)


def cut_kernel(bounds, weight_in, weight_out, *refs):
    kept_in, kept_out, packed, sems = refs[:3], refs[3:6], refs[6:9], refs[9]
    copies = []
    width = weight_in.shape[0]
    for k in range(3):
        low, half = bounds[k][0], (bounds[k][1] - bounds[k][0]) // 2
        side = bit(place_in_group(), k)
        kept = pl.ds(pl.multiple_of(low + side * half, 128), half)
        copies.append((weight_in.at[:, kept], kept_in[k], 3 * k))
        copies.append((weight_out.at[kept, :], kept_out[k], 3 * k + 1))
        start = low + (1 - side) * half
        at = 0
        for n in range(half // 128):
            part = pl.ds(pl.multiple_of(start + n * 128, 128), 128)
            copies.append((weight_in.at[:, part], packed[k].at[at : at + width], 3 * k + 2))
            at += width
        for n in range(width // 128):
            part = pl.ds(pl.multiple_of(start, 128), half)
            source = weight_out.at[part, n * 128 : n * 128 + 128]
            copies.append((source, packed[k].at[at : at + half], 3 * k + 2))
            at += half
    copies = [pltpu.make_async_copy(source, target, sems.at[n]) for n, (source, target, _) in enumerate(copies)]
    for copy in copies:
        copy.start()
    for copy in copies:
        copy.wait()


def got_weight(ref, by_row, half, width):
    at = half // 128 * width if by_row else 0
    rows = half if by_row else width
    blocks = (width if by_row else half) // 128
    return jnp.concatenate([ref[at + n * rows : at + (n + 1) * rows, :] for n in range(blocks)], axis=1)


def sums_kernel(side, halves, is_packed, *refs):
    own, pairs, own_weights, got_weights = refs[0], refs[1], refs[2:8], refs[8:14]
    rows_out, sums_out, all_rows, sems = refs[14:20], refs[20:-2], refs[-2], refs[-1]
    copies = [pltpu.make_async_copy(all_rows.at[n], rows_out[n], sems.at[n]) for n in range(6)]
    count, width = own.shape[1], own.shape[2] // 2
    for matrix in range(2):
        lanes = slice(matrix * width, (matrix + 1) * width)
        for k in range(3):
            n, half = 3 * matrix + k, halves[k]
            axis = packed_place(0, matrix, k, halves)[0]
            first, second = 1 << axis, 1 << (3 - axis - k)
            for j in range(2):
                for l in range(2):
                    chunk = flipped(place_in_group(), side * first + j * second + l * (1 << k))
                    at = (j * 2 + l) * count
                    all_rows[n, at : at + count, :width] = own[chunk, :, lanes]
                    all_rows[n, at : at + count, width:] = pairs[k, chunk, :, lanes]
            copies[n].start()
            by_row = matrix == 1
            got = got_weight(got_weights[n], by_row, half, width) if is_packed else got_weights[n][...]
            sums = partial_sum(all_rows[n], own_weights[n][...], got, by_row)
            if side:
                at = packed_place(0, matrix, k, halves)[1]
                sums_out[axis][:, at : at + half] = sums.astype(jnp.bfloat16)
            else:
                sums_out[n][...] = sums
    for copy in copies:
        copy.wait()


def add_kernel(halves, *refs):
    kept, received, total_out, sent_out = refs[:6], refs[6:9], refs[9:15], refs[15:18]
    for matrix in range(2):
        for k in range(3):
            n, half = 3 * matrix + k, halves[k]
            middle = kept[n].shape[0] // 2
            axis, at = packed_place(0, matrix, k, halves)
            total = kept[n][...] + received[axis][:, at : at + half].astype(jnp.float32)
            total_out[n][...] = total[:middle]
            axis, at = packed_place(1, matrix, k, halves)
            sent_out[axis][:, at : at + half] = total[middle:].astype(jnp.bfloat16)


def act_kernel(halves, *refs):
    kept, received, outs = refs[:6], refs[6:9], refs[9:12]
    for k in range(3):
        values = []
        for matrix in range(2):
            axis, at = packed_place(1, matrix, k, halves)
            values.append(kept[3 * matrix + k][...] + received[axis][:, at : at + halves[k]].astype(jnp.float32))
        act_value, act_slope = gelu_pair(values[0])
        for matrix, value in enumerate((act_value, values[1] * act_slope)):
            axis, at = packed_place(0, matrix, k, halves)
            outs[axis][:, at : at + halves[k]] = value.astype(jnp.bfloat16)


def join_kernel(halves, *refs):
    own, got, outs = refs[:3], refs[3:6], refs[6:9]
    for matrix in range(2):
        for k in range(3):
            source, start = packed_place(0, matrix, k, halves)
            axis, at = packed_place(1, matrix, k, halves)
            rows = own[source].shape[0]
            outs[axis][:rows, at : at + halves[k]] = own[source][:, start : start + halves[k]]
            outs[axis][rows:, at : at + halves[k]] = got[source][:, start : start + halves[k]]


def gradients(hidden_first, halves, rows, values, row_buffers, value_buffers, sems, own_out, sent_out, sums_out):
    matrix = 0 if hidden_first else 1
    part = row_buffers.shape[1] // 4
    width = row_buffers.shape[2] // 2

    def copies(n, parts, buffer):
        return [
            pltpu.make_async_copy(parts[i], buffer.at[pl.ds(i * part, part)], sems.at[n * 4 + i]) for i in range(4)
        ]

    value_copies, row_copies = {}, {}
    for k in range(3):
        axis, at = packed_place(1, matrix, k, halves)
        row_copies[k] = copies(k, rows[4 * k : 4 * k + 4], row_buffers.at[k])
        parts, buffer = values[4 * axis : 4 * axis + 4], value_buffers[axis]
        if all(half % 128 == 0 for half in halves):
            parts = [value.at[:, at : at + halves[k]] for value in parts]
            buffer = buffer.at[:, at : at + halves[k]]
        value_copies[k] = copies(3 + axis, parts, buffer)
        for copy in row_copies[k] + value_copies[k]:
            copy.start()
    for k in range(3):
        for copy in row_copies[k] + value_copies[k]:
            copy.wait()
        axis, at = packed_place(1, matrix, k, halves)
        value = value_buffers[axis][:, at : at + halves[k]]
        if hidden_first:
            grad = dot(value, row_buffers[k], 0, 0)
            own_out[k][...] = grad[:, :width]
            sent_out[k][...] = grad[:, width:].astype(jnp.bfloat16)
        else:
            grad = dot(row_buffers[k], value, 0, 0)
            own_out[k][...] = grad[:width]
            sent_out[k][...] = grad[width:].astype(jnp.bfloat16)
        square = grad * grad + EPS_ONE
        down = jnp.sum(square, axis=0, keepdims=True)
        down = jnp.broadcast_to(down, (8, square.shape[1]))
        if square.shape[1] % 128 == 0:
            square = sum(square[:, n : n + 128] for n in range(0, square.shape[1], 128))
        across = dot(jnp.ones((8, square.shape[1]), jnp.float32), square, 1, 1)
        by_width, by_hidden = (down, across) if hidden_first else (across, down)
        sums_out[k] = by_width
        sums_out[3 + k] = jnp.zeros(sums_out.shape[1:], jnp.float32)
        sums_out[3 + k, :, : by_hidden.shape[1]] = by_hidden


def grad_out_kernel(halves, *refs):
    rows, values, outs, buffers = refs[:12], refs[12:24], refs[24:31], refs[31:]
    gradients(True, halves, rows, values, buffers[0], buffers[1:4], buffers[4], outs[:3], outs[3:6], outs[6])


def grad_in_kernel(halves, *refs):
    rows, values, other_sums, hidden_prev, outs, buffers = (
        refs[:12], refs[12:24], refs[24], refs[25], refs[26:33], refs[33:]
    )
    sums = buffers[5]
    gradients(False, halves, rows, values, buffers[0], buffers[1:4], buffers[4], outs[:3], outs[3:6], sums)
    collect(hidden_prev, (sums, other_sums), outs[6])


IN_WIDTH, OUT_WIDTH, IN_HIDDEN, OUT_HIDDEN, TOTALS, STAT_ROWS = 0, 8, 16, 22, 28, 32


def collect(hidden_prev, all_sums, stats_out):
    place = place_in_group()
    stats_out[...] = jnp.zeros_like(stats_out)
    lanes = stats_out.shape[1]
    for which in range(2):
        sums = all_sums[which]
        width_row, hidden_row = (IN_WIDTH, OUT_WIDTH)[which], (IN_HIDDEN, OUT_HIDDEN)[which]
        width = sums.shape[2] // 2
        stats_out[pl.ds(width_row + place, 1), :] = sum(sums[k, 0:1, :width] for k in range(3))
        total = 0.0
        for k in range(3):
            stats_out[pl.ds(width_row + flipped(place, 1 << k), 1), :] = sums[k, 0:1, width:]
            row = sums[3 + k, 0:1, :lanes]
            stats_out[pl.ds(hidden_row + 2 * k + bit(place, k), 1), :] = row
            total = total + jnp.sum(row, axis=1, keepdims=True)
        stats_out[TOTALS + which : TOTALS + which + 1, :] = jnp.broadcast_to(total, (1, lanes))
    previous = jnp.sum(hidden_prev[...], axis=1, keepdims=True)
    stats_out[TOTALS + 2 : TOTALS + 3, :] = jnp.broadcast_to(previous, (1, lanes))


def stat_row(stats_ref, index):
    return stats_ref[pl.ds(index, 1), :]


def upright(row):
    return jnp.transpose(jnp.broadcast_to(row, (8, row.shape[1])))[:, 0:1]


def norm_kernel(prev, group_sums, whole_sums, *refs):
    own_in, sent_in, own_out, sent_out = refs[:3], refs[3:6], refs[6:9], refs[9:12]
    factors_out, norms_out = refs[12], refs[13]
    place = place_in_group()
    width = own_in[0].shape[0]
    row = lax.broadcasted_iota(jnp.int32, prev.shape, 0)
    by_width = row < IN_HIDDEN
    mean = jnp.where(by_width, whole_sums[...] / FF, group_sums[...] / D)
    factors_out[...] = DECAY_RATE * prev[...] + (1.0 - DECAY_RATE) * mean
    norm_in, norm_out = 0.0, 0.0
    for k in range(3):
        half = own_in[k].shape[1]
        partner = flipped(place, 1 << k)
        own_row = stat_row(factors_out, IN_WIDTH + place)[:, :width]
        pair_row = stat_row(factors_out, IN_WIDTH + partner)[:, :width]
        hidden_row = stat_row(factors_out, IN_HIDDEN + 2 * k + bit(place, k))[:, :half]
        sent = sent_in[k][...].astype(jnp.float32)
        down = jnp.sum(own_in[k][...] * own_in[k][...] * upright(1.0 / own_row), axis=0, keepdims=True)
        down = down + jnp.sum(sent * sent * upright(1.0 / pair_row), axis=0, keepdims=True)
        norm_in = norm_in + jnp.sum(down / hidden_row, axis=1, keepdims=True)
        own_row = stat_row(factors_out, OUT_WIDTH + place)[:, :width]
        pair_row = stat_row(factors_out, OUT_WIDTH + partner)[:, :width]
        hidden_row = stat_row(factors_out, OUT_HIDDEN + 2 * k + bit(place, k))[:, :half]
        inverse = upright(1.0 / hidden_row)
        sent = sent_out[k][...].astype(jnp.float32)
        down = jnp.sum(own_out[k][...] * own_out[k][...] * inverse, axis=0, keepdims=True) / own_row
        down = down + jnp.sum(sent * sent * inverse, axis=0, keepdims=True) / pair_row
        norm_out = norm_out + jnp.sum(down, axis=1, keepdims=True)
    row = lax.broadcasted_iota(jnp.int32, norms_out.shape, 0)
    norms_out[...] = jnp.where(row == 0, norm_in, norm_out)


def final_kernel(bounds, prev, factors, whole_sums, norms, *refs):
    own_in, own_out, got_in, got_out = refs[:3], refs[3:6], refs[6:9], refs[9:12]
    update_in, update_out = refs[12:]
    place = place_in_group()
    width = update_in.shape[0]
    count = float(D) * float(FF)
    mean_in = DECAY_RATE * jnp.mean(prev[IN_WIDTH : IN_WIDTH + 8, :width], keepdims=True)
    mean_in = mean_in + (1.0 - DECAY_RATE) * whole_sums[TOTALS : TOTALS + 1, 0:1] / count
    mean_out = DECAY_RATE * whole_sums[TOTALS + 2 : TOTALS + 3, 0:1] / (FF * GROUP)
    mean_out = mean_out + (1.0 - DECAY_RATE) * whole_sums[TOTALS + 1 : TOTALS + 2, 0:1] / count
    factor_in = jnp.sqrt(mean_in) / jnp.maximum(1.0, jnp.sqrt(mean_in * norms[0:1, 0:1] / count))
    factor_out = jnp.sqrt(mean_out) / jnp.maximum(1.0, jnp.sqrt(mean_out * norms[1:2, 0:1] / count))
    width_in = upright(lax.rsqrt(stat_row(factors, IN_WIDTH + place)[:, :width]) * factor_in)
    width_out = lax.rsqrt(stat_row(factors, OUT_WIDTH + place)[:, :width]) * factor_out
    for k in range(3):
        low, half = bounds[k][0], (bounds[k][1] - bounds[k][0]) // 2
        own_bit = bit(place, k)
        if half % 128:
            width_scaled = (own_in[k][...] * width_in, got_in[k][...].astype(jnp.float32) * width_in)
            for side in range(2):
                hidden_in = lax.rsqrt(factors[IN_HIDDEN + 2 * k + side : IN_HIDDEN + 2 * k + side + 1, :half])
                value = jnp.where(own_bit == side, *width_scaled) * hidden_in
                update_in[:, low + side * half : low + side * half + half] = value.astype(update_in.dtype)
        for own in (True, False):
            side = own_bit if own else 1 - own_bit
            start = pl.multiple_of(low + side * half, math.gcd(low, half))
            hidden_out = upright(lax.rsqrt(stat_row(factors, OUT_HIDDEN + 2 * k + side)[:, :half]))
            if half % 128 == 0:
                hidden_in = lax.rsqrt(stat_row(factors, IN_HIDDEN + 2 * k + side)[:, :half])
                value = own_in[k][...] if own else got_in[k][...].astype(jnp.float32)
                update_in[:, pl.ds(start, half)] = (value * width_in * hidden_in).astype(update_in.dtype)
            value = own_out[k][...] if own else got_out[k][...].astype(jnp.float32)
            update_out[pl.ds(start, half), :] = (value * hidden_out * width_out).astype(update_out.dtype)


def shards(tokens, cotangent, expert_ids, in_weight, out_weight, width_states, hidden_states):
    bf16, f32 = jnp.bfloat16, jnp.float32
    shape = jax.ShapeDtypeStruct
    experts = width_states.shape[1]
    tok_rows, width = tokens.shape
    capacity = 5 * tok_rows // (4 * experts)
    part_cap = capacity // 2
    places = lax.axis_size("expert")
    block_width = width // GROUP
    position = lax.axis_index("expert")
    expert = position // GROUP
    part = lax.axis_index("ffn") % 2
    bits = [position >> k & 1 for k in range(3)]
    bounds = set_bounds(in_weight.shape[2])
    halves = [(high - low) // 2 for low, high in bounds]
    sets = range(3)
    local_in = in_weight[0]
    local_out = out_weight[0]

    is_packed = all(half % 128 == 0 for half in halves) and block_width % 128 == 0
    if is_packed:
        kept_shapes = [shape((block_width, half), bf16) for half in halves]
        kept_shapes += [shape((half, block_width), bf16) for half in halves]
        packed_shapes = [shape((2 * half * block_width // 128, 128), bf16) for half in halves]
        copies = 6 + sum(half + block_width for half in halves) // 128
        cuts = call(
            functools.partial(cut_kernel, bounds), CUT_MIB, kept_shapes + packed_shapes, local_in, local_out,
            scratch=[pltpu.SemaphoreType.DMA((copies,))], whole=(0, 1),
        )
        got_weights = [swap(cuts[6 + k], MASKS[k]) for k in sets] * 2
    else:
        cuts = []
        for taken in range(2):
            at = [bounds[k][0] + (1 - bits[k] if taken else bits[k]) * halves[k] for k in sets]
            cuts += [lax.dynamic_slice_in_dim(local_in, at[k], halves[k], 1) for k in sets]
            cuts += [lax.dynamic_slice_in_dim(local_out, at[k], halves[k], 0) for k in sets]
        got_weights = [swap(cuts[6 + n], MASKS[n % 3]) for n in range(6)]

    route_ids = expert_ids[:, 0]
    onehot = (route_ids[:, None] == jnp.arange(experts, dtype=jnp.int32)[None, :]).astype(jnp.int32)
    before = jnp.cumsum(onehot, axis=0) - onehot
    slot_index = jnp.sum(before * onehot, axis=1) - part * part_cap
    valid = (slot_index >= 0) & (slot_index < part_cap)
    target = jnp.where(valid, route_ids * part_cap + slot_index, -1)
    select = (jnp.arange(experts * part_cap, dtype=jnp.int32)[:, None] == target[None, :]).astype(bf16)

    def route(values):
        routed = dot(select, values, 1, 0).astype(bf16)
        routed = routed.reshape(experts, part_cap, GROUP, block_width).transpose(0, 2, 1, 3)
        return routed.reshape(places, part_cap, block_width)

    routed = jnp.concatenate([route(tokens), route(cotangent)], axis=2)
    got = lax.all_to_all(routed, "expert", split_axis=0, concat_axis=0, tiled=True)
    got, got_weights = lax.optimization_barrier((got, got_weights))
    got = got.reshape(places // GROUP, GROUP, part_cap, 2 * block_width).transpose(1, 0, 2, 3)
    got = got.reshape(GROUP, -1, 2 * block_width)

    count = got.shape[1] * 4
    wide = 2 * block_width
    first_widths, second_widths = packed_widths(0, halves), packed_widths(1, halves)

    def shapes(rows, widths, dtype):
        return [shape((rows, width), dtype) for width in widths]

    def along_axes(values):
        return [swap(value, mask) for value, mask in zip(values, MASKS)]

    pairs = jnp.stack([swap(got, MASKS[k]) for k in sets])
    blocks = [(got, pairs), (swap(got, 1, "ffn"), swap(pairs, 1, "ffn"))]
    chains = range(2)
    row_shapes = [shape((count, wide), bf16)] * 6

    def sums(chain, side, out_shapes):
        kernel = functools.partial(sums_kernel, side, halves, is_packed)
        outs = call(
            kernel, 14, row_shapes + out_shapes, *blocks[chain], *cuts[:6], *got_weights,
            scratch=[pltpu.VMEM((6, count, wide), bf16), pltpu.SemaphoreType.DMA((6,))], whole_out=range(6),
        )
        return outs[:6], outs[6:]

    far_rows, received, near_rows, kept = [None] * 2, [None] * 2, [None] * 2, [None] * 2
    for c in chains:
        far_rows[c], sent = sums(c, 1, shapes(count, first_widths, bf16))
        received[c] = along_axes(sent)
    blocks, sent = lax.optimization_barrier((blocks, sent))
    for c in chains:
        near_rows[c], kept[c] = sums(c, 0, shapes(count, halves * 2, f32))
    kept = lax.optimization_barrier(kept)
    for c in chains:
        out_shapes = shapes(count // 2, halves * 2, f32) + shapes(count // 2, second_widths, bf16)
        outs = call(functools.partial(add_kernel, halves), 8, out_shapes, *kept[c], *received[c])
        kept[c], received[c] = outs[:6], along_axes(outs[6:])
    owns, nears, fars = [None] * 2, [None] * 2, [None] * 2
    for c in chains:
        out_shapes = shapes(count // 2, first_widths, bf16)
        owns[c] = call(functools.partial(act_kernel, halves), 8, out_shapes, *kept[c], *received[c])
        received[c] = along_axes(owns[c])
    for c in chains:
        out_shapes = shapes(count, second_widths, bf16)
        nears[c] = call(functools.partial(join_kernel, halves), 8, out_shapes, *owns[c], *received[c])
        fars[c] = along_axes(nears[c])

    def parts(near, far):
        return [value[n] for n in range(3) for chain in chains for value in (near[chain], far[chain])]

    token_rows = parts([rows[:3] for rows in near_rows], [rows[:3] for rows in far_rows])
    cotangent_rows = parts([rows[3:] for rows in near_rows], [rows[3:] for rows in far_rows])
    values = parts(nears, fars)
    buffers = [pltpu.VMEM((3, 4 * count, wide), bf16)]
    buffers += [pltpu.VMEM((4 * count, width), bf16) for width in second_widths]
    buffers += [pltpu.SemaphoreType.DMA((24,))]

    lanes = max(block_width, *halves)
    hidden_pick = lax.dynamic_index_in_dim(hidden_states, expert, 1, keepdims=False)
    sums_shape = (6, 8, wide)
    outs = call(
        functools.partial(grad_out_kernel, halves), 56,
        [shape((half, block_width), f32) for half in halves]
        + [shape((half, block_width), bf16) for half in halves]
        + [shape(sums_shape, f32)],
        *cotangent_rows, *values,
        scratch=buffers, whole=range(24), streamed_out=range(3),
    )
    out_own, out_sent, out_sums = outs[:3], outs[3:6], outs[6]
    got_out = along_axes(out_sent)
    outs = call(
        functools.partial(grad_in_kernel, halves), 56,
        [shape((block_width, half), f32) for half in halves]
        + [shape((block_width, half), bf16) for half in halves]
        + [shape((STAT_ROWS, lanes), f32)],
        *token_rows, *values, out_sums, hidden_pick[1:2],
        scratch=buffers + [pltpu.VMEM(sums_shape, f32)], whole=range(24), streamed_out=range(3),
    )
    in_own, in_sent, stats = outs[:3], outs[3:6], outs[6]
    got_in = along_axes(in_sent)

    width_pick = lax.dynamic_index_in_dim(width_states, expert, 1, keepdims=False)

    def padded(values):
        return jnp.pad(values, ((0, 0), (0, lanes - values.shape[1])), constant_values=1.0)

    prev = [padded(width_pick.reshape(2 * GROUP, block_width))]
    for which in range(2):
        for k in sets:
            low, high = bounds[k]
            prev.append(padded(hidden_pick[which, low:high].reshape(2, halves[k])))
    prev.append(jnp.ones((STAT_ROWS - TOTALS, lanes), f32))
    prev = jnp.concatenate(prev)

    def totals(values):
        values = values + swap(values, 1) + swap(values, 2) + swap(values, 3)
        if lax.axis_size("ffn") > 2:
            values = values + swap(values, 4)
            return values, ffn_total(values)
        ends = [(e, f) for e in range(places) for f in range(2)]

        def other(expert_mask, ffn_mask):
            moves = [(e * 2 + f, (e ^ expert_mask) * 2 + (f ^ ffn_mask)) for e, f in ends]
            return lax.ppermute(values, ("expert", "ffn"), moves)

        cube = values + swap(values, 4)
        return cube, cube + (other(0, 1) + other(4, 1))

    stats, got_out = lax.optimization_barrier((stats, got_out))
    group_sums, whole_sums = totals(stats)
    whole_sums, got_in = lax.optimization_barrier((whole_sums, got_in))
    factors, norms = call(
        norm_kernel, 52,
        [shape((STAT_ROWS, lanes), f32), shape((8, 128), f32)],
        prev, group_sums, whole_sums, *in_own, *in_sent, *out_own, *out_sent,
        streamed=range(3, 15),
    )
    norms = totals(norms)[1]
    update_in, update_out = call(
        functools.partial(final_kernel, bounds), 52,
        [shape(local_in.shape, bf16), shape(local_out.shape, bf16)],
        prev, factors, whole_sums, norms, *in_own, *out_own, *got_in, *got_out,
        streamed=range(4, 16), streamed_out=range(2),
    )
    return (update_in[None], update_out[None])


def solution(mesh):
    return jax.shard_map(
        shards,
        mesh=mesh,
        in_specs=(
            P("expert", None),
            P("expert", None),
            P("expert", None),
            P("expert", None, "ffn"),
            P("expert", "ffn", None),
            P(),
            P(None, None, "ffn"),
        ),
        out_specs=(P("expert", None, "ffn"), P("expert", "ffn", None)),
        check_vma=False,
    )
```

```python
import functools
import math

import jax
import jax.numpy as jnp
from jax import lax
from jax.experimental import pallas as pl
from jax.experimental.pallas import tpu as pltpu
from jax.sharding import PartitionSpec as P

D = 4096
FF = 5120
GROUP = 8


DECAY_RATE = 0.9
EPS_ONE = 1e-30
ROOT_COEF = math.sqrt(2.0 / math.pi)
CUBIC_COEF = 0.044715

MASKS = (1, 2, 4)

MIB = 1024 * 1024
CUT_MIB = 8


def swap(value, mask, axis="expert"):
    pairs = [(source, source ^ mask) for source in range(lax.axis_size(axis))]
    return lax.ppermute(value, axis, pairs)


def gelu_pair(inputs):
    inner = ROOT_COEF * (inputs + CUBIC_COEF * inputs * inputs * inputs)
    tangent = jnp.tanh(inner)
    act_value = 0.5 * inputs * (1.0 + tangent)
    act_slope = 0.5 * (1.0 + tangent) + 0.5 * inputs * (1.0 - tangent * tangent) * ROOT_COEF * (
        1.0 + 3.0 * CUBIC_COEF * inputs * inputs
    )
    return (act_value, act_slope)


def ffn_total(values):
    mask = 1
    while mask < lax.axis_size("ffn"):
        values = values + swap(values, mask, "ffn")
        mask *= 2
    return values


def set_bounds(hidden):
    unit = next(unit for unit in (256, 128, 2) if hidden % unit == 0 and hidden // unit >= 3)
    units = hidden // unit
    bounds, low = [], 0
    for k in range(3):
        high = low + (units // 3 + (k < units % 3)) * unit
        bounds.append((low, high))
        low = high
    return bounds


def dot(left, right, left_dim, right_dim):
    return lax.dot_general(
        left, right, (((left_dim,), (right_dim,)), ((), ())), preferred_element_type=jnp.float32
    )


def call(kernel, mib, out_shape, *operands, scratch=(), streamed=(), streamed_out=(), whole=()):
    def spec(value, n, blocks, refs):
        if n in refs:
            return pl.BlockSpec(memory_space=pltpu.HBM)
        if n in blocks:
            return pl.BlockSpec(value.shape, lambda: (0,) * len(value.shape))
        return pl.BlockSpec(memory_space=pltpu.VMEM)

    return pl.pallas_call(
        kernel,
        out_shape=out_shape,
        in_specs=[spec(value, n, streamed, whole) for n, value in enumerate(operands)],
        out_specs=[spec(value, n, streamed_out, ()) for n, value in enumerate(out_shape)],
        scratch_shapes=list(scratch),
        compiler_params=pltpu.CompilerParams(vmem_limit_bytes=mib * MIB),
    )(*operands)


def padded_width(half):
    return -(-half // 128) * 128


def packed_place(step, matrix, k, halves):
    axis = (k + 1 + (step + matrix) % 2) % 3
    return axis, padded_width(halves[(axis + 2 - step) % 3]) if matrix else 0


def packed_widths(step, halves):
    return [padded_width(halves[(axis + 2 - step) % 3]) + halves[(axis + 1 + step) % 3] for axis in range(3)]


def place_in_group():
    return lax.rem(lax.axis_index("expert"), GROUP)


def bit(place, k):
    return lax.rem(lax.div(place, 1 << k), 2)


def flipped(place, mask):
    for k in range(3):
        if mask >> k & 1:
            place = place + (1 - 2 * bit(place, k)) * (1 << k)
    return place


def partial_sum(rows, own_weight, got_weight, by_row):
    width = rows.shape[1] // 2
    contract = 1 if by_row else 0
    return dot(rows[:, :width], own_weight, 1, contract) + dot(rows[:, width:], got_weight, 1, contract)


def cut_kernel(bounds, weight_in, weight_out, *refs):
    kept_in, kept_out, packed, sems = refs[:3], refs[3:6], refs[6:9], refs[9]
    copies = []
    width = weight_in.shape[0]
    for k in range(3):
        low, half = bounds[k][0], (bounds[k][1] - bounds[k][0]) // 2
        side = bit(place_in_group(), k)
        kept = pl.ds(pl.multiple_of(low + side * half, 128), half)
        copies.append((weight_in.at[:, kept], kept_in[k], 3 * k))
        copies.append((weight_out.at[kept, :], kept_out[k], 3 * k + 1))
        start = low + (1 - side) * half
        at = 0
        for n in range(half // 128):
            part = pl.ds(pl.multiple_of(start + n * 128, 128), 128)
            copies.append((weight_in.at[:, part], packed[k].at[at : at + width], 3 * k + 2))
            at += width
        for n in range(width // 128):
            part = pl.ds(pl.multiple_of(start, 128), half)
            source = weight_out.at[part, n * 128 : n * 128 + 128]
            copies.append((source, packed[k].at[at : at + half], 3 * k + 2))
            at += half
    copies = [pltpu.make_async_copy(source, target, sems.at[n]) for n, (source, target, _) in enumerate(copies)]
    for copy in copies:
        copy.start()
    for copy in copies:
        copy.wait()


def got_weight(ref, by_row, half, width):
    at = half // 128 * width if by_row else 0
    rows = half if by_row else width
    blocks = (width if by_row else half) // 128
    return jnp.concatenate([ref[at + n * rows : at + (n + 1) * rows, :] for n in range(blocks)], axis=1)


def assemble(rows, start, own, pair, lanes, k, axis, side):
    count, width = own.shape[1], rows.shape[1] // 2
    first, second = 1 << axis, 1 << (3 - axis - k)
    for j in range(2):
        for l in range(2):
            chunk = flipped(place_in_group(), side * first + j * second + l * (1 << k))
            at = start + (j * 2 + l) * count
            rows[at : at + count, :width] = own[chunk, :, lanes]
            rows[at : at + count, width:] = pair[chunk, :, lanes]


def sums_kernel(side, halves, is_packed, *refs):
    own, pairs, own_weights, got_weights = refs[0], refs[1], refs[2:8], refs[8:14]
    sums_out, rows = refs[14:-1], refs[-1]
    width = own.shape[2] // 2
    for matrix in range(2):
        lanes = slice(matrix * width, (matrix + 1) * width)
        for k in range(3):
            n, half = 3 * matrix + k, halves[k]
            axis = packed_place(0, matrix, k, halves)[0]
            assemble(rows.at[n], 0, own, pairs.at[k], lanes, k, axis, side)
            by_row = matrix == 1
            got = got_weight(got_weights[n], by_row, half, width) if is_packed else got_weights[n][...]
            sums = partial_sum(rows[n], own_weights[n][...], got, by_row)
            if side:
                at = packed_place(0, matrix, k, halves)[1]
                sums_out[axis][:, at : at + half] = sums.astype(jnp.bfloat16)
            else:
                sums_out[n][...] = sums


def add_kernel(halves, *refs):
    kept, received, total_out, sent_out = refs[:6], refs[6:9], refs[9:15], refs[15:18]
    for matrix in range(2):
        for k in range(3):
            n, half = 3 * matrix + k, halves[k]
            middle = kept[n].shape[0] // 2
            axis, at = packed_place(0, matrix, k, halves)
            total = kept[n][...] + received[axis][:, at : at + half].astype(jnp.float32)
            total_out[n][...] = total[:middle]
            axis, at = packed_place(1, matrix, k, halves)
            sent_out[axis][:, at : at + half] = total[middle:].astype(jnp.bfloat16)


def act_kernel(halves, *refs):
    kept, received, outs = refs[:6], refs[6:9], refs[9:12]
    for k in range(3):
        values = []
        for matrix in range(2):
            axis, at = packed_place(1, matrix, k, halves)
            values.append(kept[3 * matrix + k][...] + received[axis][:, at : at + halves[k]].astype(jnp.float32))
        act_value, act_slope = gelu_pair(values[0])
        for matrix, value in enumerate((act_value, values[1] * act_slope)):
            axis, at = packed_place(0, matrix, k, halves)
            outs[axis][:, at : at + halves[k]] = value.astype(jnp.bfloat16)


def join_kernel(halves, *refs):
    own, got, outs = refs[:3], refs[3:6], refs[6:9]
    for matrix in range(2):
        for k in range(3):
            source, start = packed_place(0, matrix, k, halves)
            axis, at = packed_place(1, matrix, k, halves)
            rows = own[source].shape[0]
            outs[axis][:rows, at : at + halves[k]] = own[source][:, start : start + halves[k]]
            outs[axis][rows:, at : at + halves[k]] = got[source][:, start : start + halves[k]]


def gradients(hidden_first, halves, blocks, values, buffers, own_out, sent_out, sums_out):
    own_buffer, pair_buffer, rows, value_buffers, sems = buffers[0], buffers[1], buffers[2], buffers[3:6], buffers[6]
    matrix = 0 if hidden_first else 1
    part = rows.shape[0] // 4
    width = rows.shape[1] // 2
    lanes = slice(width, 2 * width) if hidden_first else slice(0, width)
    set_copies = []
    for k in range(3):
        axis, at = packed_place(1, matrix, k, halves)
        parts, buffer = values[4 * axis : 4 * axis + 4], value_buffers[axis]
        if all(half % 128 == 0 for half in halves):
            parts = [value.at[:, at : at + halves[k]] for value in parts]
            buffer = buffer.at[:, at : at + halves[k]]
        moves = [(parts[i], buffer.at[pl.ds(i * part, part)]) for i in range(4)]
        for chain in range(2):
            moves.append((blocks[2 * chain + 1].at[k, :, :, lanes], pair_buffer.at[chain, k]))
            if k == 0:
                moves.append((blocks[2 * chain].at[:, :, lanes], own_buffer.at[chain]))
        copies = [pltpu.make_async_copy(*move, sems.at[k * 8 + n]) for n, move in enumerate(moves)]
        for copy in copies:
            copy.start()
        set_copies.append(copies)
    for k in range(3):
        for copy in set_copies[k]:
            copy.wait()
        axis = packed_place(0, 1 - matrix, k, halves)[0]
        for chain in range(2):
            for side in range(2):
                start = (2 * chain + side) * part
                assemble(rows, start, own_buffer.at[chain], pair_buffer.at[chain, k], slice(None), k, axis, side)
        axis, at = packed_place(1, matrix, k, halves)
        value = value_buffers[axis][:, at : at + halves[k]]
        if hidden_first:
            grad = dot(value, rows[...], 0, 0)
            own_out[k][...] = grad[:, :width]
            sent_out[k][...] = grad[:, width:].astype(jnp.bfloat16)
        else:
            grad = dot(rows[...], value, 0, 0)
            own_out[k][...] = grad[:width]
            sent_out[k][...] = grad[width:].astype(jnp.bfloat16)
        square = grad * grad + EPS_ONE
        down = jnp.sum(square, axis=0, keepdims=True)
        down = jnp.broadcast_to(down, (8, square.shape[1]))
        if square.shape[1] % 128 == 0:
            square = sum(square[:, n : n + 128] for n in range(0, square.shape[1], 128))
        across = dot(jnp.ones((8, square.shape[1]), jnp.float32), square, 1, 1)
        by_width, by_hidden = (down, across) if hidden_first else (across, down)
        sums_out[k] = by_width
        sums_out[3 + k] = jnp.zeros(sums_out.shape[1:], jnp.float32)
        sums_out[3 + k, :, : by_hidden.shape[1]] = by_hidden


def grad_out_kernel(halves, *refs):
    blocks, values, outs, buffers = refs[:4], refs[4:16], refs[16:23], refs[23:]
    gradients(True, halves, blocks, values, buffers, outs[:3], outs[3:6], outs[6])


def grad_in_kernel(halves, *refs):
    blocks, values, other_sums, hidden_prev, outs, buffers = (
        refs[:4], refs[4:16], refs[16], refs[17], refs[18:25], refs[25:]
    )
    sums = buffers[-1]
    gradients(False, halves, blocks, values, buffers[:-1], outs[:3], outs[3:6], sums)
    collect(hidden_prev, (sums, other_sums), outs[6])


IN_WIDTH, OUT_WIDTH, IN_HIDDEN, OUT_HIDDEN, TOTALS, STAT_ROWS = 0, 8, 16, 22, 28, 32


def collect(hidden_prev, all_sums, stats_out):
    place = place_in_group()
    stats_out[...] = jnp.zeros_like(stats_out)
    lanes = stats_out.shape[1]
    for which in range(2):
        sums = all_sums[which]
        width_row, hidden_row = (IN_WIDTH, OUT_WIDTH)[which], (IN_HIDDEN, OUT_HIDDEN)[which]
        width = sums.shape[2] // 2
        stats_out[pl.ds(width_row + place, 1), :] = sum(sums[k, 0:1, :width] for k in range(3))
        total = 0.0
        for k in range(3):
            stats_out[pl.ds(width_row + flipped(place, 1 << k), 1), :] = sums[k, 0:1, width:]
            row = sums[3 + k, 0:1, :lanes]
            stats_out[pl.ds(hidden_row + 2 * k + bit(place, k), 1), :] = row
            total = total + jnp.sum(row, axis=1, keepdims=True)
        stats_out[TOTALS + which : TOTALS + which + 1, :] = jnp.broadcast_to(total, (1, lanes))
    previous = jnp.sum(hidden_prev[...], axis=1, keepdims=True)
    stats_out[TOTALS + 2 : TOTALS + 3, :] = jnp.broadcast_to(previous, (1, lanes))


def stat_row(stats_ref, index):
    return stats_ref[pl.ds(index, 1), :]


def upright(row):
    return jnp.transpose(jnp.broadcast_to(row, (8, row.shape[1])))[:, 0:1]


def norm_kernel(prev, group_sums, whole_sums, *refs):
    own_in, sent_in, own_out, sent_out = refs[:3], refs[3:6], refs[6:9], refs[9:12]
    factors_out, norms_out = refs[12], refs[13]
    place = place_in_group()
    width = own_in[0].shape[0]
    row = lax.broadcasted_iota(jnp.int32, prev.shape, 0)
    by_width = row < IN_HIDDEN
    mean = jnp.where(by_width, whole_sums[...] / FF, group_sums[...] / D)
    factors_out[...] = DECAY_RATE * prev[...] + (1.0 - DECAY_RATE) * mean
    norm_in, norm_out = 0.0, 0.0
    for k in range(3):
        half = own_in[k].shape[1]
        partner = flipped(place, 1 << k)
        own_row = stat_row(factors_out, IN_WIDTH + place)[:, :width]
        pair_row = stat_row(factors_out, IN_WIDTH + partner)[:, :width]
        hidden_row = stat_row(factors_out, IN_HIDDEN + 2 * k + bit(place, k))[:, :half]
        sent = sent_in[k][...].astype(jnp.float32)
        down = jnp.sum(own_in[k][...] * own_in[k][...] * upright(1.0 / own_row), axis=0, keepdims=True)
        down = down + jnp.sum(sent * sent * upright(1.0 / pair_row), axis=0, keepdims=True)
        norm_in = norm_in + jnp.sum(down / hidden_row, axis=1, keepdims=True)
        own_row = stat_row(factors_out, OUT_WIDTH + place)[:, :width]
        pair_row = stat_row(factors_out, OUT_WIDTH + partner)[:, :width]
        hidden_row = stat_row(factors_out, OUT_HIDDEN + 2 * k + bit(place, k))[:, :half]
        inverse = upright(1.0 / hidden_row)
        sent = sent_out[k][...].astype(jnp.float32)
        down = jnp.sum(own_out[k][...] * own_out[k][...] * inverse, axis=0, keepdims=True) / own_row
        down = down + jnp.sum(sent * sent * inverse, axis=0, keepdims=True) / pair_row
        norm_out = norm_out + jnp.sum(down, axis=1, keepdims=True)
    row = lax.broadcasted_iota(jnp.int32, norms_out.shape, 0)
    norms_out[...] = jnp.where(row == 0, norm_in, norm_out)


def final_kernel(bounds, prev, factors, whole_sums, norms, *refs):
    own_in, own_out, got_in, got_out = refs[:3], refs[3:6], refs[6:9], refs[9:12]
    update_in, update_out = refs[12:]
    place = place_in_group()
    width = update_in.shape[0]
    count = float(D) * float(FF)
    mean_in = DECAY_RATE * jnp.mean(prev[IN_WIDTH : IN_WIDTH + 8, :width], keepdims=True)
    mean_in = mean_in + (1.0 - DECAY_RATE) * whole_sums[TOTALS : TOTALS + 1, 0:1] / count
    mean_out = DECAY_RATE * whole_sums[TOTALS + 2 : TOTALS + 3, 0:1] / (FF * GROUP)
    mean_out = mean_out + (1.0 - DECAY_RATE) * whole_sums[TOTALS + 1 : TOTALS + 2, 0:1] / count
    factor_in = jnp.sqrt(mean_in) / jnp.maximum(1.0, jnp.sqrt(mean_in * norms[0:1, 0:1] / count))
    factor_out = jnp.sqrt(mean_out) / jnp.maximum(1.0, jnp.sqrt(mean_out * norms[1:2, 0:1] / count))
    width_in = upright(lax.rsqrt(stat_row(factors, IN_WIDTH + place)[:, :width]) * factor_in)
    width_out = lax.rsqrt(stat_row(factors, OUT_WIDTH + place)[:, :width]) * factor_out
    for k in range(3):
        low, half = bounds[k][0], (bounds[k][1] - bounds[k][0]) // 2
        own_bit = bit(place, k)
        if half % 128:
            width_scaled = (own_in[k][...] * width_in, got_in[k][...].astype(jnp.float32) * width_in)
            for side in range(2):
                hidden_in = lax.rsqrt(factors[IN_HIDDEN + 2 * k + side : IN_HIDDEN + 2 * k + side + 1, :half])
                value = jnp.where(own_bit == side, *width_scaled) * hidden_in
                update_in[:, low + side * half : low + side * half + half] = value.astype(update_in.dtype)
        for own in (True, False):
            side = own_bit if own else 1 - own_bit
            start = pl.multiple_of(low + side * half, math.gcd(low, half))
            hidden_out = upright(lax.rsqrt(stat_row(factors, OUT_HIDDEN + 2 * k + side)[:, :half]))
            if half % 128 == 0:
                hidden_in = lax.rsqrt(stat_row(factors, IN_HIDDEN + 2 * k + side)[:, :half])
                value = own_in[k][...] if own else got_in[k][...].astype(jnp.float32)
                update_in[:, pl.ds(start, half)] = (value * width_in * hidden_in).astype(update_in.dtype)
            value = own_out[k][...] if own else got_out[k][...].astype(jnp.float32)
            update_out[pl.ds(start, half), :] = (value * hidden_out * width_out).astype(update_out.dtype)


def shards(tokens, cotangent, expert_ids, in_weight, out_weight, width_states, hidden_states):
    bf16, f32 = jnp.bfloat16, jnp.float32
    shape = jax.ShapeDtypeStruct
    experts = width_states.shape[1]
    tok_rows, width = tokens.shape
    capacity = 5 * tok_rows // (4 * experts)
    part_cap = capacity // 2
    places = lax.axis_size("expert")
    block_width = width // GROUP
    position = lax.axis_index("expert")
    expert = position // GROUP
    part = lax.axis_index("ffn") % 2
    bits = [position >> k & 1 for k in range(3)]
    bounds = set_bounds(in_weight.shape[2])
    halves = [(high - low) // 2 for low, high in bounds]
    sets = range(3)
    local_in = in_weight[0]
    local_out = out_weight[0]

    is_packed = all(half % 128 == 0 for half in halves) and block_width % 128 == 0
    if is_packed:
        kept_shapes = [shape((block_width, half), bf16) for half in halves]
        kept_shapes += [shape((half, block_width), bf16) for half in halves]
        packed_shapes = [shape((2 * half * block_width // 128, 128), bf16) for half in halves]
        copies = 6 + sum(half + block_width for half in halves) // 128
        cuts = call(
            functools.partial(cut_kernel, bounds), CUT_MIB, kept_shapes + packed_shapes, local_in, local_out,
            scratch=[pltpu.SemaphoreType.DMA((copies,))], whole=(0, 1),
        )
        got_weights = [swap(cuts[6 + k], MASKS[k]) for k in sets] * 2
    else:
        cuts = []
        for taken in range(2):
            at = [bounds[k][0] + (1 - bits[k] if taken else bits[k]) * halves[k] for k in sets]
            cuts += [lax.dynamic_slice_in_dim(local_in, at[k], halves[k], 1) for k in sets]
            cuts += [lax.dynamic_slice_in_dim(local_out, at[k], halves[k], 0) for k in sets]
        got_weights = [swap(cuts[6 + n], MASKS[n % 3]) for n in range(6)]

    route_ids = expert_ids[:, 0]
    onehot = (route_ids[:, None] == jnp.arange(experts, dtype=jnp.int32)[None, :]).astype(jnp.int32)
    before = jnp.cumsum(onehot, axis=0) - onehot
    slot_index = jnp.sum(before * onehot, axis=1) - part * part_cap
    valid = (slot_index >= 0) & (slot_index < part_cap)
    target = jnp.where(valid, route_ids * part_cap + slot_index, -1)
    select = (jnp.arange(experts * part_cap, dtype=jnp.int32)[:, None] == target[None, :]).astype(bf16)

    def route(values):
        routed = dot(select, values, 1, 0).astype(bf16)
        routed = routed.reshape(experts, part_cap, GROUP, block_width).transpose(0, 2, 1, 3)
        return routed.reshape(places, part_cap, block_width)

    routed = jnp.concatenate([route(tokens), route(cotangent)], axis=2)
    got = lax.all_to_all(routed, "expert", split_axis=0, concat_axis=0, tiled=True)
    got, got_weights = lax.optimization_barrier((got, got_weights))
    got = got.reshape(places // GROUP, GROUP, part_cap, 2 * block_width).transpose(1, 0, 2, 3)
    got = got.reshape(GROUP, -1, 2 * block_width)

    count = got.shape[1] * 4
    wide = 2 * block_width
    first_widths, second_widths = packed_widths(0, halves), packed_widths(1, halves)

    def shapes(rows, widths, dtype):
        return [shape((rows, width), dtype) for width in widths]

    def along_axes(values):
        return [swap(value, mask) for value, mask in zip(values, MASKS)]

    pairs = jnp.stack([swap(got, MASKS[k]) for k in sets])
    blocks = [(got, pairs), (swap(got, 1, "ffn"), swap(pairs, 1, "ffn"))]
    chains = range(2)
    def sums(chain, side, out_shapes):
        return call(
            functools.partial(sums_kernel, side, halves, is_packed), 14,
            out_shapes, *blocks[chain], *cuts[:6], *got_weights,
            scratch=[pltpu.VMEM((6, count, wide), bf16)],
        )

    sent = [sums(c, 1, shapes(count, first_widths, bf16)) for c in chains]
    received = [along_axes(values) for values in sent]
    blocks, sent = lax.optimization_barrier((blocks, sent))
    kept = lax.optimization_barrier([sums(c, 0, shapes(count, halves * 2, f32)) for c in chains])
    for c in chains:
        out_shapes = shapes(count // 2, halves * 2, f32) + shapes(count // 2, second_widths, bf16)
        outs = call(functools.partial(add_kernel, halves), 8, out_shapes, *kept[c], *received[c])
        kept[c], received[c] = outs[:6], along_axes(outs[6:])
    owns, nears, fars = [None] * 2, [None] * 2, [None] * 2
    for c in chains:
        out_shapes = shapes(count // 2, first_widths, bf16)
        owns[c] = call(functools.partial(act_kernel, halves), 8, out_shapes, *kept[c], *received[c])
        received[c] = along_axes(owns[c])
    for c in chains:
        out_shapes = shapes(count, second_widths, bf16)
        nears[c] = call(functools.partial(join_kernel, halves), 8, out_shapes, *owns[c], *received[c])
        fars[c] = along_axes(nears[c])

    def parts(near, far):
        return [value[n] for n in range(3) for chain in chains for value in (near[chain], far[chain])]

    values = parts(nears, fars)
    all_blocks = [value for chain in chains for value in blocks[chain]]
    chunks = got.shape[:2] + (block_width,)
    buffers = [pltpu.VMEM((2, *chunks), bf16), pltpu.VMEM((2, 3, *chunks), bf16), pltpu.VMEM((4 * count, wide), bf16)]
    buffers += [pltpu.VMEM((4 * count, width), bf16) for width in second_widths]
    buffers += [pltpu.SemaphoreType.DMA((24,))]

    lanes = max(block_width, *halves)
    hidden_pick = lax.dynamic_index_in_dim(hidden_states, expert, 1, keepdims=False)
    sums_shape = (6, 8, wide)
    outs = call(
        functools.partial(grad_out_kernel, halves), 56,
        [shape((half, block_width), f32) for half in halves]
        + [shape((half, block_width), bf16) for half in halves]
        + [shape(sums_shape, f32)],
        *all_blocks, *values,
        scratch=buffers, whole=range(16), streamed_out=range(3),
    )
    out_own, out_sent, out_sums = outs[:3], outs[3:6], outs[6]
    got_out = along_axes(out_sent)
    outs = call(
        functools.partial(grad_in_kernel, halves), 56,
        [shape((block_width, half), f32) for half in halves]
        + [shape((block_width, half), bf16) for half in halves]
        + [shape((STAT_ROWS, lanes), f32)],
        *all_blocks, *values, out_sums, hidden_pick[1:2],
        scratch=buffers + [pltpu.VMEM(sums_shape, f32)], whole=range(16), streamed_out=range(3),
    )
    in_own, in_sent, stats = outs[:3], outs[3:6], outs[6]
    got_in = along_axes(in_sent)

    width_pick = lax.dynamic_index_in_dim(width_states, expert, 1, keepdims=False)

    def padded(values):
        return jnp.pad(values, ((0, 0), (0, lanes - values.shape[1])), constant_values=1.0)

    prev = [padded(width_pick.reshape(2 * GROUP, block_width))]
    for which in range(2):
        for k in sets:
            low, high = bounds[k]
            prev.append(padded(hidden_pick[which, low:high].reshape(2, halves[k])))
    prev.append(jnp.ones((STAT_ROWS - TOTALS, lanes), f32))
    prev = jnp.concatenate(prev)

    def totals(values):
        values = values + swap(values, 1) + swap(values, 2) + swap(values, 3)
        if lax.axis_size("ffn") > 2:
            values = values + swap(values, 4)
            return values, ffn_total(values)
        ends = [(e, f) for e in range(places) for f in range(2)]

        def other(expert_mask, ffn_mask):
            moves = [(e * 2 + f, (e ^ expert_mask) * 2 + (f ^ ffn_mask)) for e, f in ends]
            return lax.ppermute(values, ("expert", "ffn"), moves)

        cube = values + swap(values, 4)
        return cube, cube + (other(0, 1) + other(4, 1))

    stats, got_out = lax.optimization_barrier((stats, got_out))
    group_sums, whole_sums = totals(stats)
    whole_sums, got_in = lax.optimization_barrier((whole_sums, got_in))
    factors, norms = call(
        norm_kernel, 52,
        [shape((STAT_ROWS, lanes), f32), shape((8, 128), f32)],
        prev, group_sums, whole_sums, *in_own, *in_sent, *out_own, *out_sent,
        streamed=range(3, 15),
    )
    norms = totals(norms)[1]
    update_in, update_out = call(
        functools.partial(final_kernel, bounds), 52,
        [shape(local_in.shape, bf16), shape(local_out.shape, bf16)],
        prev, factors, whole_sums, norms, *in_own, *out_own, *got_in, *got_out,
        streamed=range(4, 16), streamed_out=range(2),
    )
    return (update_in[None], update_out[None])


def solution(mesh):
    return jax.shard_map(
        shards,
        mesh=mesh,
        in_specs=(
            P("expert", None),
            P("expert", None),
            P("expert", None),
            P("expert", None, "ffn"),
            P("expert", "ffn", None),
            P(),
            P(None, None, "ffn"),
        ),
        out_specs=(P("expert", None, "ffn"), P("expert", "ffn", None)),
        check_vma=False,
    )
```

```python
import functools
import math

import jax
import jax.numpy as jnp
from jax import lax
from jax.experimental import pallas as pl
from jax.experimental.pallas import tpu as pltpu
from jax.sharding import PartitionSpec as P

D = 4096
FF = 5120
GROUP = 8


DECAY_RATE = 0.9
EPS_ONE = 1e-30
ROOT_COEF = math.sqrt(2.0 / math.pi)
CUBIC_COEF = 0.044715

MASKS = (1, 2, 4)

MIB = 1024 * 1024
CUT_MIB = 8


def swap(value, mask, axis="expert"):
    pairs = [(source, source ^ mask) for source in range(lax.axis_size(axis))]
    return lax.ppermute(value, axis, pairs)


def gelu_pair(inputs):
    inner = ROOT_COEF * (inputs + CUBIC_COEF * inputs * inputs * inputs)
    tangent = jnp.tanh(inner)
    act_value = 0.5 * inputs * (1.0 + tangent)
    act_slope = 0.5 * (1.0 + tangent) + 0.5 * inputs * (1.0 - tangent * tangent) * ROOT_COEF * (
        1.0 + 3.0 * CUBIC_COEF * inputs * inputs
    )
    return (act_value, act_slope)


def ffn_total(values):
    mask = 1
    while mask < lax.axis_size("ffn"):
        values = values + swap(values, mask, "ffn")
        mask *= 2
    return values


def set_bounds(hidden):
    unit = next(unit for unit in (256, 128, 2) if hidden % unit == 0 and hidden // unit >= 3)
    units = hidden // unit
    bounds, low = [], 0
    for k in range(3):
        high = low + (units // 3 + (k < units % 3)) * unit
        bounds.append((low, high))
        low = high
    return bounds


def dot(left, right, left_dim, right_dim):
    return lax.dot_general(
        left, right, (((left_dim,), (right_dim,)), ((), ())), preferred_element_type=jnp.float32
    )


def call(kernel, mib, out_shape, *operands, scratch=(), streamed=(), streamed_out=(), whole=()):
    def spec(value, n, blocks, refs):
        if n in refs:
            return pl.BlockSpec(memory_space=pltpu.HBM)
        if n in blocks:
            return pl.BlockSpec(value.shape, lambda: (0,) * len(value.shape))
        return pl.BlockSpec(memory_space=pltpu.VMEM)

    return pl.pallas_call(
        kernel,
        out_shape=out_shape,
        in_specs=[spec(value, n, streamed, whole) for n, value in enumerate(operands)],
        out_specs=[spec(value, n, streamed_out, ()) for n, value in enumerate(out_shape)],
        scratch_shapes=list(scratch),
        compiler_params=pltpu.CompilerParams(vmem_limit_bytes=mib * MIB),
    )(*operands)


def padded_width(half):
    return -(-half // 128) * 128


def packed_place(step, matrix, k, halves):
    axis = (k + 1 + (step + matrix) % 2) % 3
    return axis, padded_width(halves[(axis + 2 - step) % 3]) if matrix else 0


def packed_widths(step, halves):
    return [padded_width(halves[(axis + 2 - step) % 3]) + halves[(axis + 1 + step) % 3] for axis in range(3)]


def place_in_group():
    return lax.rem(lax.axis_index("expert"), GROUP)


def bit(place, k):
    return lax.rem(lax.div(place, 1 << k), 2)


def flipped(place, mask):
    for k in range(3):
        if mask >> k & 1:
            place = place + (1 - 2 * bit(place, k)) * (1 << k)
    return place


def partial_sum(rows, own_weight, got_weight, by_row):
    width = rows.shape[1] // 2
    contract = 1 if by_row else 0
    return dot(rows[:, :width], own_weight, 1, contract) + dot(rows[:, width:], got_weight, 1, contract)


def route_kernel(part_cap, ids, tokens, cotangent, out):
    rows, experts, groups = ids.shape[0], out.shape[0], out.shape[1]
    width = out.shape[3] // 2
    part = lax.rem(lax.axis_index("ffn"), 2)
    onehot = lax.broadcasted_iota(jnp.int32, (rows, 128), 1) == ids[...]
    earlier = lax.broadcasted_iota(jnp.int32, (rows, rows), 0) > lax.broadcasted_iota(jnp.int32, (rows, rows), 1)
    before = dot(earlier.astype(jnp.float32), onehot.astype(jnp.float32), 1, 0)
    slot = jnp.sum(jnp.where(onehot, before, 0.0), axis=1, keepdims=True).astype(jnp.int32) - part * part_cap
    target = jnp.where((slot >= 0) & (slot < part_cap), ids[...] * part_cap + slot, -1)
    select = lax.broadcasted_iota(jnp.int32, (rows, experts * part_cap), 1) == target
    select = select.astype(jnp.float32).astype(jnp.bfloat16)
    for n, values in enumerate((tokens, cotangent)):
        routed = dot(select, values[...], 0, 0)
        for e in range(experts):
            mine = routed[e * part_cap : (e + 1) * part_cap].astype(jnp.bfloat16)
            for b in range(groups):
                out[e, b, :, n * width : (n + 1) * width] = mine[:, b * width : (b + 1) * width]


def cut_kernel(bounds, weight_in, weight_out, *refs):
    kept_in, kept_out, packed, sems = refs[:3], refs[3:6], refs[6:9], refs[9]
    copies = []
    width = weight_in.shape[0]
    for k in range(3):
        low, half = bounds[k][0], (bounds[k][1] - bounds[k][0]) // 2
        side = bit(place_in_group(), k)
        kept = pl.ds(pl.multiple_of(low + side * half, 128), half)
        copies.append((weight_in.at[:, kept], kept_in[k], 3 * k))
        copies.append((weight_out.at[kept, :], kept_out[k], 3 * k + 1))
        start = low + (1 - side) * half
        at = 0
        for n in range(half // 128):
            part = pl.ds(pl.multiple_of(start + n * 128, 128), 128)
            copies.append((weight_in.at[:, part], packed[k].at[at : at + width], 3 * k + 2))
            at += width
        for n in range(width // 128):
            part = pl.ds(pl.multiple_of(start, 128), half)
            source = weight_out.at[part, n * 128 : n * 128 + 128]
            copies.append((source, packed[k].at[at : at + half], 3 * k + 2))
            at += half
    copies = [pltpu.make_async_copy(source, target, sems.at[n]) for n, (source, target, _) in enumerate(copies)]
    for copy in copies:
        copy.start()
    for copy in copies:
        copy.wait()


def got_weight(ref, by_row, half, width):
    at = half // 128 * width if by_row else 0
    rows = half if by_row else width
    blocks = (width if by_row else half) // 128
    return jnp.concatenate([ref[at + n * rows : at + (n + 1) * rows, :] for n in range(blocks)], axis=1)


def assemble(rows, start, own, pair, lanes, k, axis, side):
    count, width = own.shape[1], rows.shape[1] // 2
    first, second = 1 << axis, 1 << (3 - axis - k)
    for j in range(2):
        for l in range(2):
            chunk = flipped(place_in_group(), side * first + j * second + l * (1 << k))
            at = start + (j * 2 + l) * count
            rows[at : at + count, :width] = own[chunk, :, lanes]
            rows[at : at + count, width:] = pair[chunk, :, lanes]


def sums_kernel(side, halves, is_packed, *refs):
    own, pairs, own_weights, got_weights = refs[0], refs[1], refs[2:8], refs[8:14]
    sums_out, rows = refs[14:-1], refs[-1]
    width = own.shape[2] // 2
    for matrix in range(2):
        lanes = slice(matrix * width, (matrix + 1) * width)
        for k in range(3):
            n, half = 3 * matrix + k, halves[k]
            axis = packed_place(0, matrix, k, halves)[0]
            assemble(rows.at[n], 0, own, pairs.at[k], lanes, k, axis, side)
            by_row = matrix == 1
            got = got_weight(got_weights[n], by_row, half, width) if is_packed else got_weights[n][...]
            sums = partial_sum(rows[n], own_weights[n][...], got, by_row)
            if side:
                at = packed_place(0, matrix, k, halves)[1]
                sums_out[axis][:, at : at + half] = sums.astype(jnp.bfloat16)
            else:
                sums_out[n][...] = sums


def add_kernel(halves, *refs):
    kept, received, total_out, sent_out = refs[:6], refs[6:9], refs[9:15], refs[15:18]
    for matrix in range(2):
        for k in range(3):
            n, half = 3 * matrix + k, halves[k]
            middle = kept[n].shape[0] // 2
            axis, at = packed_place(0, matrix, k, halves)
            total = kept[n][...] + received[axis][:, at : at + half].astype(jnp.float32)
            total_out[n][...] = total[:middle]
            axis, at = packed_place(1, matrix, k, halves)
            sent_out[axis][:, at : at + half] = total[middle:].astype(jnp.bfloat16)


def act_kernel(halves, *refs):
    kept, received, outs = refs[:6], refs[6:9], refs[9:12]
    for k in range(3):
        values = []
        for matrix in range(2):
            axis, at = packed_place(1, matrix, k, halves)
            values.append(kept[3 * matrix + k][...] + received[axis][:, at : at + halves[k]].astype(jnp.float32))
        act_value, act_slope = gelu_pair(values[0])
        for matrix, value in enumerate((act_value, values[1] * act_slope)):
            axis, at = packed_place(0, matrix, k, halves)
            outs[axis][:, at : at + halves[k]] = value.astype(jnp.bfloat16)


def join_kernel(halves, *refs):
    own, got, outs = refs[:3], refs[3:6], refs[6:9]
    for matrix in range(2):
        for k in range(3):
            source, start = packed_place(0, matrix, k, halves)
            axis, at = packed_place(1, matrix, k, halves)
            rows = own[source].shape[0]
            outs[axis][:rows, at : at + halves[k]] = own[source][:, start : start + halves[k]]
            outs[axis][rows:, at : at + halves[k]] = got[source][:, start : start + halves[k]]


def gradients(hidden_first, halves, blocks, values, buffers, own_out, sent_out, sums_out):
    own_buffer, pair_buffer, rows, value_buffers, sems = buffers[0], buffers[1], buffers[2], buffers[3:6], buffers[6]
    matrix = 0 if hidden_first else 1
    part = rows.shape[0] // 4
    width = rows.shape[1] // 2
    lanes = slice(width, 2 * width) if hidden_first else slice(0, width)
    set_copies = []
    for k in range(3):
        axis, at = packed_place(1, matrix, k, halves)
        parts, buffer = values[4 * axis : 4 * axis + 4], value_buffers[axis]
        if all(half % 128 == 0 for half in halves):
            parts = [value.at[:, at : at + halves[k]] for value in parts]
            buffer = buffer.at[:, at : at + halves[k]]
        moves = [(parts[i], buffer.at[pl.ds(i * part, part)]) for i in range(4)]
        for chain in range(2):
            moves.append((blocks[2 * chain + 1].at[k, :, :, lanes], pair_buffer.at[chain, k]))
            if k == 0:
                moves.append((blocks[2 * chain].at[:, :, lanes], own_buffer.at[chain]))
        copies = [pltpu.make_async_copy(*move, sems.at[k * 8 + n]) for n, move in enumerate(moves)]
        for copy in copies:
            copy.start()
        set_copies.append(copies)
    for k in range(3):
        for copy in set_copies[k]:
            copy.wait()
        axis = packed_place(0, 1 - matrix, k, halves)[0]
        for chain in range(2):
            for side in range(2):
                start = (2 * chain + side) * part
                assemble(rows, start, own_buffer.at[chain], pair_buffer.at[chain, k], slice(None), k, axis, side)
        axis, at = packed_place(1, matrix, k, halves)
        value = value_buffers[axis][:, at : at + halves[k]]
        if hidden_first:
            grad = dot(value, rows[...], 0, 0)
            own_out[k][...] = grad[:, :width]
            sent_out[k][...] = grad[:, width:].astype(jnp.bfloat16)
        else:
            grad = dot(rows[...], value, 0, 0)
            own_out[k][...] = grad[:width]
            sent_out[k][...] = grad[width:].astype(jnp.bfloat16)
        square = grad * grad + EPS_ONE
        down = jnp.sum(square, axis=0, keepdims=True)
        down = jnp.broadcast_to(down, (8, square.shape[1]))
        if square.shape[1] % 128 == 0:
            square = sum(square[:, n : n + 128] for n in range(0, square.shape[1], 128))
        across = dot(jnp.ones((8, square.shape[1]), jnp.float32), square, 1, 1)
        by_width, by_hidden = (down, across) if hidden_first else (across, down)
        sums_out[k] = by_width
        sums_out[3 + k] = jnp.zeros(sums_out.shape[1:], jnp.float32)
        sums_out[3 + k, :, : by_hidden.shape[1]] = by_hidden


def grad_out_kernel(halves, *refs):
    blocks, values, outs, buffers = refs[:4], refs[4:16], refs[16:23], refs[23:]
    gradients(True, halves, blocks, values, buffers, outs[:3], outs[3:6], outs[6])


def grad_in_kernel(halves, *refs):
    blocks, values, other_sums, hidden_prev, outs, buffers = (
        refs[:4], refs[4:16], refs[16], refs[17], refs[18:25], refs[25:]
    )
    sums = buffers[-1]
    gradients(False, halves, blocks, values, buffers[:-1], outs[:3], outs[3:6], sums)
    collect(hidden_prev, (sums, other_sums), outs[6])


IN_WIDTH, OUT_WIDTH, IN_HIDDEN, OUT_HIDDEN, TOTALS, STAT_ROWS = 0, 8, 16, 22, 28, 32


def collect(hidden_prev, all_sums, stats_out):
    place = place_in_group()
    stats_out[...] = jnp.zeros_like(stats_out)
    lanes = stats_out.shape[1]
    for which in range(2):
        sums = all_sums[which]
        width_row, hidden_row = (IN_WIDTH, OUT_WIDTH)[which], (IN_HIDDEN, OUT_HIDDEN)[which]
        width = sums.shape[2] // 2
        stats_out[pl.ds(width_row + place, 1), :] = sum(sums[k, 0:1, :width] for k in range(3))
        total = 0.0
        for k in range(3):
            stats_out[pl.ds(width_row + flipped(place, 1 << k), 1), :] = sums[k, 0:1, width:]
            row = sums[3 + k, 0:1, :lanes]
            stats_out[pl.ds(hidden_row + 2 * k + bit(place, k), 1), :] = row
            total = total + jnp.sum(row, axis=1, keepdims=True)
        stats_out[TOTALS + which : TOTALS + which + 1, :] = jnp.broadcast_to(total, (1, lanes))
    previous = jnp.sum(hidden_prev[...], axis=1, keepdims=True)
    stats_out[TOTALS + 2 : TOTALS + 3, :] = jnp.broadcast_to(previous, (1, lanes))


def stat_row(stats_ref, index):
    return stats_ref[pl.ds(index, 1), :]


def upright(row):
    return jnp.transpose(jnp.broadcast_to(row, (8, row.shape[1])))[:, 0:1]


def fetch(sources, buffers, sems):
    copies = [pltpu.make_async_copy(sources[n], buffers[n], sems.at[n]) for n in range(12)]
    for k in range(3):
        for copy in copies[k::3]:
            copy.start()
    return [copies[k::3] for k in range(3)]


def norm_kernel(prev, group_sums, whole_sums, *refs):
    factors_out, norms_out, buffers = refs[12], refs[13], refs[14:26]
    copies = fetch(refs[:12], buffers, refs[26])
    own_in, sent_in, own_out, sent_out = buffers[:3], buffers[3:6], buffers[6:9], buffers[9:12]
    place = place_in_group()
    width = own_in[0].shape[0]
    row = lax.broadcasted_iota(jnp.int32, prev.shape, 0)
    by_width = row < IN_HIDDEN
    mean = jnp.where(by_width, whole_sums[...] / FF, group_sums[...] / D)
    factors_out[...] = DECAY_RATE * prev[...] + (1.0 - DECAY_RATE) * mean
    norm_in, norm_out = 0.0, 0.0
    for k in range(3):
        for copy in copies[k]:
            copy.wait()
        half = own_in[k].shape[1]
        partner = flipped(place, 1 << k)
        own_row = stat_row(factors_out, IN_WIDTH + place)[:, :width]
        pair_row = stat_row(factors_out, IN_WIDTH + partner)[:, :width]
        hidden_row = stat_row(factors_out, IN_HIDDEN + 2 * k + bit(place, k))[:, :half]
        sent = sent_in[k][...].astype(jnp.float32)
        down = jnp.sum(own_in[k][...] * own_in[k][...] * upright(1.0 / own_row), axis=0, keepdims=True)
        down = down + jnp.sum(sent * sent * upright(1.0 / pair_row), axis=0, keepdims=True)
        norm_in = norm_in + jnp.sum(down / hidden_row, axis=1, keepdims=True)
        own_row = stat_row(factors_out, OUT_WIDTH + place)[:, :width]
        pair_row = stat_row(factors_out, OUT_WIDTH + partner)[:, :width]
        hidden_row = stat_row(factors_out, OUT_HIDDEN + 2 * k + bit(place, k))[:, :half]
        inverse = upright(1.0 / hidden_row)
        sent = sent_out[k][...].astype(jnp.float32)
        down = jnp.sum(own_out[k][...] * own_out[k][...] * inverse, axis=0, keepdims=True) / own_row
        down = down + jnp.sum(sent * sent * inverse, axis=0, keepdims=True) / pair_row
        norm_out = norm_out + jnp.sum(down, axis=1, keepdims=True)
    row = lax.broadcasted_iota(jnp.int32, norms_out.shape, 0)
    norms_out[...] = jnp.where(row == 0, norm_in, norm_out)


def final_kernel(bounds, prev, factors, whole_sums, norms, *refs):
    update_in, update_out, buffers = refs[12], refs[13], refs[14:26]
    copies = fetch(refs[:12], buffers, refs[26])
    own_in, own_out, got_in, got_out = buffers[:3], buffers[3:6], buffers[6:9], buffers[9:12]
    place = place_in_group()
    width = update_in.shape[0]
    count = float(D) * float(FF)
    mean_in = DECAY_RATE * jnp.mean(prev[IN_WIDTH : IN_WIDTH + 8, :width], keepdims=True)
    mean_in = mean_in + (1.0 - DECAY_RATE) * whole_sums[TOTALS : TOTALS + 1, 0:1] / count
    mean_out = DECAY_RATE * whole_sums[TOTALS + 2 : TOTALS + 3, 0:1] / (FF * GROUP)
    mean_out = mean_out + (1.0 - DECAY_RATE) * whole_sums[TOTALS + 1 : TOTALS + 2, 0:1] / count
    factor_in = jnp.sqrt(mean_in) / jnp.maximum(1.0, jnp.sqrt(mean_in * norms[0:1, 0:1] / count))
    factor_out = jnp.sqrt(mean_out) / jnp.maximum(1.0, jnp.sqrt(mean_out * norms[1:2, 0:1] / count))
    width_in = upright(lax.rsqrt(stat_row(factors, IN_WIDTH + place)[:, :width]) * factor_in)
    width_out = lax.rsqrt(stat_row(factors, OUT_WIDTH + place)[:, :width]) * factor_out
    for k in range(3):
        for copy in copies[k]:
            copy.wait()
        low, half = bounds[k][0], (bounds[k][1] - bounds[k][0]) // 2
        own_bit = bit(place, k)
        if half % 128:
            width_scaled = (own_in[k][...] * width_in, got_in[k][...].astype(jnp.float32) * width_in)
            for side in range(2):
                hidden_in = lax.rsqrt(factors[IN_HIDDEN + 2 * k + side : IN_HIDDEN + 2 * k + side + 1, :half])
                value = jnp.where(own_bit == side, *width_scaled) * hidden_in
                update_in[:, low + side * half : low + side * half + half] = value.astype(update_in.dtype)
        for own in (True, False):
            side = own_bit if own else 1 - own_bit
            start = pl.multiple_of(low + side * half, math.gcd(low, half))
            hidden_out = upright(lax.rsqrt(stat_row(factors, OUT_HIDDEN + 2 * k + side)[:, :half]))
            if half % 128 == 0:
                hidden_in = lax.rsqrt(stat_row(factors, IN_HIDDEN + 2 * k + side)[:, :half])
                value = own_in[k][...] if own else got_in[k][...].astype(jnp.float32)
                update_in[:, pl.ds(start, half)] = (value * width_in * hidden_in).astype(update_in.dtype)
            value = own_out[k][...] if own else got_out[k][...].astype(jnp.float32)
            update_out[pl.ds(start, half), :] = (value * hidden_out * width_out).astype(update_out.dtype)


def shards(tokens, cotangent, expert_ids, in_weight, out_weight, width_states, hidden_states):
    bf16, f32 = jnp.bfloat16, jnp.float32
    shape = jax.ShapeDtypeStruct
    experts = width_states.shape[1]
    tok_rows, width = tokens.shape
    capacity = 5 * tok_rows // (4 * experts)
    part_cap = capacity // 2
    places = lax.axis_size("expert")
    block_width = width // GROUP
    position = lax.axis_index("expert")
    expert = position // GROUP
    part = lax.axis_index("ffn") % 2
    bits = [position >> k & 1 for k in range(3)]
    bounds = set_bounds(in_weight.shape[2])
    halves = [(high - low) // 2 for low, high in bounds]
    sets = range(3)
    local_in = in_weight[0]
    local_out = out_weight[0]

    is_packed = all(half % 128 == 0 for half in halves) and block_width % 128 == 0
    if is_packed:
        kept_shapes = [shape((block_width, half), bf16) for half in halves]
        kept_shapes += [shape((half, block_width), bf16) for half in halves]
        packed_shapes = [shape((2 * half * block_width // 128, 128), bf16) for half in halves]
        copies = 6 + sum(half + block_width for half in halves) // 128
        cuts = call(
            functools.partial(cut_kernel, bounds), CUT_MIB, kept_shapes + packed_shapes, local_in, local_out,
            scratch=[pltpu.SemaphoreType.DMA((copies,))], whole=(0, 1),
        )
        got_weights = [swap(cuts[6 + k], MASKS[k]) for k in sets] * 2
    else:
        cuts = []
        for taken in range(2):
            at = [bounds[k][0] + (1 - bits[k] if taken else bits[k]) * halves[k] for k in sets]
            cuts += [lax.dynamic_slice_in_dim(local_in, at[k], halves[k], 1) for k in sets]
            cuts += [lax.dynamic_slice_in_dim(local_out, at[k], halves[k], 0) for k in sets]
        got_weights = [swap(cuts[6 + n], MASKS[n % 3]) for n in range(6)]

    routed_shape = shape((experts, GROUP, part_cap, 2 * block_width), bf16)
    (routed,) = call(
        functools.partial(route_kernel, part_cap), 12, [routed_shape], expert_ids, tokens, cotangent,
        streamed=range(3),
    )
    routed = routed.reshape(places, part_cap, 2 * block_width)
    got = lax.all_to_all(routed, "expert", split_axis=0, concat_axis=0, tiled=True)
    got, got_weights = lax.optimization_barrier((got, got_weights))
    got = got.reshape(places // GROUP, GROUP, part_cap, 2 * block_width).transpose(1, 0, 2, 3)
    got = got.reshape(GROUP, -1, 2 * block_width)

    count = got.shape[1] * 4
    wide = 2 * block_width
    first_widths, second_widths = packed_widths(0, halves), packed_widths(1, halves)

    def shapes(rows, widths, dtype):
        return [shape((rows, width), dtype) for width in widths]

    def along_axes(values):
        return [swap(value, mask) for value, mask in zip(values, MASKS)]

    pairs = jnp.stack([swap(got, MASKS[k]) for k in sets])
    blocks = [(got, pairs), (swap(got, 1, "ffn"), swap(pairs, 1, "ffn"))]
    chains = range(2)
    def sums(chain, side, out_shapes):
        return call(
            functools.partial(sums_kernel, side, halves, is_packed), 14,
            out_shapes, *blocks[chain], *cuts[:6], *got_weights,
            scratch=[pltpu.VMEM((6, count, wide), bf16)],
        )

    sent = [sums(c, 1, shapes(count, first_widths, bf16)) for c in chains]
    received = [along_axes(values) for values in sent]
    blocks, sent = lax.optimization_barrier((blocks, sent))
    kept = lax.optimization_barrier([sums(c, 0, shapes(count, halves * 2, f32)) for c in chains])
    for c in chains:
        out_shapes = shapes(count // 2, halves * 2, f32) + shapes(count // 2, second_widths, bf16)
        outs = call(functools.partial(add_kernel, halves), 8, out_shapes, *kept[c], *received[c])
        kept[c], received[c] = outs[:6], along_axes(outs[6:])
    owns, nears, fars = [None] * 2, [None] * 2, [None] * 2
    for c in chains:
        out_shapes = shapes(count // 2, first_widths, bf16)
        owns[c] = call(functools.partial(act_kernel, halves), 8, out_shapes, *kept[c], *received[c])
        received[c] = along_axes(owns[c])
    for c in chains:
        out_shapes = shapes(count, second_widths, bf16)
        nears[c] = call(functools.partial(join_kernel, halves), 8, out_shapes, *owns[c], *received[c])
        fars[c] = along_axes(nears[c])

    def parts(near, far):
        return [value[n] for n in range(3) for chain in chains for value in (near[chain], far[chain])]

    values = parts(nears, fars)
    all_blocks = [value for chain in chains for value in blocks[chain]]
    chunks = got.shape[:2] + (block_width,)
    buffers = [pltpu.VMEM((2, *chunks), bf16), pltpu.VMEM((2, 3, *chunks), bf16), pltpu.VMEM((4 * count, wide), bf16)]
    buffers += [pltpu.VMEM((4 * count, width), bf16) for width in second_widths]
    buffers += [pltpu.SemaphoreType.DMA((24,))]

    lanes = max(block_width, *halves)
    hidden_pick = lax.dynamic_index_in_dim(hidden_states, expert, 1, keepdims=False)
    sums_shape = (6, 8, wide)
    outs = call(
        functools.partial(grad_out_kernel, halves), 56,
        [shape((half, block_width), f32) for half in halves]
        + [shape((half, block_width), bf16) for half in halves]
        + [shape(sums_shape, f32)],
        *all_blocks, *values,
        scratch=buffers, whole=range(16), streamed_out=range(3),
    )
    out_own, out_sent, out_sums = outs[:3], outs[3:6], outs[6]
    got_out = along_axes(out_sent)
    outs = call(
        functools.partial(grad_in_kernel, halves), 56,
        [shape((block_width, half), f32) for half in halves]
        + [shape((block_width, half), bf16) for half in halves]
        + [shape((STAT_ROWS, lanes), f32)],
        *all_blocks, *values, out_sums, hidden_pick[1:2],
        scratch=buffers + [pltpu.VMEM(sums_shape, f32)], whole=range(16), streamed_out=range(3),
    )
    in_own, in_sent, stats = outs[:3], outs[3:6], outs[6]

    width_pick = lax.dynamic_index_in_dim(width_states, expert, 1, keepdims=False)

    def padded(values):
        return jnp.pad(values, ((0, 0), (0, lanes - values.shape[1])), constant_values=1.0)

    prev = [padded(width_pick.reshape(2 * GROUP, block_width))]
    for which in range(2):
        for k in sets:
            low, high = bounds[k]
            prev.append(padded(hidden_pick[which, low:high].reshape(2, halves[k])))
    prev.append(jnp.ones((STAT_ROWS - TOTALS, lanes), f32))
    prev = jnp.concatenate(prev)

    def fetched(*groups):
        arrays = [value for group in groups for value in group]
        return [pltpu.VMEM(value.shape, value.dtype) for value in arrays] + [pltpu.SemaphoreType.DMA((len(arrays),))]

    def totals(values):
        values = values + swap(values, 1) + swap(values, 2) + swap(values, 3)
        if lax.axis_size("ffn") > 2:
            values = values + swap(values, 4)
            return values, ffn_total(values)
        ends = [(e, f) for e in range(places) for f in range(2)]

        def other(expert_mask, ffn_mask):
            moves = [(e * 2 + f, (e ^ expert_mask) * 2 + (f ^ ffn_mask)) for e, f in ends]
            return lax.ppermute(values, ("expert", "ffn"), moves)

        cube = values + swap(values, 4)
        return cube, cube + (other(0, 1) + other(4, 1))

    stats, got_out = lax.optimization_barrier((stats, got_out))
    group_sums, whole_sums = totals(stats)
    in_sent, whole_sums = lax.optimization_barrier((in_sent, whole_sums))
    got_in = along_axes(in_sent)
    factors, norms = call(
        norm_kernel, 52,
        [shape((STAT_ROWS, lanes), f32), shape((8, 128), f32)],
        prev, group_sums, whole_sums, *in_own, *in_sent, *out_own, *out_sent,
        scratch=fetched(in_own, in_sent, out_own, out_sent), whole=range(3, 15),
    )
    norms, got_in = lax.optimization_barrier((norms, got_in))
    norms = totals(norms)[1]
    update_in, update_out = call(
        functools.partial(final_kernel, bounds), 52,
        [shape(local_in.shape, bf16), shape(local_out.shape, bf16)],
        prev, factors, whole_sums, norms, *in_own, *out_own, *got_in, *got_out,
        scratch=fetched(in_own, out_own, got_in, got_out), whole=range(4, 16), streamed_out=range(2),
    )
    return (update_in[None], update_out[None])


def solution(mesh):
    return jax.shard_map(
        shards,
        mesh=mesh,
        in_specs=(
            P("expert", None),
            P("expert", None),
            P("expert", None),
            P("expert", None, "ffn"),
            P("expert", "ffn", None),
            P(),
            P(None, None, "ffn"),
        ),
        out_specs=(P("expert", None, "ffn"), P("expert", "ffn", None)),
        check_vma=False,
    )
```

```python
import functools
import math

import jax
import jax.numpy as jnp
from jax import lax
from jax.experimental import pallas as pl
from jax.experimental.pallas import tpu as pltpu
from jax.sharding import PartitionSpec as P

D = 4096
FF = 5120
GROUP = 8


DECAY_RATE = 0.9
EPS_ONE = 1e-30
ROOT_COEF = math.sqrt(2.0 / math.pi)
CUBIC_COEF = 0.044715

MASKS = (1, 2, 4)

MIB = 1024 * 1024
PACK_MIB = 44


def swap(value, mask, axis="expert"):
    pairs = [(source, source ^ mask) for source in range(lax.axis_size(axis))]
    return lax.ppermute(value, axis, pairs)


def gelu_pair(inputs):
    inner = ROOT_COEF * (inputs + CUBIC_COEF * inputs * inputs * inputs)
    tangent = jnp.tanh(inner)
    act_value = 0.5 * inputs * (1.0 + tangent)
    act_slope = 0.5 * (1.0 + tangent) + 0.5 * inputs * (1.0 - tangent * tangent) * ROOT_COEF * (
        1.0 + 3.0 * CUBIC_COEF * inputs * inputs
    )
    return (act_value, act_slope)


def ffn_total(values):
    mask = 1
    while mask < lax.axis_size("ffn"):
        values = values + swap(values, mask, "ffn")
        mask *= 2
    return values


def set_bounds(hidden):
    unit = next(unit for unit in (256, 128, 2) if hidden % unit == 0 and hidden // unit >= 3)
    units = hidden // unit
    bounds, low = [], 0
    for k in range(3):
        high = low + (units // 3 + (k < units % 3)) * unit
        bounds.append((low, high))
        low = high
    return bounds


def dot(left, right, left_dim, right_dim):
    return lax.dot_general(
        left, right, (((left_dim,), (right_dim,)), ((), ())), preferred_element_type=jnp.float32
    )


def call(kernel, mib, out_shape, *operands, scratch=(), streamed=(), streamed_out=(), whole=()):
    def spec(value, n, blocks, refs):
        if n in refs:
            return pl.BlockSpec(memory_space=pltpu.HBM)
        if n in blocks:
            return pl.BlockSpec(value.shape, lambda: (0,) * len(value.shape))
        return pl.BlockSpec(memory_space=pltpu.VMEM)

    return pl.pallas_call(
        kernel,
        out_shape=out_shape,
        in_specs=[spec(value, n, streamed, whole) for n, value in enumerate(operands)],
        out_specs=[spec(value, n, streamed_out, ()) for n, value in enumerate(out_shape)],
        scratch_shapes=list(scratch),
        compiler_params=pltpu.CompilerParams(vmem_limit_bytes=mib * MIB),
    )(*operands)


def padded_width(half):
    return -(-half // 128) * 128


def packed_place(step, matrix, k, halves):
    axis = (k + 1 + (step + matrix) % 2) % 3
    return axis, padded_width(halves[(axis + 2 - step) % 3]) if matrix else 0


def packed_widths(step, halves):
    return [padded_width(halves[(axis + 2 - step) % 3]) + halves[(axis + 1 + step) % 3] for axis in range(3)]


def place_in_group():
    return lax.rem(lax.axis_index("expert"), GROUP)


def bit(place, k):
    return lax.rem(lax.div(place, 1 << k), 2)


def flipped(place, mask):
    for k in range(3):
        if mask >> k & 1:
            place = place + (1 - 2 * bit(place, k)) * (1 << k)
    return place


def partial_sum(rows, own_weight, got_weight, by_row):
    width = rows.shape[1] // 2
    contract = 1 if by_row else 0
    return dot(rows[:, :width], own_weight, 1, contract) + dot(rows[:, width:], got_weight, 1, contract)


def route_kernel(part_cap, ids, tokens, cotangent, out):
    rows, experts, groups = ids.shape[0], out.shape[0], out.shape[1]
    width = out.shape[3] // 2
    part = lax.rem(lax.axis_index("ffn"), 2)
    onehot = lax.broadcasted_iota(jnp.int32, (rows, 128), 1) == ids[...]
    earlier = lax.broadcasted_iota(jnp.int32, (rows, rows), 0) > lax.broadcasted_iota(jnp.int32, (rows, rows), 1)
    before = dot(earlier.astype(jnp.float32), onehot.astype(jnp.float32), 1, 0)
    slot = jnp.sum(jnp.where(onehot, before, 0.0), axis=1, keepdims=True).astype(jnp.int32) - part * part_cap
    target = jnp.where((slot >= 0) & (slot < part_cap), ids[...] * part_cap + slot, -1)
    select = lax.broadcasted_iota(jnp.int32, (rows, experts * part_cap), 1) == target
    select = select.astype(jnp.float32).astype(jnp.bfloat16)
    for n, values in enumerate((tokens, cotangent)):
        routed = dot(select, values[...], 0, 0)
        for e in range(experts):
            mine = routed[e * part_cap : (e + 1) * part_cap].astype(jnp.bfloat16)
            for b in range(groups):
                out[e, b, :, n * width : (n + 1) * width] = mine[:, b * width : (b + 1) * width]


def run_copies(moves, sems):
    copies = [pltpu.make_async_copy(source, target, sems.at[n]) for n, (source, target) in enumerate(moves)]
    for copy in copies:
        copy.start()
    for copy in copies:
        copy.wait()


def keep_kernel(bounds, weight_in, weight_out, *refs):
    moves = []
    for k in range(3):
        low, half = bounds[k][0], (bounds[k][1] - bounds[k][0]) // 2
        kept = pl.ds(pl.multiple_of(low + bit(place_in_group(), k) * half, 128), half)
        moves += [(weight_in.at[:, kept], refs[k]), (weight_out.at[kept, :], refs[3 + k])]
    run_copies(moves, refs[6])


def pack_kernel(bounds, weight_in, weight_out, *refs):
    packed, moves = refs[:3], []
    width = weight_in.shape[0]
    for k in range(3):
        low, half = bounds[k][0], (bounds[k][1] - bounds[k][0]) // 2
        start = low + (1 - bit(place_in_group(), k)) * half
        at = 0
        for n in range(half // 128):
            part = pl.ds(pl.multiple_of(start + n * 128, 128), 128)
            moves.append((weight_in.at[:, part], packed[k].at[at : at + width]))
            at += width
        for n in range(width // 128):
            part = pl.ds(pl.multiple_of(start, 128), half)
            moves.append((weight_out.at[part, n * 128 : n * 128 + 128], packed[k].at[at : at + half]))
            at += half
    run_copies(moves, refs[3])


def got_weight(ref, by_row, half, width):
    at = half // 128 * width if by_row else 0
    rows = half if by_row else width
    blocks = (width if by_row else half) // 128
    return jnp.concatenate([ref[at + n * rows : at + (n + 1) * rows, :] for n in range(blocks)], axis=1)


def assemble(rows, start, own, pair, lanes, k, axis, side):
    count, width = own.shape[1], rows.shape[1] // 2
    first, second = 1 << axis, 1 << (3 - axis - k)
    for j in range(2):
        for l in range(2):
            chunk = flipped(place_in_group(), side * first + j * second + l * (1 << k))
            at = start + (j * 2 + l) * count
            rows[at : at + count, :width] = own[chunk, :, lanes]
            rows[at : at + count, width:] = pair[chunk, :, lanes]


def sums_kernel(side, halves, is_packed, *refs):
    own, pairs, own_weights, got_weights = refs[0], refs[1], refs[2:8], refs[8:14]
    sums_out, rows = refs[14:-1], refs[-1]
    width = own.shape[2] // 2
    for matrix in range(2):
        lanes = slice(matrix * width, (matrix + 1) * width)
        for k in range(3):
            n, half = 3 * matrix + k, halves[k]
            axis = packed_place(0, matrix, k, halves)[0]
            assemble(rows.at[n], 0, own, pairs.at[k], lanes, k, axis, side)
            by_row = matrix == 1
            got = got_weight(got_weights[n], by_row, half, width) if is_packed else got_weights[n][...]
            sums = partial_sum(rows[n], own_weights[n][...], got, by_row)
            if side:
                at = packed_place(0, matrix, k, halves)[1]
                sums_out[axis][:, at : at + half] = sums.astype(jnp.bfloat16)
            else:
                sums_out[n][...] = sums


def add_kernel(halves, *refs):
    kept, received, total_out, sent_out = refs[:6], refs[6:9], refs[9:15], refs[15:18]
    for matrix in range(2):
        for k in range(3):
            n, half = 3 * matrix + k, halves[k]
            middle = kept[n].shape[0] // 2
            axis, at = packed_place(0, matrix, k, halves)
            total = kept[n][...] + received[axis][:, at : at + half].astype(jnp.float32)
            total_out[n][...] = total[:middle]
            axis, at = packed_place(1, matrix, k, halves)
            sent_out[axis][:, at : at + half] = total[middle:].astype(jnp.bfloat16)


def act_kernel(halves, *refs):
    kept, received, outs = refs[:6], refs[6:9], refs[9:12]
    for k in range(3):
        values = []
        for matrix in range(2):
            axis, at = packed_place(1, matrix, k, halves)
            values.append(kept[3 * matrix + k][...] + received[axis][:, at : at + halves[k]].astype(jnp.float32))
        act_value, act_slope = gelu_pair(values[0])
        for matrix, value in enumerate((act_value, values[1] * act_slope)):
            axis, at = packed_place(0, matrix, k, halves)
            outs[axis][:, at : at + halves[k]] = value.astype(jnp.bfloat16)


def join_kernel(halves, *refs):
    own, got, outs = refs[:3], refs[3:6], refs[6:9]
    for matrix in range(2):
        for k in range(3):
            source, start = packed_place(0, matrix, k, halves)
            axis, at = packed_place(1, matrix, k, halves)
            rows = own[source].shape[0]
            outs[axis][:rows, at : at + halves[k]] = own[source][:, start : start + halves[k]]
            outs[axis][rows:, at : at + halves[k]] = got[source][:, start : start + halves[k]]


def gradients(hidden_first, halves, blocks, values, buffers, own_out, sent_out, sums_out):
    own_buffer, pair_buffer, rows, value_buffers, sems = buffers[0], buffers[1], buffers[2], buffers[3:6], buffers[6]
    matrix = 0 if hidden_first else 1
    part = rows.shape[0] // 4
    width = rows.shape[1] // 2
    lanes = slice(width, 2 * width) if hidden_first else slice(0, width)
    set_copies = []
    for k in range(3):
        axis, at = packed_place(1, matrix, k, halves)
        parts, buffer = values[4 * axis : 4 * axis + 4], value_buffers[axis]
        if all(half % 128 == 0 for half in halves):
            parts = [value.at[:, at : at + halves[k]] for value in parts]
            buffer = buffer.at[:, at : at + halves[k]]
        moves = [(parts[i], buffer.at[pl.ds(i * part, part)]) for i in range(4)]
        for chain in range(2):
            moves.append((blocks[2 * chain + 1].at[k, :, :, lanes], pair_buffer.at[chain, k]))
            if k == 0:
                moves.append((blocks[2 * chain].at[:, :, lanes], own_buffer.at[chain]))
        copies = [pltpu.make_async_copy(*move, sems.at[k * 8 + n]) for n, move in enumerate(moves)]
        for copy in copies:
            copy.start()
        set_copies.append(copies)
    for k in range(3):
        for copy in set_copies[k]:
            copy.wait()
        axis = packed_place(0, 1 - matrix, k, halves)[0]
        for chain in range(2):
            for side in range(2):
                start = (2 * chain + side) * part
                assemble(rows, start, own_buffer.at[chain], pair_buffer.at[chain, k], slice(None), k, axis, side)
        axis, at = packed_place(1, matrix, k, halves)
        value = value_buffers[axis][:, at : at + halves[k]]
        if hidden_first:
            grad = dot(value, rows[...], 0, 0)
            own_out[k][...] = grad[:, :width]
            sent_out[k][...] = grad[:, width:].astype(jnp.bfloat16)
        else:
            grad = dot(rows[...], value, 0, 0)
            own_out[k][...] = grad[:width]
            sent_out[k][...] = grad[width:].astype(jnp.bfloat16)
        square = grad * grad + EPS_ONE
        down = jnp.sum(square, axis=0, keepdims=True)
        down = jnp.broadcast_to(down, (8, square.shape[1]))
        if square.shape[1] % 128 == 0:
            square = sum(square[:, n : n + 128] for n in range(0, square.shape[1], 128))
        across = dot(jnp.ones((8, square.shape[1]), jnp.float32), square, 1, 1)
        by_width, by_hidden = (down, across) if hidden_first else (across, down)
        sums_out[k] = by_width
        sums_out[3 + k] = jnp.zeros(sums_out.shape[1:], jnp.float32)
        sums_out[3 + k, :, : by_hidden.shape[1]] = by_hidden


def grad_out_kernel(halves, *refs):
    blocks, values, outs, buffers = refs[:4], refs[4:16], refs[16:23], refs[23:]
    gradients(True, halves, blocks, values, buffers, outs[:3], outs[3:6], outs[6])


def grad_in_kernel(halves, *refs):
    blocks, values, other_sums, hidden_prev, outs, buffers = (
        refs[:4], refs[4:16], refs[16], refs[17], refs[18:25], refs[25:]
    )
    sums = buffers[-1]
    gradients(False, halves, blocks, values, buffers[:-1], outs[:3], outs[3:6], sums)
    collect(hidden_prev, (sums, other_sums), outs[6])


IN_WIDTH, OUT_WIDTH, IN_HIDDEN, OUT_HIDDEN, TOTALS, STAT_ROWS = 0, 8, 16, 22, 28, 32


def collect(hidden_prev, all_sums, stats_out):
    place = place_in_group()
    stats_out[...] = jnp.zeros_like(stats_out)
    lanes = stats_out.shape[1]
    for which in range(2):
        sums = all_sums[which]
        width_row, hidden_row = (IN_WIDTH, OUT_WIDTH)[which], (IN_HIDDEN, OUT_HIDDEN)[which]
        width = sums.shape[2] // 2
        stats_out[pl.ds(width_row + place, 1), :] = sum(sums[k, 0:1, :width] for k in range(3))
        total = 0.0
        for k in range(3):
            stats_out[pl.ds(width_row + flipped(place, 1 << k), 1), :] = sums[k, 0:1, width:]
            row = sums[3 + k, 0:1, :lanes]
            stats_out[pl.ds(hidden_row + 2 * k + bit(place, k), 1), :] = row
            total = total + jnp.sum(row, axis=1, keepdims=True)
        stats_out[TOTALS + which : TOTALS + which + 1, :] = jnp.broadcast_to(total, (1, lanes))
    previous = jnp.sum(hidden_prev[...], axis=1, keepdims=True)
    stats_out[TOTALS + 2 : TOTALS + 3, :] = jnp.broadcast_to(previous, (1, lanes))


def stat_row(stats_ref, index):
    return stats_ref[pl.ds(index, 1), :]


def upright(row):
    return jnp.transpose(jnp.broadcast_to(row, (8, row.shape[1])))[:, 0:1]


def fetch(sources, buffers, sems):
    copies = [pltpu.make_async_copy(sources[n], buffers[n], sems.at[n]) for n in range(12)]
    for k in range(3):
        for copy in copies[k::3]:
            copy.start()
    return [copies[k::3] for k in range(3)]


def norm_kernel(prev, group_sums, whole_sums, *refs):
    factors_out, norms_out, buffers = refs[12], refs[13], refs[14:26]
    copies = fetch(refs[:12], buffers, refs[26])
    own_in, sent_in, own_out, sent_out = buffers[:3], buffers[3:6], buffers[6:9], buffers[9:12]
    place = place_in_group()
    width = own_in[0].shape[0]
    row = lax.broadcasted_iota(jnp.int32, prev.shape, 0)
    by_width = row < IN_HIDDEN
    mean = jnp.where(by_width, whole_sums[...] / FF, group_sums[...] / D)
    factors_out[...] = DECAY_RATE * prev[...] + (1.0 - DECAY_RATE) * mean
    norm_in, norm_out = 0.0, 0.0
    for k in range(3):
        for copy in copies[k]:
            copy.wait()
        half = own_in[k].shape[1]
        partner = flipped(place, 1 << k)
        own_row = stat_row(factors_out, IN_WIDTH + place)[:, :width]
        pair_row = stat_row(factors_out, IN_WIDTH + partner)[:, :width]
        hidden_row = stat_row(factors_out, IN_HIDDEN + 2 * k + bit(place, k))[:, :half]
        sent = sent_in[k][...].astype(jnp.float32)
        down = jnp.sum(own_in[k][...] * own_in[k][...] * upright(1.0 / own_row), axis=0, keepdims=True)
        down = down + jnp.sum(sent * sent * upright(1.0 / pair_row), axis=0, keepdims=True)
        norm_in = norm_in + jnp.sum(down / hidden_row, axis=1, keepdims=True)
        own_row = stat_row(factors_out, OUT_WIDTH + place)[:, :width]
        pair_row = stat_row(factors_out, OUT_WIDTH + partner)[:, :width]
        hidden_row = stat_row(factors_out, OUT_HIDDEN + 2 * k + bit(place, k))[:, :half]
        inverse = upright(1.0 / hidden_row)
        sent = sent_out[k][...].astype(jnp.float32)
        down = jnp.sum(own_out[k][...] * own_out[k][...] * inverse, axis=0, keepdims=True) / own_row
        down = down + jnp.sum(sent * sent * inverse, axis=0, keepdims=True) / pair_row
        norm_out = norm_out + jnp.sum(down, axis=1, keepdims=True)
    row = lax.broadcasted_iota(jnp.int32, norms_out.shape, 0)
    norms_out[...] = jnp.where(row == 0, norm_in, norm_out)


def final_kernel(bounds, prev, factors, whole_sums, norms, *refs):
    update_in, update_out, buffers = refs[12], refs[13], refs[14:26]
    copies = fetch(refs[:12], buffers, refs[26])
    own_in, own_out, got_in, got_out = buffers[:3], buffers[3:6], buffers[6:9], buffers[9:12]
    place = place_in_group()
    width = update_in.shape[0]
    count = float(D) * float(FF)
    mean_in = DECAY_RATE * jnp.mean(prev[IN_WIDTH : IN_WIDTH + 8, :width], keepdims=True)
    mean_in = mean_in + (1.0 - DECAY_RATE) * whole_sums[TOTALS : TOTALS + 1, 0:1] / count
    mean_out = DECAY_RATE * whole_sums[TOTALS + 2 : TOTALS + 3, 0:1] / (FF * GROUP)
    mean_out = mean_out + (1.0 - DECAY_RATE) * whole_sums[TOTALS + 1 : TOTALS + 2, 0:1] / count
    factor_in = jnp.sqrt(mean_in) / jnp.maximum(1.0, jnp.sqrt(mean_in * norms[0:1, 0:1] / count))
    factor_out = jnp.sqrt(mean_out) / jnp.maximum(1.0, jnp.sqrt(mean_out * norms[1:2, 0:1] / count))
    width_in = upright(lax.rsqrt(stat_row(factors, IN_WIDTH + place)[:, :width]) * factor_in)
    width_out = lax.rsqrt(stat_row(factors, OUT_WIDTH + place)[:, :width]) * factor_out
    for k in range(3):
        for copy in copies[k]:
            copy.wait()
        low, half = bounds[k][0], (bounds[k][1] - bounds[k][0]) // 2
        own_bit = bit(place, k)
        if half % 128:
            width_scaled = (own_in[k][...] * width_in, got_in[k][...].astype(jnp.float32) * width_in)
            for side in range(2):
                hidden_in = lax.rsqrt(factors[IN_HIDDEN + 2 * k + side : IN_HIDDEN + 2 * k + side + 1, :half])
                value = jnp.where(own_bit == side, *width_scaled) * hidden_in
                update_in[:, low + side * half : low + side * half + half] = value.astype(update_in.dtype)
        for own in (True, False):
            side = own_bit if own else 1 - own_bit
            start = pl.multiple_of(low + side * half, math.gcd(low, half))
            hidden_out = upright(lax.rsqrt(stat_row(factors, OUT_HIDDEN + 2 * k + side)[:, :half]))
            if half % 128 == 0:
                hidden_in = lax.rsqrt(stat_row(factors, IN_HIDDEN + 2 * k + side)[:, :half])
                value = own_in[k][...] if own else got_in[k][...].astype(jnp.float32)
                update_in[:, pl.ds(start, half)] = (value * width_in * hidden_in).astype(update_in.dtype)
            value = own_out[k][...] if own else got_out[k][...].astype(jnp.float32)
            update_out[pl.ds(start, half), :] = (value * hidden_out * width_out).astype(update_out.dtype)


def shards(tokens, cotangent, expert_ids, in_weight, out_weight, width_states, hidden_states):
    bf16, f32 = jnp.bfloat16, jnp.float32
    shape = jax.ShapeDtypeStruct
    experts = width_states.shape[1]
    tok_rows, width = tokens.shape
    capacity = 5 * tok_rows // (4 * experts)
    part_cap = capacity // 2
    places = lax.axis_size("expert")
    block_width = width // GROUP
    position = lax.axis_index("expert")
    expert = position // GROUP
    part = lax.axis_index("ffn") % 2
    bits = [position >> k & 1 for k in range(3)]
    bounds = set_bounds(in_weight.shape[2])
    halves = [(high - low) // 2 for low, high in bounds]
    sets = range(3)
    local_in = in_weight[0]
    local_out = out_weight[0]

    is_packed = all(half % 128 == 0 for half in halves) and block_width % 128 == 0
    if is_packed:
        packed_shapes = [shape((2 * half * block_width // 128, 128), bf16) for half in halves]
        copies = sum(half + block_width for half in halves) // 128
        cuts = call(
            functools.partial(pack_kernel, bounds), PACK_MIB, packed_shapes, local_in, local_out,
            scratch=[pltpu.SemaphoreType.DMA((copies,))], whole=(0, 1),
        )
        got_weights = [swap(cuts[k], MASKS[k]) for k in sets] * 2
    else:
        cuts = []
        for taken in range(2):
            at = [bounds[k][0] + (1 - bits[k] if taken else bits[k]) * halves[k] for k in sets]
            cuts += [lax.dynamic_slice_in_dim(local_in, at[k], halves[k], 1) for k in sets]
            cuts += [lax.dynamic_slice_in_dim(local_out, at[k], halves[k], 0) for k in sets]
        got_weights = [swap(cuts[6 + n], MASKS[n % 3]) for n in range(6)]

    routed_shape = shape((experts, GROUP, part_cap, 2 * block_width), bf16)
    (routed,) = call(
        functools.partial(route_kernel, part_cap), 12, [routed_shape], expert_ids, tokens, cotangent,
        streamed=range(3),
    )
    routed = routed.reshape(places, part_cap, 2 * block_width)
    got = lax.all_to_all(routed, "expert", split_axis=0, concat_axis=0, tiled=True)
    got, got_weights, local_in, local_out = lax.optimization_barrier((got, got_weights, local_in, local_out))
    if is_packed:
        kept_shapes = [shape((block_width, half), bf16) for half in halves]
        kept_shapes += [shape((half, block_width), bf16) for half in halves]
        cuts = call(
            functools.partial(keep_kernel, bounds), PACK_MIB, kept_shapes, local_in, local_out,
            scratch=[pltpu.SemaphoreType.DMA((6,))], whole=(0, 1),
        )
    got = got.reshape(places // GROUP, GROUP, part_cap, 2 * block_width).transpose(1, 0, 2, 3)
    got = got.reshape(GROUP, -1, 2 * block_width)

    count = got.shape[1] * 4
    wide = 2 * block_width
    first_widths, second_widths = packed_widths(0, halves), packed_widths(1, halves)

    def shapes(rows, widths, dtype):
        return [shape((rows, width), dtype) for width in widths]

    def along_axes(values):
        return [swap(value, mask) for value, mask in zip(values, MASKS)]

    pairs = jnp.stack([swap(got, MASKS[k]) for k in sets])
    blocks = [(got, pairs), (swap(got, 1, "ffn"), swap(pairs, 1, "ffn"))]
    chains = range(2)
    def sums(chain, side, out_shapes):
        return call(
            functools.partial(sums_kernel, side, halves, is_packed), 14,
            out_shapes, *blocks[chain], *cuts[:6], *got_weights,
            scratch=[pltpu.VMEM((6, count, wide), bf16)],
        )

    sent = [sums(c, 1, shapes(count, first_widths, bf16)) for c in chains]
    received = [along_axes(values) for values in sent]
    blocks, sent = lax.optimization_barrier((blocks, sent))
    kept = lax.optimization_barrier([sums(c, 0, shapes(count, halves * 2, f32)) for c in chains])
    for c in chains:
        out_shapes = shapes(count // 2, halves * 2, f32) + shapes(count // 2, second_widths, bf16)
        outs = call(functools.partial(add_kernel, halves), 8, out_shapes, *kept[c], *received[c])
        kept[c], received[c] = outs[:6], along_axes(outs[6:])
    owns, nears, fars = [None] * 2, [None] * 2, [None] * 2
    for c in chains:
        out_shapes = shapes(count // 2, first_widths, bf16)
        owns[c] = call(functools.partial(act_kernel, halves), 8, out_shapes, *kept[c], *received[c])
        received[c] = along_axes(owns[c])
    for c in chains:
        out_shapes = shapes(count, second_widths, bf16)
        nears[c] = call(functools.partial(join_kernel, halves), 8, out_shapes, *owns[c], *received[c])
        fars[c] = along_axes(nears[c])

    def parts(near, far):
        return [value[n] for n in range(3) for chain in chains for value in (near[chain], far[chain])]

    values = parts(nears, fars)
    all_blocks = [value for chain in chains for value in blocks[chain]]
    chunks = got.shape[:2] + (block_width,)
    buffers = [pltpu.VMEM((2, *chunks), bf16), pltpu.VMEM((2, 3, *chunks), bf16), pltpu.VMEM((4 * count, wide), bf16)]
    buffers += [pltpu.VMEM((4 * count, width), bf16) for width in second_widths]
    buffers += [pltpu.SemaphoreType.DMA((24,))]

    lanes = max(block_width, *halves)
    hidden_pick = lax.dynamic_index_in_dim(hidden_states, expert, 1, keepdims=False)
    sums_shape = (6, 8, wide)
    outs = call(
        functools.partial(grad_out_kernel, halves), 56,
        [shape((half, block_width), f32) for half in halves]
        + [shape((half, block_width), bf16) for half in halves]
        + [shape(sums_shape, f32)],
        *all_blocks, *values,
        scratch=buffers, whole=range(16), streamed_out=range(3),
    )
    out_own, out_sent, out_sums = outs[:3], outs[3:6], outs[6]
    got_out = along_axes(out_sent)
    outs = call(
        functools.partial(grad_in_kernel, halves), 56,
        [shape((block_width, half), f32) for half in halves]
        + [shape((block_width, half), bf16) for half in halves]
        + [shape((STAT_ROWS, lanes), f32)],
        *all_blocks, *values, out_sums, hidden_pick[1:2],
        scratch=buffers + [pltpu.VMEM(sums_shape, f32)], whole=range(16), streamed_out=range(3),
    )
    in_own, in_sent, stats = outs[:3], outs[3:6], outs[6]

    width_pick = lax.dynamic_index_in_dim(width_states, expert, 1, keepdims=False)

    def padded(values):
        return jnp.pad(values, ((0, 0), (0, lanes - values.shape[1])), constant_values=1.0)

    prev = [padded(width_pick.reshape(2 * GROUP, block_width))]
    for which in range(2):
        for k in sets:
            low, high = bounds[k]
            prev.append(padded(hidden_pick[which, low:high].reshape(2, halves[k])))
    prev.append(jnp.ones((STAT_ROWS - TOTALS, lanes), f32))
    prev = jnp.concatenate(prev)

    def fetched(*groups):
        arrays = [value for group in groups for value in group]
        return [pltpu.VMEM(value.shape, value.dtype) for value in arrays] + [pltpu.SemaphoreType.DMA((len(arrays),))]

    def totals(values, others):
        values = values + swap(values, 1) + swap(values, 2) + swap(values, 3)
        values, others = lax.optimization_barrier((values, others))
        if lax.axis_size("ffn") > 2:
            values = values + swap(values, 4)
            return values, ffn_total(values), others
        ends = [(e, f) for e in range(places) for f in range(2)]

        def other(expert_mask, ffn_mask):
            moves = [(e * 2 + f, (e ^ expert_mask) * 2 + (f ^ ffn_mask)) for e, f in ends]
            return lax.ppermute(values, ("expert", "ffn"), moves)

        cube = values + swap(values, 4)
        return cube, cube + (other(0, 1) + other(4, 1)), others

    stats, got_out = lax.optimization_barrier((stats, got_out))
    group_sums, whole_sums, got_out = totals(stats, got_out)
    in_sent, whole_sums = lax.optimization_barrier((in_sent, whole_sums))
    got_in = along_axes(in_sent)
    factors, norms = call(
        norm_kernel, 52,
        [shape((STAT_ROWS, lanes), f32), shape((8, 128), f32)],
        prev, group_sums, whole_sums, *in_own, *in_sent, *out_own, *out_sent,
        scratch=fetched(in_own, in_sent, out_own, out_sent), whole=range(3, 15),
    )
    norms, got_in = totals(norms, got_in)[1:]
    update_in, update_out = call(
        functools.partial(final_kernel, bounds), 52,
        [shape(local_in.shape, bf16), shape(local_out.shape, bf16)],
        prev, factors, whole_sums, norms, *in_own, *out_own, *got_in, *got_out,
        scratch=fetched(in_own, out_own, got_in, got_out), whole=range(4, 16), streamed_out=range(2),
    )
    return (update_in[None], update_out[None])


def solution(mesh):
    return jax.shard_map(
        shards,
        mesh=mesh,
        in_specs=(
            P("expert", None),
            P("expert", None),
            P("expert", None),
            P("expert", None, "ffn"),
            P("expert", "ffn", None),
            P(),
            P(None, None, "ffn"),
        ),
        out_specs=(P("expert", None, "ffn"), P("expert", "ffn", None)),
        check_vma=False,
    )
```

```python
import functools
import math

import jax
import jax.numpy as jnp
from jax import lax
from jax.experimental import pallas as pl
from jax.experimental.pallas import tpu as pltpu
from jax.sharding import PartitionSpec as P

D = 4096
FF = 5120
GROUP = 8


DECAY_RATE = 0.9
EPS_ONE = 1e-30
ROOT_COEF = math.sqrt(2.0 / math.pi)
CUBIC_COEF = 0.044715

MASKS = (1, 2, 4)

MIB = 1024 * 1024
CUT_MIB = 8


def swap(value, mask, axis="expert"):
    pairs = [(source, source ^ mask) for source in range(lax.axis_size(axis))]
    return lax.ppermute(value, axis, pairs)


def gelu_pair(inputs):
    inner = ROOT_COEF * (inputs + CUBIC_COEF * inputs * inputs * inputs)
    tangent = jnp.tanh(inner)
    act_value = 0.5 * inputs * (1.0 + tangent)
    act_slope = 0.5 * (1.0 + tangent) + 0.5 * inputs * (1.0 - tangent * tangent) * ROOT_COEF * (
        1.0 + 3.0 * CUBIC_COEF * inputs * inputs
    )
    return (act_value, act_slope)


def ffn_total(values):
    mask = 1
    while mask < lax.axis_size("ffn"):
        values = values + swap(values, mask, "ffn")
        mask *= 2
    return values


def set_bounds(hidden):
    unit = next(unit for unit in (256, 128, 2) if hidden % unit == 0 and hidden // unit >= 3)
    units = hidden // unit
    bounds, low = [], 0
    for k in range(3):
        high = low + (units // 3 + (k < units % 3)) * unit
        bounds.append((low, high))
        low = high
    return bounds


def dot(left, right, left_dim, right_dim):
    return lax.dot_general(
        left, right, (((left_dim,), (right_dim,)), ((), ())), preferred_element_type=jnp.float32
    )


def call(kernel, mib, out_shape, *operands, scratch=(), streamed=(), streamed_out=(), whole=()):
    def spec(value, n, blocks, refs):
        if n in refs:
            return pl.BlockSpec(memory_space=pltpu.HBM)
        if n in blocks:
            return pl.BlockSpec(value.shape, lambda: (0,) * len(value.shape))
        return pl.BlockSpec(memory_space=pltpu.VMEM)

    return pl.pallas_call(
        kernel,
        out_shape=out_shape,
        in_specs=[spec(value, n, streamed, whole) for n, value in enumerate(operands)],
        out_specs=[spec(value, n, streamed_out, ()) for n, value in enumerate(out_shape)],
        scratch_shapes=list(scratch),
        compiler_params=pltpu.CompilerParams(vmem_limit_bytes=mib * MIB),
    )(*operands)


def padded_width(half):
    return -(-half // 128) * 128


def packed_place(step, matrix, k, halves):
    axis = (k + 1 + (step + matrix) % 2) % 3
    return axis, padded_width(halves[(axis + 2 - step) % 3]) if matrix else 0


def packed_widths(step, halves):
    return [padded_width(halves[(axis + 2 - step) % 3]) + halves[(axis + 1 + step) % 3] for axis in range(3)]


def place_in_group():
    return lax.rem(lax.axis_index("expert"), GROUP)


def bit(place, k):
    return lax.rem(lax.div(place, 1 << k), 2)


def flipped(place, mask):
    for k in range(3):
        if mask >> k & 1:
            place = place + (1 - 2 * bit(place, k)) * (1 << k)
    return place


def partial_sum(rows, own_weight, got_weight, by_row):
    width = rows.shape[1] // 2
    contract = 1 if by_row else 0
    return dot(rows[:, :width], own_weight, 1, contract) + dot(rows[:, width:], got_weight, 1, contract)


def route_kernel(part_cap, ids, tokens, cotangent, out):
    rows, experts, groups = ids.shape[0], out.shape[0], out.shape[1]
    width = out.shape[3] // 2
    part = lax.rem(lax.axis_index("ffn"), 2)
    onehot = lax.broadcasted_iota(jnp.int32, (rows, 128), 1) == ids[...]
    earlier = lax.broadcasted_iota(jnp.int32, (rows, rows), 0) > lax.broadcasted_iota(jnp.int32, (rows, rows), 1)
    before = dot(earlier.astype(jnp.float32), onehot.astype(jnp.float32), 1, 0)
    slot = jnp.sum(jnp.where(onehot, before, 0.0), axis=1, keepdims=True).astype(jnp.int32) - part * part_cap
    target = jnp.where((slot >= 0) & (slot < part_cap), ids[...] * part_cap + slot, -1)
    select = lax.broadcasted_iota(jnp.int32, (rows, experts * part_cap), 1) == target
    select = select.astype(jnp.float32).astype(jnp.bfloat16)
    for n, values in enumerate((tokens, cotangent)):
        routed = dot(select, values[...], 0, 0)
        for e in range(experts):
            mine = routed[e * part_cap : (e + 1) * part_cap].astype(jnp.bfloat16)
            for b in range(groups):
                out[e, b, :, n * width : (n + 1) * width] = mine[:, b * width : (b + 1) * width]


def cut_kernel(bounds, weight_in, weight_out, *refs):
    kept_in, kept_out, packed, sems = refs[:3], refs[3:6], refs[6:9], refs[9]
    copies = []
    width = weight_in.shape[0]
    for k in range(3):
        low, half = bounds[k][0], (bounds[k][1] - bounds[k][0]) // 2
        side = bit(place_in_group(), k)
        kept = pl.ds(pl.multiple_of(low + side * half, 128), half)
        copies.append((weight_in.at[:, kept], kept_in[k], 3 * k))
        copies.append((weight_out.at[kept, :], kept_out[k], 3 * k + 1))
        start = low + (1 - side) * half
        at = 0
        for n in range(half // 128):
            part = pl.ds(pl.multiple_of(start + n * 128, 128), 128)
            copies.append((weight_in.at[:, part], packed[k].at[at : at + width], 3 * k + 2))
            at += width
        for n in range(width // 128):
            part = pl.ds(pl.multiple_of(start, 128), half)
            source = weight_out.at[part, n * 128 : n * 128 + 128]
            copies.append((source, packed[k].at[at : at + half], 3 * k + 2))
            at += half
    copies = [pltpu.make_async_copy(source, target, sems.at[n]) for n, (source, target, _) in enumerate(copies)]
    for copy in copies:
        copy.start()
    for copy in copies:
        copy.wait()


def got_weight(ref, by_row, half, width):
    at = half // 128 * width if by_row else 0
    rows = half if by_row else width
    blocks = (width if by_row else half) // 128
    return jnp.concatenate([ref[at + n * rows : at + (n + 1) * rows, :] for n in range(blocks)], axis=1)


def assemble(rows, start, own, pair, lanes, k, axis, side):
    count, width = own.shape[1], rows.shape[1] // 2
    first, second = 1 << axis, 1 << (3 - axis - k)
    for j in range(2):
        for l in range(2):
            chunk = flipped(place_in_group(), side * first + j * second + l * (1 << k))
            at = start + (j * 2 + l) * count
            rows[at : at + count, :width] = own[chunk, :, lanes]
            rows[at : at + count, width:] = pair[chunk, :, lanes]


def sums_kernel(side, halves, is_packed, *refs):
    own, pairs, own_weights, got_weights = refs[0], refs[1], refs[2:8], refs[8:14]
    sums_out, rows = refs[14:-1], refs[-1]
    width = own.shape[2] // 2
    for matrix in range(2):
        lanes = slice(matrix * width, (matrix + 1) * width)
        for k in range(3):
            n, half = 3 * matrix + k, halves[k]
            axis = packed_place(0, matrix, k, halves)[0]
            assemble(rows.at[n], 0, own, pairs.at[k], lanes, k, axis, side)
            by_row = matrix == 1
            got = got_weight(got_weights[n], by_row, half, width) if is_packed else got_weights[n][...]
            sums = partial_sum(rows[n], own_weights[n][...], got, by_row)
            if side:
                at = packed_place(0, matrix, k, halves)[1]
                sums_out[axis][:, at : at + half] = sums.astype(jnp.bfloat16)
            else:
                sums_out[n][...] = sums


def add_kernel(halves, *refs):
    kept, received, total_out, sent_out = refs[:6], refs[6:9], refs[9:15], refs[15:18]
    for matrix in range(2):
        for k in range(3):
            n, half = 3 * matrix + k, halves[k]
            middle = kept[n].shape[0] // 2
            axis, at = packed_place(0, matrix, k, halves)
            total = kept[n][...] + received[axis][:, at : at + half].astype(jnp.float32)
            total_out[n][...] = total[:middle]
            axis, at = packed_place(1, matrix, k, halves)
            sent_out[axis][:, at : at + half] = total[middle:].astype(jnp.bfloat16)


def act_kernel(halves, *refs):
    kept, received, outs = refs[:6], refs[6:9], refs[9:12]
    for k in range(3):
        values = []
        for matrix in range(2):
            axis, at = packed_place(1, matrix, k, halves)
            values.append(kept[3 * matrix + k][...] + received[axis][:, at : at + halves[k]].astype(jnp.float32))
        act_value, act_slope = gelu_pair(values[0])
        for matrix, value in enumerate((act_value, values[1] * act_slope)):
            axis, at = packed_place(0, matrix, k, halves)
            outs[axis][:, at : at + halves[k]] = value.astype(jnp.bfloat16)


def join_kernel(halves, *refs):
    own, got, outs = refs[:3], refs[3:6], refs[6:9]
    for matrix in range(2):
        for k in range(3):
            source, start = packed_place(0, matrix, k, halves)
            axis, at = packed_place(1, matrix, k, halves)
            rows = own[source].shape[0]
            outs[axis][:rows, at : at + halves[k]] = own[source][:, start : start + halves[k]]
            outs[axis][rows:, at : at + halves[k]] = got[source][:, start : start + halves[k]]


def gradients(hidden_first, halves, blocks, values, buffers, own_out, sent_out, sums_out):
    own_buffer, pair_buffer, rows, value_buffers, sems = buffers[0], buffers[1], buffers[2], buffers[3:6], buffers[6]
    matrix = 0 if hidden_first else 1
    part = rows.shape[0] // 4
    width = rows.shape[1] // 2
    lanes = slice(width, 2 * width) if hidden_first else slice(0, width)
    set_copies = []
    for k in range(3):
        axis, at = packed_place(1, matrix, k, halves)
        parts, buffer = values[4 * axis : 4 * axis + 4], value_buffers[axis]
        if all(half % 128 == 0 for half in halves):
            parts = [value.at[:, at : at + halves[k]] for value in parts]
            buffer = buffer.at[:, at : at + halves[k]]
        moves = [(parts[i], buffer.at[pl.ds(i * part, part)]) for i in range(4)]
        for chain in range(2):
            moves.append((blocks[2 * chain + 1].at[k, :, :, lanes], pair_buffer.at[chain, k]))
            if k == 0:
                moves.append((blocks[2 * chain].at[:, :, lanes], own_buffer.at[chain]))
        copies = [pltpu.make_async_copy(*move, sems.at[k * 8 + n]) for n, move in enumerate(moves)]
        for copy in copies:
            copy.start()
        set_copies.append(copies)
    for k in range(3):
        for copy in set_copies[k]:
            copy.wait()
        axis = packed_place(0, 1 - matrix, k, halves)[0]
        for chain in range(2):
            for side in range(2):
                start = (2 * chain + side) * part
                assemble(rows, start, own_buffer.at[chain], pair_buffer.at[chain, k], slice(None), k, axis, side)
        axis, at = packed_place(1, matrix, k, halves)
        value = value_buffers[axis][:, at : at + halves[k]]
        if hidden_first:
            grad = dot(value, rows[...], 0, 0)
            own_out[k][...] = grad[:, :width]
            sent_out[k][...] = grad[:, width:].astype(jnp.bfloat16)
        else:
            grad = dot(rows[...], value, 0, 0)
            own_out[k][...] = grad[:width]
            sent_out[k][...] = grad[width:].astype(jnp.bfloat16)
        square = grad * grad + EPS_ONE
        down = jnp.sum(square, axis=0, keepdims=True)
        down = jnp.broadcast_to(down, (8, square.shape[1]))
        if square.shape[1] % 128 == 0:
            square = sum(square[:, n : n + 128] for n in range(0, square.shape[1], 128))
        across = dot(jnp.ones((8, square.shape[1]), jnp.float32), square, 1, 1)
        by_width, by_hidden = (down, across) if hidden_first else (across, down)
        sums_out[k] = by_width
        sums_out[3 + k] = jnp.zeros(sums_out.shape[1:], jnp.float32)
        sums_out[3 + k, :, : by_hidden.shape[1]] = by_hidden


def grad_out_kernel(halves, *refs):
    blocks, values, outs, buffers = refs[:4], refs[4:16], refs[16:23], refs[23:]
    gradients(True, halves, blocks, values, buffers, outs[:3], outs[3:6], outs[6])


def grad_in_kernel(halves, *refs):
    blocks, values, other_sums, hidden_prev, outs, buffers = (
        refs[:4], refs[4:16], refs[16], refs[17], refs[18:25], refs[25:]
    )
    sums = buffers[-1]
    gradients(False, halves, blocks, values, buffers[:-1], outs[:3], outs[3:6], sums)
    collect(hidden_prev, (sums, other_sums), outs[6])


IN_WIDTH, OUT_WIDTH, IN_HIDDEN, OUT_HIDDEN, TOTALS, STAT_ROWS = 0, 8, 16, 22, 28, 32


def collect(hidden_prev, all_sums, stats_out):
    place = place_in_group()
    stats_out[...] = jnp.zeros_like(stats_out)
    lanes = stats_out.shape[1]
    for which in range(2):
        sums = all_sums[which]
        width_row, hidden_row = (IN_WIDTH, OUT_WIDTH)[which], (IN_HIDDEN, OUT_HIDDEN)[which]
        width = sums.shape[2] // 2
        stats_out[pl.ds(width_row + place, 1), :] = sum(sums[k, 0:1, :width] for k in range(3))
        total = 0.0
        for k in range(3):
            stats_out[pl.ds(width_row + flipped(place, 1 << k), 1), :] = sums[k, 0:1, width:]
            row = sums[3 + k, 0:1, :lanes]
            stats_out[pl.ds(hidden_row + 2 * k + bit(place, k), 1), :] = row
            total = total + jnp.sum(row, axis=1, keepdims=True)
        stats_out[TOTALS + which : TOTALS + which + 1, :] = jnp.broadcast_to(total, (1, lanes))
    previous = jnp.sum(hidden_prev[...], axis=1, keepdims=True)
    stats_out[TOTALS + 2 : TOTALS + 3, :] = jnp.broadcast_to(previous, (1, lanes))


def stat_row(stats_ref, index):
    return stats_ref[pl.ds(index, 1), :]


def upright(row):
    return jnp.transpose(jnp.broadcast_to(row, (8, row.shape[1])))[:, 0:1]


def fetch(sources, buffers, sems):
    copies = [pltpu.make_async_copy(sources[n], buffers[n], sems.at[n]) for n in range(12)]
    for k in range(3):
        for copy in copies[k::3]:
            copy.start()
    return [copies[k::3] for k in range(3)]


def norm_kernel(prev, group_sums, whole_sums, *refs):
    factors_out, norms_out, buffers = refs[12], refs[13], refs[14:26]
    copies = fetch(refs[:12], buffers, refs[26])
    own_in, sent_in, own_out, sent_out = buffers[:3], buffers[3:6], buffers[6:9], buffers[9:12]
    place = place_in_group()
    width = own_in[0].shape[0]
    row = lax.broadcasted_iota(jnp.int32, prev.shape, 0)
    by_width = row < IN_HIDDEN
    mean = jnp.where(by_width, whole_sums[...] / FF, group_sums[...] / D)
    factors_out[...] = DECAY_RATE * prev[...] + (1.0 - DECAY_RATE) * mean
    norm_in, norm_out = 0.0, 0.0
    for k in range(3):
        for copy in copies[k]:
            copy.wait()
        half = own_in[k].shape[1]
        partner = flipped(place, 1 << k)
        own_row = stat_row(factors_out, IN_WIDTH + place)[:, :width]
        pair_row = stat_row(factors_out, IN_WIDTH + partner)[:, :width]
        hidden_row = stat_row(factors_out, IN_HIDDEN + 2 * k + bit(place, k))[:, :half]
        sent = sent_in[k][...].astype(jnp.float32)
        down = jnp.sum(own_in[k][...] * own_in[k][...] * upright(1.0 / own_row), axis=0, keepdims=True)
        down = down + jnp.sum(sent * sent * upright(1.0 / pair_row), axis=0, keepdims=True)
        norm_in = norm_in + jnp.sum(down / hidden_row, axis=1, keepdims=True)
        own_row = stat_row(factors_out, OUT_WIDTH + place)[:, :width]
        pair_row = stat_row(factors_out, OUT_WIDTH + partner)[:, :width]
        hidden_row = stat_row(factors_out, OUT_HIDDEN + 2 * k + bit(place, k))[:, :half]
        inverse = upright(1.0 / hidden_row)
        sent = sent_out[k][...].astype(jnp.float32)
        down = jnp.sum(own_out[k][...] * own_out[k][...] * inverse, axis=0, keepdims=True) / own_row
        down = down + jnp.sum(sent * sent * inverse, axis=0, keepdims=True) / pair_row
        norm_out = norm_out + jnp.sum(down, axis=1, keepdims=True)
    row = lax.broadcasted_iota(jnp.int32, norms_out.shape, 0)
    norms_out[...] = jnp.where(row == 0, norm_in, norm_out)


def final_kernel(bounds, prev, factors, whole_sums, norms, *refs):
    update_in, update_out, buffers = refs[12], refs[13], refs[14:26]
    copies = fetch(refs[:12], buffers, refs[26])
    own_in, own_out, got_in, got_out = buffers[:3], buffers[3:6], buffers[6:9], buffers[9:12]
    place = place_in_group()
    width = update_in.shape[0]
    count = float(D) * float(FF)
    mean_in = DECAY_RATE * jnp.mean(prev[IN_WIDTH : IN_WIDTH + 8, :width], keepdims=True)
    mean_in = mean_in + (1.0 - DECAY_RATE) * whole_sums[TOTALS : TOTALS + 1, 0:1] / count
    mean_out = DECAY_RATE * whole_sums[TOTALS + 2 : TOTALS + 3, 0:1] / (FF * GROUP)
    mean_out = mean_out + (1.0 - DECAY_RATE) * whole_sums[TOTALS + 1 : TOTALS + 2, 0:1] / count
    factor_in = jnp.sqrt(mean_in) / jnp.maximum(1.0, jnp.sqrt(mean_in * norms[0:1, 0:1] / count))
    factor_out = jnp.sqrt(mean_out) / jnp.maximum(1.0, jnp.sqrt(mean_out * norms[1:2, 0:1] / count))
    width_in = upright(lax.rsqrt(stat_row(factors, IN_WIDTH + place)[:, :width]) * factor_in)
    width_out = lax.rsqrt(stat_row(factors, OUT_WIDTH + place)[:, :width]) * factor_out
    for k in range(3):
        for copy in copies[k]:
            copy.wait()
        low, half = bounds[k][0], (bounds[k][1] - bounds[k][0]) // 2
        own_bit = bit(place, k)
        if half % 128:
            width_scaled = (own_in[k][...] * width_in, got_in[k][...].astype(jnp.float32) * width_in)
            for side in range(2):
                hidden_in = lax.rsqrt(factors[IN_HIDDEN + 2 * k + side : IN_HIDDEN + 2 * k + side + 1, :half])
                value = jnp.where(own_bit == side, *width_scaled) * hidden_in
                update_in[:, low + side * half : low + side * half + half] = value.astype(update_in.dtype)
        for own in (True, False):
            side = own_bit if own else 1 - own_bit
            start = pl.multiple_of(low + side * half, math.gcd(low, half))
            hidden_out = upright(lax.rsqrt(stat_row(factors, OUT_HIDDEN + 2 * k + side)[:, :half]))
            if half % 128 == 0:
                hidden_in = lax.rsqrt(stat_row(factors, IN_HIDDEN + 2 * k + side)[:, :half])
                value = own_in[k][...] if own else got_in[k][...].astype(jnp.float32)
                update_in[:, pl.ds(start, half)] = (value * width_in * hidden_in).astype(update_in.dtype)
            value = own_out[k][...] if own else got_out[k][...].astype(jnp.float32)
            update_out[pl.ds(start, half), :] = (value * hidden_out * width_out).astype(update_out.dtype)


def shards(tokens, cotangent, expert_ids, in_weight, out_weight, width_states, hidden_states):
    bf16, f32 = jnp.bfloat16, jnp.float32
    shape = jax.ShapeDtypeStruct
    experts = width_states.shape[1]
    tok_rows, width = tokens.shape
    capacity = 5 * tok_rows // (4 * experts)
    part_cap = capacity // 2
    places = lax.axis_size("expert")
    block_width = width // GROUP
    position = lax.axis_index("expert")
    expert = position // GROUP
    part = lax.axis_index("ffn") % 2
    bits = [position >> k & 1 for k in range(3)]
    bounds = set_bounds(in_weight.shape[2])
    halves = [(high - low) // 2 for low, high in bounds]
    sets = range(3)
    local_in = in_weight[0]
    local_out = out_weight[0]

    is_packed = all(half % 128 == 0 for half in halves) and block_width % 128 == 0
    if is_packed:
        kept_shapes = [shape((block_width, half), bf16) for half in halves]
        kept_shapes += [shape((half, block_width), bf16) for half in halves]
        packed_shapes = [shape((2 * half * block_width // 128, 128), bf16) for half in halves]
        copies = 6 + sum(half + block_width for half in halves) // 128
        cuts = call(
            functools.partial(cut_kernel, bounds), CUT_MIB, kept_shapes + packed_shapes, local_in, local_out,
            scratch=[pltpu.SemaphoreType.DMA((copies,))], whole=(0, 1),
        )
        got_weights = [swap(cuts[6 + k], MASKS[k]) for k in sets] * 2
    else:
        cuts = []
        for taken in range(2):
            at = [bounds[k][0] + (1 - bits[k] if taken else bits[k]) * halves[k] for k in sets]
            cuts += [lax.dynamic_slice_in_dim(local_in, at[k], halves[k], 1) for k in sets]
            cuts += [lax.dynamic_slice_in_dim(local_out, at[k], halves[k], 0) for k in sets]
        got_weights = [swap(cuts[6 + n], MASKS[n % 3]) for n in range(6)]

    routed_shape = shape((experts, GROUP, part_cap, 2 * block_width), bf16)
    (routed,) = call(
        functools.partial(route_kernel, part_cap), 12, [routed_shape], expert_ids, tokens, cotangent,
        streamed=range(3),
    )
    routed = routed.reshape(places, part_cap, 2 * block_width)
    got = lax.all_to_all(routed, "expert", split_axis=0, concat_axis=0, tiled=True)
    got, got_weights = lax.optimization_barrier((got, got_weights))
    got = got.reshape(places // GROUP, GROUP, part_cap, 2 * block_width).transpose(1, 0, 2, 3)
    got = got.reshape(GROUP, -1, 2 * block_width)

    count = got.shape[1] * 4
    wide = 2 * block_width
    first_widths, second_widths = packed_widths(0, halves), packed_widths(1, halves)

    def shapes(rows, widths, dtype):
        return [shape((rows, width), dtype) for width in widths]

    def along_axes(values):
        return [swap(value, mask) for value, mask in zip(values, MASKS)]

    pairs = jnp.stack([swap(got, MASKS[k]) for k in sets])
    blocks = [(got, pairs), (swap(got, 1, "ffn"), swap(pairs, 1, "ffn"))]
    chains = range(2)
    def sums(chain, side, out_shapes):
        return call(
            functools.partial(sums_kernel, side, halves, is_packed), 14,
            out_shapes, *blocks[chain], *cuts[:6], *got_weights,
            scratch=[pltpu.VMEM((6, count, wide), bf16)],
        )

    sent = [sums(c, 1, shapes(count, first_widths, bf16)) for c in chains]
    received = [along_axes(values) for values in sent]
    blocks, sent = lax.optimization_barrier((blocks, sent))
    kept = lax.optimization_barrier([sums(c, 0, shapes(count, halves * 2, f32)) for c in chains])
    for c in chains:
        out_shapes = shapes(count // 2, halves * 2, f32) + shapes(count // 2, second_widths, bf16)
        outs = call(functools.partial(add_kernel, halves), 8, out_shapes, *kept[c], *received[c])
        kept[c], received[c] = outs[:6], along_axes(outs[6:])
    owns, nears, fars = [None] * 2, [None] * 2, [None] * 2
    for c in chains:
        out_shapes = shapes(count // 2, first_widths, bf16)
        owns[c] = call(functools.partial(act_kernel, halves), 8, out_shapes, *kept[c], *received[c])
        received[c] = along_axes(owns[c])
    for c in chains:
        out_shapes = shapes(count, second_widths, bf16)
        nears[c] = call(functools.partial(join_kernel, halves), 8, out_shapes, *owns[c], *received[c])
        fars[c] = along_axes(nears[c])

    def parts(near, far):
        return [value[n] for n in range(3) for chain in chains for value in (near[chain], far[chain])]

    values = parts(nears, fars)
    all_blocks = [value for chain in chains for value in blocks[chain]]
    chunks = got.shape[:2] + (block_width,)
    buffers = [pltpu.VMEM((2, *chunks), bf16), pltpu.VMEM((2, 3, *chunks), bf16), pltpu.VMEM((4 * count, wide), bf16)]
    buffers += [pltpu.VMEM((4 * count, width), bf16) for width in second_widths]
    buffers += [pltpu.SemaphoreType.DMA((24,))]

    lanes = max(block_width, *halves)
    hidden_pick = lax.dynamic_index_in_dim(hidden_states, expert, 1, keepdims=False)
    sums_shape = (6, 8, wide)
    outs = call(
        functools.partial(grad_out_kernel, halves), 56,
        [shape((half, block_width), f32) for half in halves]
        + [shape((half, block_width), bf16) for half in halves]
        + [shape(sums_shape, f32)],
        *all_blocks, *values,
        scratch=buffers, whole=range(16), streamed_out=range(3),
    )
    out_own, out_sent, out_sums = outs[:3], outs[3:6], outs[6]
    got_out = along_axes(out_sent)
    outs = call(
        functools.partial(grad_in_kernel, halves), 56,
        [shape((block_width, half), f32) for half in halves]
        + [shape((block_width, half), bf16) for half in halves]
        + [shape((STAT_ROWS, lanes), f32)],
        *all_blocks, *values, out_sums, hidden_pick[1:2],
        scratch=buffers + [pltpu.VMEM(sums_shape, f32)], whole=range(16), streamed_out=range(3),
    )
    in_own, in_sent, stats = outs[:3], outs[3:6], outs[6]
    got_in = along_axes(in_sent)

    width_pick = lax.dynamic_index_in_dim(width_states, expert, 1, keepdims=False)

    def padded(values):
        return jnp.pad(values, ((0, 0), (0, lanes - values.shape[1])), constant_values=1.0)

    prev = [padded(width_pick.reshape(2 * GROUP, block_width))]
    for which in range(2):
        for k in sets:
            low, high = bounds[k]
            prev.append(padded(hidden_pick[which, low:high].reshape(2, halves[k])))
    prev.append(jnp.ones((STAT_ROWS - TOTALS, lanes), f32))
    prev = jnp.concatenate(prev)

    def fetched(*groups):
        arrays = [value for group in groups for value in group]
        return [pltpu.VMEM(value.shape, value.dtype) for value in arrays] + [pltpu.SemaphoreType.DMA((len(arrays),))]

    def totals(values):
        values = values + swap(values, 1) + swap(values, 2) + swap(values, 3)
        if lax.axis_size("ffn") > 2:
            values = values + swap(values, 4)
            return values, ffn_total(values)
        ends = [(e, f) for e in range(places) for f in range(2)]

        def other(expert_mask, ffn_mask):
            moves = [(e * 2 + f, (e ^ expert_mask) * 2 + (f ^ ffn_mask)) for e, f in ends]
            return lax.ppermute(values, ("expert", "ffn"), moves)

        cube = values + swap(values, 4)
        return cube, cube + (other(0, 1) + other(4, 1))

    stats, got_out = lax.optimization_barrier((stats, got_out))
    group_sums, whole_sums = totals(stats)
    whole_sums, got_in = lax.optimization_barrier((whole_sums, got_in))
    factors, norms = call(
        norm_kernel, 52,
        [shape((STAT_ROWS, lanes), f32), shape((8, 128), f32)],
        prev, group_sums, whole_sums, *in_own, *in_sent, *out_own, *out_sent,
        scratch=fetched(in_own, in_sent, out_own, out_sent), whole=range(3, 15),
    )
    norms = totals(norms)[1]
    update_in, update_out = call(
        functools.partial(final_kernel, bounds), 52,
        [shape(local_in.shape, bf16), shape(local_out.shape, bf16)],
        prev, factors, whole_sums, norms, *in_own, *out_own, *got_in, *got_out,
        scratch=fetched(in_own, out_own, got_in, got_out), whole=range(4, 16), streamed_out=range(2),
    )
    return (update_in[None], update_out[None])


def solution(mesh):
    return jax.shard_map(
        shards,
        mesh=mesh,
        in_specs=(
            P("expert", None),
            P("expert", None),
            P("expert", None),
            P("expert", None, "ffn"),
            P("expert", "ffn", None),
            P(),
            P(None, None, "ffn"),
        ),
        out_specs=(P("expert", None, "ffn"), P("expert", "ffn", None)),
        check_vma=False,
    )
```
